256 devices in a mesh: grp: 2 (over z_lo), gy: 8 (over z_hi, core), gz: 16 (over y, x).
Axes of the slice: x: 4, y: 4, z: 8 (z_hi: 4, z_lo: 2; z = z_hi * 2 + z_lo), core: 2. Of those that a mesh axis runs over, the one named last changes fastest.
Arguments:
- field_pairs: float32 [2, 2, 384, 256, 128], P('grp', None, 'gy', 'gz'), may hold values from -6 to 6
- tile_owner: int32 [2, 48, 16, 1], replicated, may hold values from 0 to 511
- electrode_volts: float32 [512], P(('grp', 'gy', 'gz')), may hold values from -6 to 6
Outputs:
- advanced: float32 [2, 2, 384, 256, 128], P('grp', None, 'gy', 'gz')
- electrode_grad: float32 [512], P(('grp', 'gy', 'gz'))
The draws below stay inside these ranges and needn't reach their ends.
Inputs may be any that keep to these rules, and one draw needn't show every extreme that they name: `tile_owner`: electrode numbers; every electrode owns at least one wall tile.
All inputs are finite; a program needn't handle non-finite values.
Results may differ from the reference program's by a relative error of at most 0.00011.
Values sent between devices are 32-bit elements; how exact they have to be, the bound alone decides.
No kernel may reach another device: no remote copies, remote signals or barrier semaphores. Data moves between devices by JAX's collectives and lax.ppermute only.
A program may use at most 64 MiB of HBM per device.

```python
import jax
import jax.numpy as jnp
from jax import lax

NX = 128
STEPS = 2
SWEEPS = 2
TILE_Y = 8
TILE_X = 8
ELECTRODES = 512
NY = 384
NZ = 256


def shard_levels(stream_key, dims, split, smallest, high):
    level, own = 1.0, jax.random.fold_in(stream_key, 6)
    for dim, shards_of in split:
        steps = jnp.exp(jax.random.uniform(jax.random.fold_in(own, dim), (shards_of,), jnp.float32, smallest / len(split), high / len(split)))
        level = level * jnp.repeat(steps, dims[dim] // shards_of).reshape([-1 if axis == dim else 1 for axis in range(len(dims))])
    return level


def distinct(rng, rows, amount, top, lift):
    sequence = jax.random.permutation(jax.random.fold_in(rng, 1), amount)
    pull = sequence
    for power in range(3):
        pull = pull * pull // amount
    pull = pull * lift // amount
    tickets = jax.random.randint(jax.random.fold_in(rng, 2), (rows, amount), 0, 4096) + pull
    sure = jax.random.permutation(jax.random.fold_in(rng, 3), rows)[jnp.arange(amount) % rows]
    tickets = jnp.where(jnp.arange(rows)[:, None] == sure[None, :], 1 << 14, tickets)
    priority = tickets * amount + jnp.arange(amount)
    return lax.top_k(priority.astype(jnp.int32), top)[1].astype(jnp.int32)


def bell_draw(own_key, shape, deviation, reach, cuts=(), held_as=jnp.bfloat16):
    drawn = jax.random.normal(own_key, shape, jnp.float32) * deviation
    if len(cuts) > 0:
        drawn = shard_levels(own_key, shape, cuts, -0.22, 0.18) * drawn
    return jnp.clip(drawn, min=-reach, max=reach).astype(held_as)


def setup_inputs(seed: int = 0) -> dict:
    keys = jax.random.split(jax.random.key(seed), 4)
    return {
        "field_pairs": bell_draw(keys[0], (2, 2, NY, NZ, NX), 1.0, 6.0, ((0, 2), (2, 8), (3, 16)), jnp.float32),
        "tile_owner": distinct(keys[1], 2 * (NY // TILE_Y) * (NX // TILE_X), ELECTRODES, 1, 32).reshape((2, NY // TILE_Y, NX // TILE_X, 1)),
        "electrode_volts": bell_draw(keys[2], (ELECTRODES,), 1.0, 6.0, ((0, 256),), jnp.float32),
    }


self_weight = 0.35
diffusion = 0.1
induction = 0.5
coupling = 0.5

def neighbour_sum(field):
    padded = jnp.pad(field, ((1, 1), (1, 1), (0, 0)))
    total = padded[2:, 1:-1] + padded[:-2, 1:-1] + padded[1:-1, 2:] + padded[1:-1, :-2]
    return total + jnp.roll(field, 1, 2) + jnp.roll(field, -1, 2)

def span_diff(field):
    padded = jnp.pad(field, ((0, 0), (1, 1), (0, 0)))
    return padded[:, 2:] - padded[:, :-2]

def window(velocity, potential, volts, tile_owner):
    tiles = jnp.take(volts, tile_owner[..., 0], axis=0)
    wall = jnp.repeat(jnp.repeat(tiles, TILE_Y, 1), TILE_X, 2)
    ghost = jnp.zeros((NY, NZ, NX), jnp.float32)
    ghost = ghost.at[:, 0, :].add(wall[0]).at[:, -1, :].add(wall[1])
    states = []
    for step in range(STEPS):
        source = induction * span_diff(velocity)
        for sweep in range(SWEEPS):
            potential = (neighbour_sum(potential) + ghost - source) / 6.0
        velocity = self_weight * velocity + diffusion * neighbour_sum(velocity) + coupling * span_diff(potential)
        states.append(velocity)
    return (tuple(states), potential)

def reference(field_pairs, tile_owner, electrode_volts):
    start_vel = field_pairs[0, 0]
    start_pot = field_pairs[0, 1]
    end_vel = field_pairs[1, 0]
    end_pot = field_pairs[1, 1]
    outputs, pullback = jax.vjp(lambda first, second, third: window(first, second, third, tile_owner), start_vel, start_pot, electrode_volts)
    states, final_pot = outputs
    cotangent = []
    for step in range(STEPS):
        if step == STEPS - 1:
            cotangent.append(states[step] + end_vel)
        else:
            cotangent.append(states[step])
    adj_vel, adj_pot, volt_grad = pullback((tuple(cotangent), end_pot))
    advanced = jnp.stack([jnp.stack([states[-1], final_pot]), jnp.stack([adj_vel, adj_pot])])
    return (advanced, volt_grad)
```

```python
import jax
import jax.numpy as jnp
from jax import lax
from jax.experimental import pallas as pl
from jax.experimental.pallas import tpu as pltpu
from jax.sharding import PartitionSpec as P

AXES = ("grp", "gy", "gz")
TY = 6
ROWS, COLS, LANES = 48, 16, 128
HY = 8
EXT = ROWS + 2 * HY
ZE = 48
ZO = 16


def rows_loop(first, last, n, body):
    def step(i, carry):
        body(first + i * n)
        return carry
    lax.fori_loop(0, (last - first + 1) // n, step, 0)


def zshift(v):
    z = v.shape[1]
    return pltpu.roll(v, z - 1, 1), pltpu.roll(v, 1, 1)


def around(w):
    c = w[1:-1]
    zp, zm = zshift(c)
    s = (w[:-2] + w[2:]) + (zp + zm)
    s = s + (pltpu.roll(c, 1, 2) + pltpu.roll(c, LANES - 1, 2))
    return c, s, zp - zm


def ld(ref, r, n, z0=0, z1=ZE):
    return ref[pl.ds(r, n), z0:z1, :]


def zero_edges(edge, ref):
    ylo, yhi, zlo, zhi = edge

    @pl.when(ylo)
    def _():
        ref[HY - 1] = jnp.zeros((ZE, LANES), jnp.float32)

    @pl.when(yhi)
    def _():
        ref[HY + ROWS] = jnp.zeros((ZE, LANES), jnp.float32)

    @pl.when(zlo)
    def _():
        ref[:, ZO - 8:ZO, :] = jnp.zeros((EXT, 8, LANES), jnp.float32)

    @pl.when(zhi)
    def _():
        ref[:, ZO + COLS:ZO + COLS + 8, :] = jnp.zeros((EXT, 8, LANES), jnp.float32)


def add_ghost(edge, ref, ghost):
    if ghost is None:
        return
    _, _, zlo, zhi = edge

    @pl.when(zlo)
    def _():
        ref[:, ZO:ZO + 8, :] += ghost[...]

    @pl.when(zhi)
    def _():
        ref[:, ZO + 8:ZO + 16, :] += ghost[...]


N = 2
M0, M1 = 8, 40


def forward(edge, ghost, U, P, SRC, B, Q, U1, A):
    def stage_a(r):
        c, s, d = around(ld(U, r - 1, N + 2))
        src = (0.5 / 6.0) * d
        SRC[pl.ds(r, N)] = src
        B[pl.ds(r, N)] = 0.35 * c + 0.1 * s
        _, s, _ = around(ld(P, r - 1, N + 2))
        Q[pl.ds(r, N)] = s * (1.0 / 6.0) - src
    rows_loop(1, 62, N, stage_a)
    add_ghost(edge, Q, ghost)
    zero_edges(edge, Q)

    def stage_b(r):
        _, s, _ = around(ld(Q, r - 1, N + 2))
        P[pl.ds(r, N)] = s * (1.0 / 6.0) - ld(SRC, r, N)
    rows_loop(2, 61, N, stage_b)
    add_ghost(edge, P, ghost)
    zero_edges(edge, P)

    def stage_c(r):
        zp, zm = zshift(ld(P, r, N))
        U1[pl.ds(r, N)] = ld(B, r, N) + 0.5 * (zp - zm)
    rows_loop(3, 60, N, stage_c)
    zero_edges(edge, U1)

    def stage_d(r):
        c, s, d = around(ld(U1, r - 1, N + 2))
        src = (0.5 / 6.0) * d[:, M0:M1]
        SRC[pl.ds(r, N), M0:M1, :] = src
        B[pl.ds(r, N), M0:M1, :] = 0.35 * c[:, M0:M1] + 0.1 * s[:, M0:M1]
        _, s, _ = around(ld(P, r - 1, N + 2))
        Q[pl.ds(r, N), M0:M1, :] = s[:, M0:M1] * (1.0 / 6.0) - src
    rows_loop(3, 60, N, stage_d)
    add_ghost(edge, Q, ghost)
    zero_edges(edge, Q)

    def stage_e(r):
        _, s, _ = around(ld(Q, r - 1, N + 2, M0, M1))
        P[pl.ds(r, N), M0:M1, :] = s * (1.0 / 6.0) - ld(SRC, r, N, M0, M1)
    rows_loop(4, 59, N, stage_e)
    add_ghost(edge, P, ghost)
    zero_edges(edge, P)

    def stage_f(r):
        zp, zm = zshift(ld(P, r, N, M0, M1))
        A[pl.ds(r, N), M0:M1, :] = ld(B, r, N, M0, M1) + 0.5 * (zp - zm)
    rows_loop(4, 59, N, stage_f)
    zero_edges(edge, A)


def adjoint(edge, A, pot, u1, B, SP, S2, T, A1, S3, T2, out_u, out_p):
    def stage_g(r):
        c, s, d = around(ld(A, r - 1, N + 2, M0, M1))
        B[pl.ds(r, N), M0:M1, :] = 0.35 * c + 0.1 * s
        sp = -0.5 * d
        if pot is not None:
            sp = sp + ld(pot, r, N, M0, M1)
        SP[pl.ds(r, N), M0:M1, :] = sp
    rows_loop(4, 59, N, stage_g)
    zero_edges(edge, SP)

    def stage_h(r):
        c, s, _ = around(ld(SP, r - 1, N + 2, M0, M1))
        s = s * (1.0 / 6.0)
        S2[pl.ds(r, N), M0:M1, :] = s
        T[pl.ds(r, N), M0:M1, :] = (c + s) * (1.0 / 6.0)
    rows_loop(5, 58, N, stage_h)
    zero_edges(edge, S2)
    zero_edges(edge, T)

    def stage_i(r):
        _, s, _ = around(ld(S2, r - 1, N + 2, M0, M1))
        S3[pl.ds(r, N), M0:M1, :] = s * (1.0 / 6.0)
        zp, zm = zshift(ld(T, r, N, M0, M1))
        a = ld(B, r, N, M0, M1) + 0.5 * (zp - zm)
        if u1 is not None:
            a = a + ld(u1, r, N, M0, M1)
        A1[pl.ds(r, N), M0:M1, :] = a
    rows_loop(6, 57, N, stage_i)
    zero_edges(edge, A1)

    def stage_j(r):
        c, s, d = around(ld(A1, r - 1, N + 2, M0, M1))
        B[pl.ds(r, N), M0:M1, :] = 0.35 * c + 0.1 * s
        SP[pl.ds(r, N), M0:M1, :] = ld(S3, r, N, M0, M1) - 0.5 * d
    rows_loop(6, 57, N, stage_j)
    zero_edges(edge, SP)

    def stage_k(r):
        c, s, _ = around(ld(SP, r - 1, N + 2, M0, M1))
        s = s * (1.0 / 6.0)
        S2[pl.ds(r, N), M0:M1, :] = s
        T2[pl.ds(r, N), M0:M1, :] = (c + s) * (1.0 / 6.0)
    rows_loop(7, 56, N, stage_k)
    zero_edges(edge, S2)
    zero_edges(edge, T2)

    c0, c1 = ZO - M0, ZO - M0 + COLS

    def stage_l(r):
        _, s, _ = around(ld(S2, r - 1, N + 2, M0, M1))
        out_p[pl.ds(r - HY, N)] = s[:, c0:c1] * (1.0 / 6.0)
        zp, zm = zshift(ld(T2, r, N, M0, M1))
        out_u[pl.ds(r - HY, N)] = (ld(B, r, N, M0, M1) + 0.5 * (zp - zm))[:, c0:c1]
    rows_loop(8, 55, N, stage_l)


def load_extended(dst, f, own, yd, yu, zd, zu):
    dst[0:HY, ZO:ZO + COLS, :] = yd[f]
    dst[HY:HY + ROWS, ZO:ZO + COLS, :] = own[f]
    dst[HY + ROWS:, ZO:ZO + COLS, :] = yu[f]
    h = EXT // 2
    dst[:, 8:16, :] = zd[f, 0:EXT]
    dst[0:h, 4:8, :] = zd[f, EXT:, 0:4, :]
    dst[h:, 4:8, :] = zd[f, EXT:, 4:8, :]
    dst[:, 0:4, :] = jnp.zeros((EXT, 4, LANES), jnp.float32)
    dst[:, 32:40, :] = zu[f, 0:EXT]
    dst[0:h, 40:44, :] = zu[f, EXT:, 0:4, :]
    dst[h:, 40:44, :] = zu[f, EXT:, 4:8, :]
    dst[:, 44:48, :] = jnp.zeros((EXT, 4, LANES), jnp.float32)


def pack_kernel(own, yd, yu, up, dn):
    h = EXT // 2
    for f in range(2):
        for r0, r1, src in ((0, HY, yd), (HY, HY + ROWS, own), (HY + ROWS, EXT, yu)):
            up[f, r0:r1] = src[f, :, 8:16, :]
            dn[f, r0:r1] = src[f, :, 0:8, :]
        up[f, EXT:EXT + HY, 0:4, :] = yd[f, :, 4:8, :]
        up[f, EXT + HY:, 0:4, :] = own[f, 0:h - HY, 4:8, :]
        up[f, EXT:EXT + h - HY, 4:8, :] = own[f, h - HY:, 4:8, :]
        up[f, EXT + h - HY:, 4:8, :] = yu[f, :, 4:8, :]
        dn[f, EXT:EXT + HY, 0:4, :] = yd[f, :, 8:12, :]
        dn[f, EXT + HY:, 0:4, :] = own[f, 0:h - HY, 8:12, :]
        dn[f, EXT:EXT + h - HY, 4:8, :] = own[f, h - HY:, 8:12, :]
        dn[f, EXT + h - HY:, 4:8, :] = yu[f, :, 8:12, :]


HIGHEST = lax.Precision.HIGHEST


def edges():
    gy, gz = lax.axis_index("gy"), lax.axis_index("gz")
    return (gy == 0, gy == lax.axis_size("gy") - 1, gz == 0, gz == lax.axis_size("gz") - 1)


def iota(shape, dim):
    return lax.broadcasted_iota(jnp.int32, shape, dim)


def tile_volts(volts, labels):
    n = volts.shape[0]
    first = 2 * iota((n, LANES), 0)
    lab = jnp.broadcast_to(labels, (n, LANES))
    zero = jnp.zeros((), jnp.float32)
    hit = jnp.where(lab == first, volts[:, 0:1], zero) + jnp.where(lab == first + 1, volts[:, 1:2], zero)
    return jnp.sum(hit, axis=0, keepdims=True)


def fill_ghost(edge, ghost, volts, labels):
    v = tile_volts(volts, labels)
    lane, row = iota((8, LANES), 1), iota((8, LANES), 0)
    apart = jnp.where((lane >> 4) == row, jnp.broadcast_to(v, (8, LANES)), 0.0)
    spread = ((iota((LANES, LANES), 0) & 15) == (iota((LANES, LANES), 1) >> 3)).astype(jnp.float32)
    wall = jnp.dot(apart, spread, precision=HIGHEST, preferred_element_type=jnp.float32) * (1.0 / 6.0)
    sub = jnp.where(edge[2], 0, 7)
    for ty in range(8):
        tile = jnp.where(row == sub, jnp.broadcast_to(wall[ty:ty + 1], (8, LANES)), 0.0)
        ghost[8 * ty:8 * ty + 8] = jnp.broadcast_to(tile[None], (8, 8, LANES))


def wall_tiles(T, T2, z, held):
    w = T[HY:HY + ROWS, z, :] + T2[HY:HY + ROWS, z, :]
    held[...] = jnp.zeros((8, LANES), jnp.float32)
    held[0:TY] = jnp.sum(w.reshape(TY, 8, LANES), axis=1)
    gather = ((iota((LANES, LANES), 0) >> 3) == (iota((LANES, LANES), 1) & 15)).astype(jnp.float32)
    sums = jnp.dot(held[...], gather, precision=HIGHEST, preferred_element_type=jnp.float32)
    keep = (iota((8, LANES), 1) >> 4) == iota((8, LANES), 0)
    return jnp.sum(jnp.where(keep, sums, 0.0), axis=0, keepdims=True)


def bulk_kernel(own, yd, yu, zd, zu, volts, labels, main, send, wall,
                U, V, SRC, B, Q, U1, A, SP, S2, T, A1, S3, T2, ghost, held):
    edge = edges()
    is_forward = lax.axis_index("grp") == 0
    load_extended(U, 0, own, yd, yu, zd, zu)
    load_extended(V, 1, own, yd, yu, zd, zu)

    @pl.when(jnp.logical_or(edge[2], edge[3]))
    def _():
        fill_ghost(edge, ghost, volts[...], labels[...])

    @pl.when(is_forward)
    def _():
        forward(edge, ghost, U, V, SRC, B, Q, U1, A)
        main[0] = A[HY:HY + ROWS, ZO:ZO + COLS, :]
        main[1] = V[HY:HY + ROWS, ZO:ZO + COLS, :]
        adjoint(edge, A, None, U1, B, SP, S2, T, A1, S3, T2, send.at[0], send.at[1])

    @pl.when(jnp.logical_not(is_forward))
    def _():
        adjoint(edge, U, V, None, B, SP, S2, T, A1, S3, T2, main.at[0], main.at[1])

    wall[...] = jnp.zeros((1, LANES), jnp.float32)

    @pl.when(edge[2])
    def _():
        wall[...] = wall_tiles(T, T2, ZO, held)

    @pl.when(edge[3])
    def _():
        wall[...] = wall_tiles(T, T2, ZO + COLS - 1, held)


def final_kernel(main, extra, sums, labels, out, grad):
    out[0] = main[...] + extra[...]
    me = (lax.axis_index("grp") * lax.axis_size("gy") + lax.axis_index("gy")) * lax.axis_size("gz") + lax.axis_index("gz")
    gz, gy = lax.axis_size("gz"), lax.axis_size("gy")
    total = jnp.zeros((8, LANES), jnp.float32)
    pair = [total, total]
    for s in range(2):
        w = sums[pl.ds(s * (gz - 1), gy, stride=gz), :] + sums[pl.ds(gy * gz + s * (gz - 1), gy, stride=gz), :]
        lab = labels[s]
        for j in range(2):
            pair[j] = pair[j] + jnp.where(lab == 2 * me + j, w, 0.0)
    g = [jnp.sum(p) for p in pair]
    lane = iota((1, 2), 1)
    grad[...] = jnp.where(lane == 0, g[0], g[1])


def vmem(n):
    return [pl.BlockSpec(memory_space=pltpu.VMEM)] * n


def shape(*dims):
    return jax.ShapeDtypeStruct(dims, jnp.float32)


def to_all(row):
    n = lax.axis_size(AXES)
    return lax.all_to_all(jnp.broadcast_to(row, (n, LANES)), AXES, 0, 0, tiled=True)


def shifted(array, axis, by):
    count = lax.axis_size(axis)
    pairs = [(i, i + by) for i in range(count) if 0 <= i + by < count]
    return lax.ppermute(array, axis, pairs)


def per_device(field_pairs, tile_owner, electrode_volts):
    own = field_pairs[0]
    labels = tile_owner[..., 0]
    gy, gz = lax.axis_index("gy"), lax.axis_index("gz")
    big = pltpu.VMEM((EXT, ZE, LANES), jnp.float32)
    roomy = pltpu.CompilerParams(vmem_limit_bytes=40 * 1024 * 1024)

    yd = shifted(own[:, ROWS - HY:], "gy", 1)
    yu = shifted(own[:, :HY], "gy", -1)
    volts = to_all(jnp.pad(electrode_volts, (0, LANES - 2))[None])
    up, dn = pl.pallas_call(
        pack_kernel, out_shape=(shape(2, EXT * 3 // 2, 8, LANES),) * 2,
        in_specs=vmem(3), out_specs=vmem(2),
    )(own, yd, yu)
    zd = shifted(up, "gz", 1)
    zu = shifted(dn, "gz", -1)

    fenced = jnp.pad(labels, ((0, 0), (1, 1), (0, 0)), constant_values=-1)
    side = (gz == lax.axis_size("gz") - 1).astype(jnp.int32)
    near = lax.dynamic_slice(fenced, (side, gy * TY, 0), (1, 8, 16)).reshape(1, LANES)
    block = shape(2, ROWS, COLS, LANES)
    main, send, wall = pl.pallas_call(
        bulk_kernel, out_shape=(block, block, shape(1, LANES)),
        in_specs=vmem(7), out_specs=vmem(3),
        scratch_shapes=[big] * 13 + [pltpu.VMEM((EXT, 8, LANES), jnp.float32), pltpu.VMEM((8, LANES), jnp.float32)],
        compiler_params=roomy,
    )(own, yd, yu, zd, zu, volts, near)

    extra = lax.ppermute(send, "grp", [(0, 1)])
    sums = to_all(wall)
    by_block = jnp.pad(labels.reshape(2, 8, TY * 16), ((0, 0), (0, 0), (0, LANES - TY * 16)), constant_values=-1)
    advanced, grad = pl.pallas_call(
        final_kernel, out_shape=(shape(1, 2, ROWS, COLS, LANES), shape(1, 2)),
        in_specs=vmem(4), out_specs=vmem(2), compiler_params=roomy,
    )(main, extra, sums, by_block)
    return (advanced, grad.reshape(2))


def solution(mesh):
    placed = (P("grp", None, "gy", "gz", None), P(), P(AXES))
    return jax.shard_map(
        per_device, mesh=mesh, in_specs=placed,
        out_specs=(P("grp", None, "gy", "gz", None), P(AXES)), check_vma=False,
    )
```

```python
import functools

import jax
import jax.numpy as jnp
import numpy as np
from jax import lax
from jax.experimental import pallas as pl
from jax.experimental.pallas import tpu as pltpu
from jax.sharding import PartitionSpec as P

AXES = ("grp", "gy", "gz")
TY = 6
VOLT = TY * 16
ROWS, COLS, LANES = 48, 16, 128
HY = 8
EXT = ROWS + 2 * HY
ZE = 48
ZO = 16


def rows_loop(first, last, body):
    n = (last - first + 1) // 2

    def step(i, carry):
        body(first + i * n, n)
        return carry
    lax.fori_loop(0, 2, step, 0)


def zshift(v, closed):
    z = v.shape[1]
    zp, zm = pltpu.roll(v, z - 1, 1), pltpu.roll(v, 1, 1)
    if closed:
        layer = lax.broadcasted_iota(jnp.int32, v.shape, 1)
        zp = jnp.where(layer == z - 1, 0.0, zp)
        zm = jnp.where(layer == 0, 0.0, zm)
    return zp, zm


def around(w, closed):
    c = w[1:-1]
    zp, zm = zshift(c, closed)
    s = (w[:-2] + w[2:]) + (zp + zm)
    s = s + (pltpu.roll(c, 1, 2) + pltpu.roll(c, LANES - 1, 2))
    return c, s, zp - zm


def zero_edges(edge, ref):
    ylo, yhi, zlo, zhi = edge
    depth = ref.shape[1]

    @pl.when(ylo)
    def _():
        ref[HY - 1] = jnp.zeros((depth, LANES), jnp.float32)

    @pl.when(yhi)
    def _():
        ref[HY + ROWS] = jnp.zeros((depth, LANES), jnp.float32)

    if zlo is None:
        return

    @pl.when(zlo)
    def _():
        ref[:, ZO - 8:ZO, :] = jnp.zeros((EXT, 8, LANES), jnp.float32)

    @pl.when(zhi)
    def _():
        ref[:, ZO + COLS:ZO + COLS + 8, :] = jnp.zeros((EXT, 8, LANES), jnp.float32)


BULK = (0, ZE, 8, 40, ZO, False)
NEAR = (0, COLS, 0, COLS, 0, True)


def forward(edge, ghost, window, U, V, SRC, B, Q, U1, A):
    W0, W1, M0, M1, _, closed = window
    m = slice(M0 - W0, M1 - W0)

    def ld(ref, r, n, z0=M0, z1=M1):
        return ref[pl.ds(r, n), z0:z1, :]

    def finish(ref):
        if ghost is not None:
            ref[...] += ghost[...]
        zero_edges(edge, ref)

    def stage_a(r, n):
        c, s, d = around(ld(U, r - 1, n + 2, W0, W1), closed)
        src = (0.5 / 6.0) * d
        SRC[pl.ds(r, n), W0:W1, :] = src
        B[pl.ds(r, n), W0:W1, :] = 0.35 * c + 0.1 * s
        _, s, _ = around(ld(V, r - 1, n + 2, W0, W1), closed)
        Q[pl.ds(r, n), W0:W1, :] = s * (1.0 / 6.0) - src
    if U is None:
        Q[...] = ghost[...]
        zero_edges(edge, Q)
    else:
        rows_loop(1, 62, stage_a)
        finish(Q)

    def stage_b(r, n):
        _, s, _ = around(ld(Q, r - 1, n + 2, W0, W1), closed)
        s = s * (1.0 / 6.0)
        V[pl.ds(r, n), W0:W1, :] = s if U is None else s - ld(SRC, r, n, W0, W1)
    rows_loop(2, 61, stage_b)
    finish(V)

    def stage_c(r, n):
        zp, zm = zshift(ld(V, r, n, W0, W1), closed)
        u = 0.5 * (zp - zm)
        U1[pl.ds(r, n), W0:W1, :] = u if U is None else u + ld(B, r, n, W0, W1)
    rows_loop(3, 60, stage_c)
    zero_edges(edge, U1)

    def stage_d(r, n):
        c, s, d = around(ld(U1, r - 1, n + 2, W0, W1), closed)
        src = (0.5 / 6.0) * d[:, m]
        SRC[pl.ds(r, n), M0:M1, :] = src
        B[pl.ds(r, n), M0:M1, :] = 0.35 * c[:, m] + 0.1 * s[:, m]
        _, s, _ = around(ld(V, r - 1, n + 2, W0, W1), closed)
        Q[pl.ds(r, n), M0:M1, :] = s[:, m] * (1.0 / 6.0) - src
    rows_loop(3, 60, stage_d)
    finish(Q)

    def stage_e(r, n):
        _, s, _ = around(ld(Q, r - 1, n + 2), closed)
        V[pl.ds(r, n), M0:M1, :] = s * (1.0 / 6.0) - ld(SRC, r, n)
    rows_loop(4, 59, stage_e)
    finish(V)

    def stage_f(r, n):
        zp, zm = zshift(ld(V, r, n), closed)
        A[pl.ds(r, n), M0:M1, :] = ld(B, r, n) + 0.5 * (zp - zm)
    rows_loop(4, 59, stage_f)
    zero_edges(edge, A)


def adjoint(edge, window, A, pot, u1, B, SP, S2, T, A1, S3, T2, give):
    _, _, M0, M1, first, closed = window

    def ld(ref, r, n):
        return ref[pl.ds(r, n), M0:M1, :]

    def stage_g(r, n):
        c, s, d = around(ld(A, r - 1, n + 2), closed)
        B[pl.ds(r, n), M0:M1, :] = 0.35 * c + 0.1 * s
        sp = -0.5 * d
        if pot is not None:
            sp = sp + ld(pot, r, n)
        SP[pl.ds(r, n), M0:M1, :] = sp
    rows_loop(4, 59, stage_g)
    zero_edges(edge, SP)

    def stage_h(r, n):
        c, s, _ = around(ld(SP, r - 1, n + 2), closed)
        s = s * (1.0 / 6.0)
        S2[pl.ds(r, n), M0:M1, :] = s
        T[pl.ds(r, n), M0:M1, :] = (c + s) * (1.0 / 6.0)
    rows_loop(5, 58, stage_h)
    zero_edges(edge, S2)
    zero_edges(edge, T)

    def stage_i(r, n):
        _, s, _ = around(ld(S2, r - 1, n + 2), closed)
        S3[pl.ds(r, n), M0:M1, :] = s * (1.0 / 6.0)
        zp, zm = zshift(ld(T, r, n), closed)
        a = ld(B, r, n) + 0.5 * (zp - zm)
        if u1 is not None:
            a = a + ld(u1, r, n)
        A1[pl.ds(r, n), M0:M1, :] = a
    rows_loop(6, 57, stage_i)
    zero_edges(edge, A1)

    def stage_j(r, n):
        c, s, d = around(ld(A1, r - 1, n + 2), closed)
        B[pl.ds(r, n), M0:M1, :] = 0.35 * c + 0.1 * s
        SP[pl.ds(r, n), M0:M1, :] = ld(S3, r, n) - 0.5 * d
    rows_loop(6, 57, stage_j)
    zero_edges(edge, SP)

    def stage_k(r, n):
        c, s, _ = around(ld(SP, r - 1, n + 2), closed)
        s = s * (1.0 / 6.0)
        S2[pl.ds(r, n), M0:M1, :] = s
        T2[pl.ds(r, n), M0:M1, :] = (c + s) * (1.0 / 6.0)
    rows_loop(7, 56, stage_k)
    zero_edges(edge, S2)
    zero_edges(edge, T2)
    if give is None:
        return
    own = slice(first - M0, first - M0 + COLS)

    def stage_l(r, n):
        _, s, _ = around(ld(S2, r - 1, n + 2), closed)
        zp, zm = zshift(ld(T2, r, n), closed)
        u = ld(B, r, n) + 0.5 * (zp - zm)
        give(pl.ds(r - HY, n), u[:, own], s[:, own] * (1.0 / 6.0))
    rows_loop(8, 55, stage_l)


HALF = ROWS // 2


def load_extended(dst, f, own, yd, yu, zd, zu, cd, cu):
    top = HY + ROWS
    dst[0:HY, ZO:ZO + COLS, :] = yd[f]
    dst[HY:top, ZO:ZO + COLS, :] = own[f]
    dst[top:, ZO:ZO + COLS, :] = yu[f]
    for z, c, near, far in ((zd, cd, 8, 4), (zu, cu, 32, 40)):
        dst[HY:top, near:near + 8, :] = z[f, 0:ROWS]
        dst[HY:HY + HALF, far:far + 4, :] = z[f, ROWS:, 0:4, :]
        dst[HY + HALF:top, far:far + 4, :] = z[f, ROWS:, 4:8, :]
        dst[0:HY, near:near + 8, :] = c[f, 0:HY]
        dst[top:, near:near + 8, :] = c[f, HY:2 * HY]
        dst[0:HY, far:far + 4, :] = c[f, 2 * HY:, 0:4, :]
        dst[top:, far:far + 4, :] = c[f, 2 * HY:, 4:8, :]
    for z in (0, 44):
        dst[:, z:z + 4, :] = jnp.zeros((EXT, 4, LANES), jnp.float32)


def pack_kernel(own, low, high, up, dn):
    low[...] = own[:, 0:HY]
    high[...] = own[:, ROWS - HY:]
    up[:, 0:ROWS] = own[:, :, 8:16, :]
    up[:, ROWS:, 0:4, :] = own[:, 0:HALF, 4:8, :]
    up[:, ROWS:, 4:8, :] = own[:, HALF:, 4:8, :]
    dn[:, 0:ROWS] = own[:, :, 0:8, :]
    dn[:, ROWS:, 0:4, :] = own[:, 0:HALF, 8:12, :]
    dn[:, ROWS:, 4:8, :] = own[:, HALF:, 8:12, :]


def corner_kernel(yd, yu, up, dn):
    up[:, 0:HY] = yd[:, :, 8:16, :]
    up[:, HY:2 * HY] = yu[:, :, 8:16, :]
    up[:, 2 * HY:, 0:4, :] = yd[:, :, 4:8, :]
    up[:, 2 * HY:, 4:8, :] = yu[:, :, 4:8, :]
    dn[:, 0:HY] = yd[:, :, 0:8, :]
    dn[:, HY:2 * HY] = yu[:, :, 0:8, :]
    dn[:, 2 * HY:, 0:4, :] = yd[:, :, 8:12, :]
    dn[:, 2 * HY:, 4:8, :] = yu[:, :, 8:12, :]


HIGHEST = lax.Precision.HIGHEST


def edges():
    gy, gz = lax.axis_index("gy"), lax.axis_index("gz")
    return (gy == 0, gy == lax.axis_size("gy") - 1, gz == 0, gz == lax.axis_size("gz") - 1)


def iota(shape, dim):
    return lax.broadcasted_iota(jnp.int32, shape, dim)


def tile_volts(first, second, labels):
    lab = jnp.broadcast_to(labels, first.shape) - 2 * iota(first.shape, 0)
    hit = jnp.where(lab == 0, first, 0.0) + jnp.where(lab == 1, second, 0.0)
    return jnp.sum(hit, axis=0, keepdims=True)


def fill_ghost(upper, ghost, volts):
    lane, row = iota((8, LANES), 1), iota((8, LANES), 0)
    apart = jnp.where((lane >> 4) == row, jnp.broadcast_to(volts, (8, LANES)), 0.0)
    spread = ((iota((LANES, LANES), 0) & 15) == (iota((LANES, LANES), 1) >> 3)).astype(jnp.float32)
    wall = jnp.dot(apart, spread, precision=HIGHEST, preferred_element_type=jnp.float32) * (1.0 / 6.0)
    layer = iota((COLS, LANES), 0) == jnp.where(upper, COLS - 1, 0)
    for ty in range(8):
        tile = jnp.where(layer, jnp.broadcast_to(wall[ty:ty + 1], (COLS, LANES)), 0.0)
        ghost[8 * ty:8 * ty + 8] = jnp.broadcast_to(tile[None], (8, COLS, LANES))


def wall_tiles(upper, T, T2, held):
    layer = iota((ROWS, COLS, LANES), 1) == jnp.where(upper, COLS - 1, 0)
    w = jnp.sum(jnp.where(layer, T[HY:HY + ROWS] + T2[HY:HY + ROWS], 0.0), axis=1)
    held[...] = jnp.zeros((8, LANES), jnp.float32)
    held[0:TY] = jnp.sum(w.reshape(TY, 8, LANES), axis=1)
    gather = ((iota((LANES, LANES), 0) >> 3) == (iota((LANES, LANES), 1) & 15)).astype(jnp.float32)
    sums = jnp.dot(held[...], gather, precision=HIGHEST, preferred_element_type=jnp.float32)
    keep = (iota((8, LANES), 1) >> 4) == iota((8, LANES), 0)
    return jnp.sum(jnp.where(keep, sums, 0.0), axis=0, keepdims=True)


def wall_kernel(own, yd, yu, volts, row, U, V, SRC, B, Q, U1, A, SP, S2, T, A1, S3, T2, held, sums):
    ylo, yhi, zlo, zhi = edges()
    edge = (ylo, yhi, None, None)
    is_forward = lax.axis_index("grp") == 0
    sums[...] = jnp.zeros((1, LANES), jnp.float32)

    @pl.when(jnp.logical_or(zlo, zhi))
    def _():
        for f, ref in ((0, U), (1, V)):
            ref[0:HY] = yd[f]
            ref[HY:HY + ROWS] = own[f]
            ref[HY + ROWS:] = yu[f]

        @pl.when(is_forward)
        def _():
            forward(edge, None, NEAR, U, V, SRC, B, Q, U1, A)
            adjoint(edge, NEAR, A, None, U1, B, SP, S2, T, A1, S3, T2, None)

        @pl.when(jnp.logical_not(is_forward))
        def _():
            adjoint(edge, NEAR, U, V, None, B, SP, S2, T, A1, S3, T2, None)

        sums[...] = wall_tiles(zhi, T, T2, held)

    lane = iota((1, LANES), 1)
    out = jnp.where(lane == VOLT, volts[0], jnp.where(lane == VOLT + 1, volts[1], sums[...]))
    row[...] = jnp.broadcast_to(out, row.shape)


def bulk_kernel(own, yd, yu, zd, zu, cd, cu, main, send, U, V, SRC, B, Q, U1, A, SP, S2, T, A1, S3, T2):
    edge = edges()
    is_forward = lax.axis_index("grp") == 0
    load_extended(U, 0, own, yd, yu, zd, zu, cd, cu)
    load_extended(V, 1, own, yd, yu, zd, zu, cd, cu)

    def into(ref):
        def give(rows, u, p):
            ref[0, rows] = u
            ref[1, rows] = p
        return give

    @pl.when(is_forward)
    def _():
        forward(edge, None, BULK, U, V, SRC, B, Q, U1, A)
        main[0] = A[HY:HY + ROWS, ZO:ZO + COLS, :]
        main[1] = V[HY:HY + ROWS, ZO:ZO + COLS, :]
        adjoint(edge, BULK, A, None, U1, B, SP, S2, T, A1, S3, T2, into(send))

    @pl.when(jnp.logical_not(is_forward))
    def _():
        adjoint(edge, BULK, U, V, None, B, SP, S2, T, A1, S3, T2, into(main))


def volts_kernel(main, rows, near, labels, response, out, grad, V, SRC, B, Q, U1, A, SP, S2, T, A1, S3, T2, ghost):
    ylo, yhi, zlo, zhi = edges()
    edge = (ylo, yhi, None, None)
    is_forward = lax.axis_index("grp") == 0
    n = rows.shape[0]
    first = jnp.broadcast_to(rows[:, VOLT:VOLT + 1], (n, LANES))
    second = jnp.broadcast_to(rows[:, VOLT + 1:VOLT + 2], (n, LANES))

    @pl.when(jnp.logical_or(zlo, zhi))
    def _():
        fill_ghost(zhi, ghost, tile_volts(first, second, near[...]))
        forward(edge, ghost, NEAR, None, V, SRC, B, Q, U1, A)

        @pl.when(is_forward)
        def _():
            out[0] = main[0] + A[HY:HY + ROWS]
            out[1] = main[1] + V[HY:HY + ROWS]

        @pl.when(jnp.logical_not(is_forward))
        def _():
            def give(at, u, p):
                out[0, at] = main[0, at] + u
                out[1, at] = main[1, at] + p
            adjoint(edge, NEAR, A, None, U1, B, SP, S2, T, A1, S3, T2, give)

    @pl.when(jnp.logical_not(jnp.logical_or(zlo, zhi)))
    def _():
        out[...] = main[...]

    gy, gz = lax.axis_size("gy"), lax.axis_size("gz")
    me = (lax.axis_index("grp") * gy + lax.axis_index("gy")) * gz + lax.axis_index("gz")
    pair = [jnp.zeros((gy, LANES), jnp.float32)] * 2
    block = iota((gy, LANES), 0)
    for s in range(2):
        v = jnp.concatenate([tile_volts(first, second, labels[s, g:g + 1]) for g in range(gy)], axis=0)
        r = jnp.dot(v, response[...], precision=HIGHEST, preferred_element_type=jnp.float32)
        r = [r[:, k * LANES:(k + 1) * LANES] for k in range(5)]
        w = jnp.where(block == 0, r[3], jnp.where(block == gy - 1, r[4], r[0]))
        w = w + jnp.where(block == 0, 0.0, pltpu.roll(r[1], 1, 0))
        w = w + jnp.where(block == gy - 1, 0.0, pltpu.roll(r[2], gy - 1, 0))
        for g in range(2):
            w = w + rows[pl.ds(g * gy * gz + s * (gz - 1), gy, stride=gz), :]
        for j in range(2):
            pair[j] = pair[j] + jnp.where(labels[s] == 2 * me + j, w, 0.0)
    total = [jnp.sum(p) for p in pair]
    grad[...] = jnp.where(iota((1, 2), 1) == 0, total[0], total[1])


def sum_kernel(main, extra, out):
    out[0] = main[...] + extra[...]


def wall_response():
    def near_sum(f):
        g = np.pad(f, ((0, 0), (1, 1), (1, 1), (0, 0)))
        t = g[:, 2:, 1:-1] + g[:, :-2, 1:-1] + g[:, 1:-1, 2:] + g[:, 1:-1, :-2]
        return t + np.roll(f, 1, 3) + np.roll(f, -1, 3)

    def diff(f):
        g = np.pad(f, ((0, 0), (0, 0), (1, 1), (0, 0)))
        return g[:, :, 2:] - g[:, :, :-2]

    def sums(blocks, at):
        ghost = np.zeros((TY, blocks * ROWS, 13, LANES))
        for t in range(TY):
            ghost[t, at * ROWS + 8 * t:at * ROWS + 8 * t + 8, 0, 0:8] = 1.0
        u, p, states = np.zeros_like(ghost), np.zeros_like(ghost), []
        for _ in range(2):
            source = 0.5 * diff(u)
            for _ in range(2):
                p = (near_sum(p) + ghost - source) / 6.0
            u = 0.35 * u + 0.1 * near_sum(u) + 0.5 * diff(p)
            states.append(u)
        a, q, wall = np.zeros_like(ghost), np.zeros_like(ghost), 0.0
        for u in reversed(states):
            a = a + u
            spread, total = q - 0.5 * diff(a), 0.0
            for _ in range(2):
                total = total + spread / 6.0
                spread = near_sum(spread) / 6.0
            a = 0.35 * a + 0.1 * near_sum(a) + 0.5 * diff(total)
            q = spread
            wall = wall + total[:, :, 0]
        return wall.reshape(TY, blocks, TY, 8, 16, 8).sum((3, 5))

    def matrix(got):
        m = np.zeros((LANES, LANES), np.float32)
        for t in range(TY):
            for x in range(16):
                m[t * 16 + x, 0:TY * 16] = np.roll(got[t], x, 1).reshape(-1)
        return m

    middle, low, high = sums(3, 1), sums(2, 0), sums(2, 1)
    return np.concatenate([matrix(middle[:, 1]), matrix(middle[:, 2]), matrix(middle[:, 0]),
                           matrix(low[:, 0]), matrix(high[:, 1])], axis=1)


def vmem(n):
    return [pl.BlockSpec(memory_space=pltpu.VMEM)] * n


def shape(*dims):
    return jax.ShapeDtypeStruct(dims, jnp.float32)


def scratch(count, depth):
    return [pltpu.VMEM((EXT, depth, LANES), jnp.float32)] * count


def shifted(array, axis, by):
    count = lax.axis_size(axis)
    pairs = [(i, i + by) for i in range(count) if 0 <= i + by < count]
    return lax.ppermute(array, axis, pairs)


def per_device(response, field_pairs, tile_owner, electrode_volts):
    own = field_pairs[0]
    labels = tile_owner[..., 0]
    gy, gz = lax.axis_index("gy"), lax.axis_index("gz")
    devices = lax.axis_size(AXES)
    roomy = pltpu.CompilerParams(vmem_limit_bytes=40 * 1024 * 1024)
    middling = pltpu.CompilerParams(vmem_limit_bytes=24 * 1024 * 1024)
    tight = pltpu.CompilerParams(vmem_limit_bytes=8 * 1024 * 1024)
    block = shape(2, ROWS, COLS, LANES)

    low, high, up, dn = pl.pallas_call(
        pack_kernel,
        out_shape=(shape(2, HY, COLS, LANES),) * 2 + (shape(2, ROWS * 3 // 2, 8, LANES),) * 2,
        in_specs=vmem(1), out_specs=vmem(4), compiler_params=tight,
    )(own)
    yd = shifted(high, "gy", 1)
    yu = shifted(low, "gy", -1)
    zd = shifted(up, "gz", 1)
    zu = shifted(dn, "gz", -1)
    up, dn = pl.pallas_call(
        corner_kernel, out_shape=(shape(2, 3 * HY, 8, LANES),) * 2,
        in_specs=vmem(2), out_specs=vmem(2), compiler_params=tight,
    )(yd, yu)
    cd = shifted(up, "gz", 1)
    cu = shifted(dn, "gz", -1)

    row = pl.pallas_call(
        wall_kernel, out_shape=shape(devices, LANES),
        in_specs=vmem(3) + [pl.BlockSpec(memory_space=pltpu.SMEM)], out_specs=vmem(1)[0],
        scratch_shapes=scratch(13, COLS) + [pltpu.VMEM((8, LANES), jnp.float32), pltpu.VMEM((1, LANES), jnp.float32)],
        compiler_params=middling,
    )(own, yd, yu, electrode_volts)
    rows = lax.all_to_all(row, AXES, 0, 0, tiled=True)

    main, send = pl.pallas_call(
        bulk_kernel, out_shape=(block, block), in_specs=vmem(7), out_specs=vmem(2),
        scratch_shapes=scratch(13, ZE), compiler_params=roomy,
    )(own, yd, yu, zd, zu, cd, cu)
    extra = lax.ppermute(send, "grp", [(0, 1)])

    fenced = jnp.pad(labels, ((0, 0), (1, 1), (0, 0)), constant_values=-1)
    side = (gz == lax.axis_size("gz") - 1).astype(jnp.int32)
    near = lax.dynamic_slice(fenced, (side, gy * TY, 0), (1, 8, 16)).reshape(1, LANES)
    by_block = jnp.pad(labels.reshape(2, 8, TY * 16), ((0, 0), (0, 0), (0, LANES - TY * 16)), constant_values=-1)
    main, grad = pl.pallas_call(
        volts_kernel, out_shape=(block, shape(1, 2)), in_specs=vmem(5), out_specs=vmem(2),
        scratch_shapes=scratch(13, COLS), compiler_params=middling,
    )(main, rows, near, by_block, response)
    advanced = pl.pallas_call(
        sum_kernel, out_shape=shape(1, 2, ROWS, COLS, LANES), in_specs=vmem(2), out_specs=vmem(1)[0],
        compiler_params=tight,
    )(main, extra)
    return (advanced, grad.reshape(2))


def solution(mesh):
    response = jnp.asarray(wall_response())
    placed = (P("grp", None, "gy", "gz", None), P(), P(AXES))
    return jax.shard_map(
        functools.partial(per_device, response), mesh=mesh, in_specs=placed,
        out_specs=(P("grp", None, "gy", "gz", None), P(AXES)), check_vma=False,
    )
```

```python
import functools

import jax
import jax.numpy as jnp
import numpy as np
from jax import lax
from jax.experimental import pallas as pl
from jax.experimental.pallas import tpu as pltpu
from jax.sharding import PartitionSpec as P

AXES = ("grp", "gy", "gz")
TY = 6
VOLT = TY * 16
ROWS, COLS, LANES = 48, 16, 128
HY = 8
EXT = ROWS + 2 * HY
ZE = 48
ZO = 16


def rows_loop(first, last, body):
    n = (last - first + 1) // 2

    def step(i, carry):
        body(first + i * n, n)
        return carry
    lax.fori_loop(0, 2, step, 0)


def zshift(v, closed):
    z = v.shape[1]
    zp, zm = pltpu.roll(v, z - 1, 1), pltpu.roll(v, 1, 1)
    if closed:
        layer = lax.broadcasted_iota(jnp.int32, v.shape, 1)
        zp = jnp.where(layer == z - 1, 0.0, zp)
        zm = jnp.where(layer == 0, 0.0, zm)
    return zp, zm


def around(w, closed):
    c = w[1:-1]
    zp, zm = zshift(c, closed)
    s = (w[:-2] + w[2:]) + (zp + zm)
    s = s + (pltpu.roll(c, 1, 2) + pltpu.roll(c, LANES - 1, 2))
    return c, s, zp - zm


def zero_edges(edge, ref):
    ylo, yhi, zlo, zhi = edge
    depth = ref.shape[1]

    @pl.when(ylo)
    def _():
        ref[HY - 1] = jnp.zeros((depth, LANES), jnp.float32)

    @pl.when(yhi)
    def _():
        ref[HY + ROWS] = jnp.zeros((depth, LANES), jnp.float32)

    if zlo is None:
        return

    @pl.when(zlo)
    def _():
        ref[:, ZO - 8:ZO, :] = jnp.zeros((EXT, 8, LANES), jnp.float32)

    @pl.when(zhi)
    def _():
        ref[:, ZO + COLS:ZO + COLS + 8, :] = jnp.zeros((EXT, 8, LANES), jnp.float32)


BULK = (0, ZE, 8, 40, ZO, False)
NEAR = (0, COLS, 0, COLS, 0, True)


def forward(edge, ghost, window, U, V, SRC, B, Q, U1, A):
    W0, W1, M0, M1, _, closed = window
    m = slice(M0 - W0, M1 - W0)

    def ld(ref, r, n, z0=M0, z1=M1):
        return ref[pl.ds(r, n), z0:z1, :]

    def finish(ref):
        if ghost is not None:
            ref[...] += ghost[...]
        zero_edges(edge, ref)

    def stage_a(r, n):
        c, s, d = around(ld(U, r - 1, n + 2, W0, W1), closed)
        src = (0.5 / 6.0) * d
        SRC[pl.ds(r, n), W0:W1, :] = src
        B[pl.ds(r, n), W0:W1, :] = 0.35 * c + 0.1 * s
        _, s, _ = around(ld(V, r - 1, n + 2, W0, W1), closed)
        Q[pl.ds(r, n), W0:W1, :] = s * (1.0 / 6.0) - src
    if U is None:
        Q[...] = ghost[...]
        zero_edges(edge, Q)
    else:
        rows_loop(1, 62, stage_a)
        finish(Q)

    def stage_b(r, n):
        _, s, _ = around(ld(Q, r - 1, n + 2, W0, W1), closed)
        s = s * (1.0 / 6.0)
        V[pl.ds(r, n), W0:W1, :] = s if U is None else s - ld(SRC, r, n, W0, W1)
    rows_loop(2, 61, stage_b)
    finish(V)

    def stage_c(r, n):
        zp, zm = zshift(ld(V, r, n, W0, W1), closed)
        u = 0.5 * (zp - zm)
        U1[pl.ds(r, n), W0:W1, :] = u if U is None else u + ld(B, r, n, W0, W1)
    rows_loop(3, 60, stage_c)
    zero_edges(edge, U1)

    def stage_d(r, n):
        c, s, d = around(ld(U1, r - 1, n + 2, W0, W1), closed)
        src = (0.5 / 6.0) * d[:, m]
        SRC[pl.ds(r, n), M0:M1, :] = src
        B[pl.ds(r, n), M0:M1, :] = 0.35 * c[:, m] + 0.1 * s[:, m]
        _, s, _ = around(ld(V, r - 1, n + 2, W0, W1), closed)
        Q[pl.ds(r, n), M0:M1, :] = s[:, m] * (1.0 / 6.0) - src
    rows_loop(3, 60, stage_d)
    finish(Q)

    def stage_e(r, n):
        _, s, _ = around(ld(Q, r - 1, n + 2), closed)
        V[pl.ds(r, n), M0:M1, :] = s * (1.0 / 6.0) - ld(SRC, r, n)
    rows_loop(4, 59, stage_e)
    finish(V)

    def stage_f(r, n):
        zp, zm = zshift(ld(V, r, n), closed)
        A[pl.ds(r, n), M0:M1, :] = ld(B, r, n) + 0.5 * (zp - zm)
    rows_loop(4, 59, stage_f)
    zero_edges(edge, A)


def adjoint(edge, window, A, pot, u1, B, SP, S2, T, A1, S3, T2, give):
    _, _, M0, M1, first, closed = window

    def ld(ref, r, n):
        return ref[pl.ds(r, n), M0:M1, :]

    def stage_g(r, n):
        c, s, d = around(ld(A, r - 1, n + 2), closed)
        B[pl.ds(r, n), M0:M1, :] = 0.35 * c + 0.1 * s
        sp = -0.5 * d
        if pot is not None:
            sp = sp + ld(pot, r, n)
        SP[pl.ds(r, n), M0:M1, :] = sp
    rows_loop(4, 59, stage_g)
    zero_edges(edge, SP)

    def stage_h(r, n):
        c, s, _ = around(ld(SP, r - 1, n + 2), closed)
        s = s * (1.0 / 6.0)
        S2[pl.ds(r, n), M0:M1, :] = s
        T[pl.ds(r, n), M0:M1, :] = (c + s) * (1.0 / 6.0)
    rows_loop(5, 58, stage_h)
    zero_edges(edge, S2)
    zero_edges(edge, T)

    def stage_i(r, n):
        _, s, _ = around(ld(S2, r - 1, n + 2), closed)
        S3[pl.ds(r, n), M0:M1, :] = s * (1.0 / 6.0)
        zp, zm = zshift(ld(T, r, n), closed)
        a = ld(B, r, n) + 0.5 * (zp - zm)
        if u1 is not None:
            a = a + ld(u1, r, n)
        A1[pl.ds(r, n), M0:M1, :] = a
    rows_loop(6, 57, stage_i)
    zero_edges(edge, A1)

    def stage_j(r, n):
        c, s, d = around(ld(A1, r - 1, n + 2), closed)
        B[pl.ds(r, n), M0:M1, :] = 0.35 * c + 0.1 * s
        SP[pl.ds(r, n), M0:M1, :] = ld(S3, r, n) - 0.5 * d
    rows_loop(6, 57, stage_j)
    zero_edges(edge, SP)

    def stage_k(r, n):
        c, s, _ = around(ld(SP, r - 1, n + 2), closed)
        s = s * (1.0 / 6.0)
        S2[pl.ds(r, n), M0:M1, :] = s
        T2[pl.ds(r, n), M0:M1, :] = (c + s) * (1.0 / 6.0)
    rows_loop(7, 56, stage_k)
    zero_edges(edge, S2)
    zero_edges(edge, T2)
    if give is None:
        return
    own = slice(first - M0, first - M0 + COLS)

    def stage_l(r, n):
        _, s, _ = around(ld(S2, r - 1, n + 2), closed)
        zp, zm = zshift(ld(T2, r, n), closed)
        u = ld(B, r, n) + 0.5 * (zp - zm)
        give(pl.ds(r - HY, n), u[:, own], s[:, own] * (1.0 / 6.0))
    rows_loop(8, 55, stage_l)


HALF = EXT // 2


def load_extended(dst, f, own, yd, yu, zd, zu):
    top = HY + ROWS
    dst[0:HY, ZO:ZO + COLS, :] = yd[f]
    dst[HY:top, ZO:ZO + COLS, :] = own[f]
    dst[top:, ZO:ZO + COLS, :] = yu[f]
    for z, near, far in ((zd, 8, 4), (zu, 32, 40)):
        dst[:, near:near + 8, :] = z[f, 0:EXT]
        dst[0:HALF, far:far + 4, :] = z[f, EXT:, 0:4, :]
        dst[HALF:, far:far + 4, :] = z[f, EXT:, 4:8, :]
    for z in (0, 44):
        dst[:, z:z + 4, :] = jnp.zeros((EXT, 4, LANES), jnp.float32)


def is_even(axis):
    return lax.rem(lax.axis_index(axis), 2) == 0


def pack_kernel(own, far, near, yd, yu, z_near, z_far):
    even = is_even("gy")
    yd[...] = jnp.where(even, far[...], near[...])
    yu[...] = jnp.where(even, near[...], far[...])

    def pack(dst, whole, part):
        for r0, r1, src in ((0, HY, yd), (HY, HY + ROWS, own), (HY + ROWS, EXT, yu)):
            dst[:, r0:r1] = src[:, :, whole:whole + 8, :]
        dst[:, EXT:EXT + HY, 0:4, :] = yd[:, :, part:part + 4, :]
        dst[:, EXT + HY:, 0:4, :] = own[:, 0:HALF - HY, part:part + 4, :]
        dst[:, EXT:EXT + HALF - HY, 4:8, :] = own[:, HALF - HY:, part:part + 4, :]
        dst[:, EXT + HALF - HY:, 4:8, :] = yu[:, :, part:part + 4, :]

    @pl.when(is_even("gz"))
    def _():
        pack(z_near, 8, 4)
        pack(z_far, 0, 8)

    @pl.when(jnp.logical_not(is_even("gz")))
    def _():
        pack(z_near, 0, 8)
        pack(z_far, 8, 4)


HIGHEST = lax.Precision.HIGHEST


def edges():
    gy, gz = lax.axis_index("gy"), lax.axis_index("gz")
    return (gy == 0, gy == lax.axis_size("gy") - 1, gz == 0, gz == lax.axis_size("gz") - 1)


def iota(shape, dim):
    return lax.broadcasted_iota(jnp.int32, shape, dim)


def tile_volts(first, second, labels):
    lab = jnp.broadcast_to(labels, first.shape) - 2 * iota(first.shape, 0)
    hit = jnp.where(lab == 0, first, 0.0) + jnp.where(lab == 1, second, 0.0)
    return jnp.sum(hit, axis=0, keepdims=True)


def fill_ghost(upper, ghost, volts):
    lane, row = iota((8, LANES), 1), iota((8, LANES), 0)
    apart = jnp.where((lane >> 4) == row, jnp.broadcast_to(volts, (8, LANES)), 0.0)
    spread = ((iota((LANES, LANES), 0) & 15) == (iota((LANES, LANES), 1) >> 3)).astype(jnp.float32)
    wall = jnp.dot(apart, spread, precision=HIGHEST, preferred_element_type=jnp.float32) * (1.0 / 6.0)
    layer = iota((COLS, LANES), 0) == jnp.where(upper, COLS - 1, 0)
    for ty in range(8):
        tile = jnp.where(layer, jnp.broadcast_to(wall[ty:ty + 1], (COLS, LANES)), 0.0)
        ghost[8 * ty:8 * ty + 8] = jnp.broadcast_to(tile[None], (8, COLS, LANES))


def wall_tiles(upper, T, T2, held):
    layer = iota((ROWS, COLS, LANES), 1) == jnp.where(upper, COLS - 1, 0)
    w = jnp.sum(jnp.where(layer, T[HY:HY + ROWS] + T2[HY:HY + ROWS], 0.0), axis=1)
    held[...] = jnp.zeros((8, LANES), jnp.float32)
    held[0:TY] = jnp.sum(w.reshape(TY, 8, LANES), axis=1)
    gather = ((iota((LANES, LANES), 0) >> 3) == (iota((LANES, LANES), 1) & 15)).astype(jnp.float32)
    sums = jnp.dot(held[...], gather, precision=HIGHEST, preferred_element_type=jnp.float32)
    keep = (iota((8, LANES), 1) >> 4) == iota((8, LANES), 0)
    return jnp.sum(jnp.where(keep, sums, 0.0), axis=0, keepdims=True)


def wall_kernel(own, yd, yu, volts, row, U, V, SRC, B, Q, U1, A, SP, S2, T, A1, S3, T2, held, sums):
    ylo, yhi, zlo, zhi = edges()
    edge = (ylo, yhi, None, None)
    is_forward = lax.axis_index("grp") == 0
    sums[...] = jnp.zeros((1, LANES), jnp.float32)

    @pl.when(jnp.logical_or(zlo, zhi))
    def _():
        for f, ref in ((0, U), (1, V)):
            ref[0:HY] = yd[f]
            ref[HY:HY + ROWS] = own[f]
            ref[HY + ROWS:] = yu[f]

        @pl.when(is_forward)
        def _():
            forward(edge, None, NEAR, U, V, SRC, B, Q, U1, A)
            adjoint(edge, NEAR, A, None, U1, B, SP, S2, T, A1, S3, T2, None)

        @pl.when(jnp.logical_not(is_forward))
        def _():
            adjoint(edge, NEAR, U, V, None, B, SP, S2, T, A1, S3, T2, None)

        sums[...] = wall_tiles(zhi, T, T2, held)

    lane = iota((1, LANES), 1)
    out = jnp.where(lane == VOLT, volts[0], jnp.where(lane == VOLT + 1, volts[1], sums[...]))
    row[...] = jnp.broadcast_to(out, row.shape)


def bulk_kernel(own, yd, yu, far, near, main, send, U, V, SRC, B, Q, U1, A, SP, S2, T, A1, S3, T2):
    edge = edges()
    is_forward = lax.axis_index("grp") == 0
    @pl.when(is_even("gz"))
    def _():
        load_extended(U, 0, own, yd, yu, far, near)
        load_extended(V, 1, own, yd, yu, far, near)

    @pl.when(jnp.logical_not(is_even("gz")))
    def _():
        load_extended(U, 0, own, yd, yu, near, far)
        load_extended(V, 1, own, yd, yu, near, far)

    def into(ref):
        def give(rows, u, p):
            ref[0, rows] = u
            ref[1, rows] = p
        return give

    @pl.when(is_forward)
    def _():
        forward(edge, None, BULK, U, V, SRC, B, Q, U1, A)
        main[0] = A[HY:HY + ROWS, ZO:ZO + COLS, :]
        main[1] = V[HY:HY + ROWS, ZO:ZO + COLS, :]
        adjoint(edge, BULK, A, None, U1, B, SP, S2, T, A1, S3, T2, into(send))

    @pl.when(jnp.logical_not(is_forward))
    def _():
        adjoint(edge, BULK, U, V, None, B, SP, S2, T, A1, S3, T2, into(main))


def volts_kernel(main, rows, near, labels, response, out, grad, V, SRC, B, Q, U1, A, SP, S2, T, A1, S3, T2, ghost):
    ylo, yhi, zlo, zhi = edges()
    edge = (ylo, yhi, None, None)
    is_forward = lax.axis_index("grp") == 0
    n = rows.shape[0]
    first = jnp.broadcast_to(rows[:, VOLT:VOLT + 1], (n, LANES))
    second = jnp.broadcast_to(rows[:, VOLT + 1:VOLT + 2], (n, LANES))

    @pl.when(jnp.logical_or(zlo, zhi))
    def _():
        fill_ghost(zhi, ghost, tile_volts(first, second, near[...]))
        forward(edge, ghost, NEAR, None, V, SRC, B, Q, U1, A)

        @pl.when(is_forward)
        def _():
            out[0] = main[0] + A[HY:HY + ROWS]
            out[1] = main[1] + V[HY:HY + ROWS]

        @pl.when(jnp.logical_not(is_forward))
        def _():
            def give(at, u, p):
                out[0, at] = main[0, at] + u
                out[1, at] = main[1, at] + p
            adjoint(edge, NEAR, A, None, U1, B, SP, S2, T, A1, S3, T2, give)

    @pl.when(jnp.logical_not(jnp.logical_or(zlo, zhi)))
    def _():
        out[...] = main[...]

    gy, gz = lax.axis_size("gy"), lax.axis_size("gz")
    me = (lax.axis_index("grp") * gy + lax.axis_index("gy")) * gz + lax.axis_index("gz")
    pair = [jnp.zeros((gy, LANES), jnp.float32)] * 2
    block = iota((gy, LANES), 0)
    for s in range(2):
        v = jnp.concatenate([tile_volts(first, second, labels[s, g:g + 1]) for g in range(gy)], axis=0)
        r = jnp.dot(v, response[...], precision=HIGHEST, preferred_element_type=jnp.float32)
        r = [r[:, k * LANES:(k + 1) * LANES] for k in range(5)]
        w = jnp.where(block == 0, r[3], jnp.where(block == gy - 1, r[4], r[0]))
        w = w + jnp.where(block == 0, 0.0, pltpu.roll(r[1], 1, 0))
        w = w + jnp.where(block == gy - 1, 0.0, pltpu.roll(r[2], gy - 1, 0))
        for g in range(2):
            w = w + rows[pl.ds(g * gy * gz + s * (gz - 1), gy, stride=gz), :]
        for j in range(2):
            pair[j] = pair[j] + jnp.where(labels[s] == 2 * me + j, w, 0.0)
    total = [jnp.sum(p) for p in pair]
    grad[...] = jnp.where(iota((1, 2), 1) == 0, total[0], total[1])


def sum_kernel(main, extra, out):
    out[0] = main[...] + extra[...]


def wall_response():
    def near_sum(f):
        g = np.pad(f, ((0, 0), (1, 1), (1, 1), (0, 0)))
        t = g[:, 2:, 1:-1] + g[:, :-2, 1:-1] + g[:, 1:-1, 2:] + g[:, 1:-1, :-2]
        return t + np.roll(f, 1, 3) + np.roll(f, -1, 3)

    def diff(f):
        g = np.pad(f, ((0, 0), (0, 0), (1, 1), (0, 0)))
        return g[:, :, 2:] - g[:, :, :-2]

    def sums(blocks, at):
        ghost = np.zeros((TY, blocks * ROWS, 13, LANES))
        for t in range(TY):
            ghost[t, at * ROWS + 8 * t:at * ROWS + 8 * t + 8, 0, 0:8] = 1.0
        u, p, states = np.zeros_like(ghost), np.zeros_like(ghost), []
        for _ in range(2):
            source = 0.5 * diff(u)
            for _ in range(2):
                p = (near_sum(p) + ghost - source) / 6.0
            u = 0.35 * u + 0.1 * near_sum(u) + 0.5 * diff(p)
            states.append(u)
        a, q, wall = np.zeros_like(ghost), np.zeros_like(ghost), 0.0
        for u in reversed(states):
            a = a + u
            spread, total = q - 0.5 * diff(a), 0.0
            for _ in range(2):
                total = total + spread / 6.0
                spread = near_sum(spread) / 6.0
            a = 0.35 * a + 0.1 * near_sum(a) + 0.5 * diff(total)
            q = spread
            wall = wall + total[:, :, 0]
        return wall.reshape(TY, blocks, TY, 8, 16, 8).sum((3, 5))

    def matrix(got):
        m = np.zeros((LANES, LANES), np.float32)
        for t in range(TY):
            for x in range(16):
                m[t * 16 + x, 0:TY * 16] = np.roll(got[t], x, 1).reshape(-1)
        return m

    middle, low, high = sums(3, 1), sums(2, 0), sums(2, 1)
    return np.concatenate([matrix(middle[:, 1]), matrix(middle[:, 2]), matrix(middle[:, 0]),
                           matrix(low[:, 0]), matrix(high[:, 1])], axis=1)


def vmem(n):
    return [pl.BlockSpec(memory_space=pltpu.VMEM)] * n


def shape(*dims):
    return jax.ShapeDtypeStruct(dims, jnp.float32)


def scratch(count, depth):
    return [pltpu.VMEM((EXT, depth, LANES), jnp.float32)] * count


def swapped(array, axis, first):
    pairs = []
    for i in range(first, lax.axis_size(axis) - 1, 2):
        pairs += [(i, i + 1), (i + 1, i)]
    return lax.ppermute(array, axis, pairs)


def per_device(response, field_pairs, tile_owner, electrode_volts):
    own = field_pairs[0]
    labels = tile_owner[..., 0]
    gy, gz = lax.axis_index("gy"), lax.axis_index("gz")
    devices = lax.axis_size(AXES)
    roomy = pltpu.CompilerParams(vmem_limit_bytes=40 * 1024 * 1024)
    middling = pltpu.CompilerParams(vmem_limit_bytes=24 * 1024 * 1024)
    tight = pltpu.CompilerParams(vmem_limit_bytes=8 * 1024 * 1024)
    block = shape(2, ROWS, COLS, LANES)

    even = is_even("gy")
    low, high = own[:, :HY], own[:, ROWS - HY:]
    far = swapped(jnp.where(even, low, high), "gy", 1)
    near = swapped(jnp.where(even, high, low), "gy", 0)
    rows_of, strip = shape(2, HY, COLS, LANES), shape(2, EXT * 3 // 2, 8, LANES)
    yd, yu, z_near, z_far = pl.pallas_call(
        pack_kernel, out_shape=(rows_of, rows_of, strip, strip),
        in_specs=vmem(3), out_specs=vmem(4), compiler_params=tight,
    )(own, far, near)
    far = swapped(z_far, "gz", 1)
    near = swapped(z_near, "gz", 0)

    mine, _ = lax.optimization_barrier((own, z_far))
    row = pl.pallas_call(
        wall_kernel, out_shape=shape(devices, LANES),
        in_specs=vmem(3) + [pl.BlockSpec(memory_space=pltpu.SMEM)], out_specs=vmem(1)[0],
        scratch_shapes=scratch(13, COLS) + [pltpu.VMEM((8, LANES), jnp.float32), pltpu.VMEM((1, LANES), jnp.float32)],
        compiler_params=middling,
    )(mine, yd, yu, electrode_volts)
    rows = lax.all_to_all(row, AXES, 0, 0, tiled=True)

    mine, _ = lax.optimization_barrier((own, row))
    main, send = pl.pallas_call(
        bulk_kernel, out_shape=(block, block), in_specs=vmem(5), out_specs=vmem(2),
        scratch_shapes=scratch(13, ZE), compiler_params=roomy,
        cost_estimate=pl.CostEstimate(flops=10 ** 8, bytes_accessed=36 * 10 ** 6, transcendentals=0),
    )(mine, yd, yu, far, near)
    send, rows = lax.optimization_barrier((send, rows))
    extra = lax.ppermute(send, "grp", [(0, 1)])

    fenced = jnp.pad(labels, ((0, 0), (1, 1), (0, 0)), constant_values=-1)
    side = (gz == lax.axis_size("gz") - 1).astype(jnp.int32)
    by_wall = lax.dynamic_slice(fenced, (side, gy * TY, 0), (1, 8, 16)).reshape(1, LANES)
    by_block = jnp.pad(labels.reshape(2, 8, TY * 16), ((0, 0), (0, 0), (0, LANES - TY * 16)), constant_values=-1)
    main, grad = pl.pallas_call(
        volts_kernel, out_shape=(block, shape(1, 2)), in_specs=vmem(5), out_specs=vmem(2),
        scratch_shapes=scratch(13, COLS), compiler_params=middling,
    )(main, rows, by_wall, by_block, response)
    advanced = pl.pallas_call(
        sum_kernel, out_shape=shape(1, 2, ROWS, COLS, LANES), in_specs=vmem(2), out_specs=vmem(1)[0],
        compiler_params=tight,
    )(main, extra)
    return (advanced, grad.reshape(2))


def solution(mesh):
    response = jnp.asarray(wall_response())
    placed = (P("grp", None, "gy", "gz", None), P(), P(AXES))
    return jax.shard_map(
        functools.partial(per_device, response), mesh=mesh, in_specs=placed,
        out_specs=(P("grp", None, "gy", "gz", None), P(AXES)), check_vma=False,
    )
```

```python
import functools

import jax
import jax.numpy as jnp
import numpy as np
from jax import lax
from jax.experimental import pallas as pl
from jax.experimental.pallas import tpu as pltpu
from jax.sharding import PartitionSpec as P

AXES = ("grp", "gy", "gz")
TY = 6
VOLT = TY * 16
ROWS, COLS, LANES = 48, 16, 128
HY, HZ = 8, 12
EXT = ROWS + 2 * HY
HALF = EXT // 2
PART = ROWS // 2
SIXTH = 1.0 / 6.0

BULK = ((12, 40), (8, 32), (4, 24))
NEAR = ((0, COLS),) * 3
LOWER = ((0, COLS), (0, 8), (0, 8))
UPPER = ((0, COLS), (-8, 8), (-8, 8))


def piece(outer, inner):
    start = outer[0] - inner[0]
    return slice(start, start + inner[1])


def rows_loop(first, last, body, pieces):
    n = (last - first + 1) // pieces
    for i in range(pieces):
        body(first + i * n, n)


def zshift(v, closed):
    z = v.shape[1]
    zp, zm = pltpu.roll(v, z - 1, 1), pltpu.roll(v, 1, 1)
    if closed:
        layer = lax.broadcasted_iota(jnp.int32, v.shape, 1)
        zp = jnp.where(layer == z - 1, 0.0, zp)
        zm = jnp.where(layer == 0, 0.0, zm)
    return zp, zm


def around(w, closed):
    c = w[1:-1]
    zp, zm = zshift(c, closed)
    s = (w[:-2] + w[2:]) + (zp + zm)
    s = s + (pltpu.roll(c, 1, 2) + pltpu.roll(c, LANES - 1, 2))
    return c, s, zp - zm


def zero_edges(edge, ref, at):
    ylo, yhi, zlo, zhi = edge
    rows, layers, _ = ref.shape

    def clear(when, index):
        if when is not None:
            @pl.when(when)
            def _():
                part = ref.at[index]
                part[...] = jnp.zeros(part.shape, jnp.float32)
    clear(ylo, pl.ds(HY - 1, 1))
    clear(yhi, pl.ds(rows - HY, 1))
    clear(zlo, (slice(None), pl.ds(at - 1, 1)))
    clear(zhi, (slice(None), pl.ds(at + COLS, 1)))


def early_scratch(rows, window):
    return [pltpu.VMEM((rows, window[0][1], LANES), jnp.float32)] * 6


def mid_scratch(rows, window):
    return [pltpu.VMEM((rows, window[1][1], LANES), jnp.float32)] * 7


def late_scratch(rows, window):
    return [pltpu.VMEM((rows, window[2][1], LANES), jnp.float32)] * 8


def scratch(rows, window):
    return early_scratch(rows, window) + mid_scratch(rows, window) + late_scratch(rows, window)


def forward(edge, ghost, window, pieces, early, mid):
    U, V, SRC, B, Q, U1 = early
    SRC2, B2, Q2, P2, A = mid[:5]
    top = U1.shape[0] - 1
    closed = window[0][0] == 0
    m = piece(window[0], window[1])
    first, second = window[0][0], window[1][0]

    def finish(ref, at):
        if ghost is not None:
            ref[...] += ghost[...]
        zero_edges(edge, ref, at)

    def stage_a(r, n):
        c, s, d = around(U[pl.ds(r - 1, n + 2)], closed)
        src = (0.5 / 6.0) * d
        SRC[pl.ds(r, n)] = src
        B[pl.ds(r, n)] = 0.35 * c + 0.1 * s
        _, s, _ = around(V[pl.ds(r - 1, n + 2)], closed)
        Q[pl.ds(r, n)] = s * SIXTH - src
    if ghost is not None:
        Q[...] = ghost[...]
        zero_edges(edge, Q, first)
    else:
        rows_loop(1, top - 1, stage_a, pieces)
        finish(Q, first)

    def stage_b(r, n):
        _, s, _ = around(Q[pl.ds(r - 1, n + 2)], closed)
        s = s * SIXTH
        V[pl.ds(r, n)] = s if ghost is not None else s - SRC[pl.ds(r, n)]
    rows_loop(2, top - 2, stage_b, pieces)
    finish(V, first)

    def stage_c(r, n):
        zp, zm = zshift(V[pl.ds(r, n)], closed)
        u = 0.5 * (zp - zm)
        U1[pl.ds(r, n)] = u if ghost is not None else u + B[pl.ds(r, n)]
    rows_loop(3, top - 3, stage_c, pieces)
    zero_edges(edge, U1, first)

    def stage_d(r, n):
        c, s, d = around(U1[pl.ds(r - 1, n + 2)], closed)
        src = (0.5 / 6.0) * d[:, m]
        SRC2[pl.ds(r, n)] = src
        B2[pl.ds(r, n)] = 0.35 * c[:, m] + 0.1 * s[:, m]
        _, s, _ = around(V[pl.ds(r - 1, n + 2)], closed)
        Q2[pl.ds(r, n)] = s[:, m] * SIXTH - src
    rows_loop(3, top - 3, stage_d, pieces)
    finish(Q2, second)

    def stage_e(r, n):
        _, s, _ = around(Q2[pl.ds(r - 1, n + 2)], closed)
        P2[pl.ds(r, n)] = s * SIXTH - SRC2[pl.ds(r, n)]
    rows_loop(4, top - 4, stage_e, pieces)
    finish(P2, second)

    def stage_f(r, n):
        zp, zm = zshift(P2[pl.ds(r, n)], closed)
        A[pl.ds(r, n)] = B2[pl.ds(r, n)] + 0.5 * (zp - zm)
    rows_loop(4, top - 4, stage_f, pieces)
    zero_edges(edge, A, second)


def adjoint(edge, window, pieces, a2, pot, u1, mid, late, give):
    BM, SP = mid[5:7]
    S2, T, B, A1, S3, SP2, S4, T2 = late
    top = SP.shape[0] - 1
    closed = window[0][0] == 0
    second, third = window[1][0], window[2][0]
    m = piece(window[1], window[2])

    def take(source, inner, r, n):
        ref, place = source
        return ref[pl.ds(r, n), piece(place, inner), :]

    def stage_g(r, n):
        c, s, d = around(take(a2, window[1], r - 1, n + 2), closed)
        BM[pl.ds(r, n)] = 0.35 * c + 0.1 * s
        sp = -0.5 * d
        if pot is not None:
            sp = sp + take(pot, window[1], r, n)
        SP[pl.ds(r, n)] = sp
    rows_loop(4, top - 4, stage_g, pieces)
    zero_edges(edge, SP, second)

    def stage_h(r, n):
        c, s, _ = around(SP[pl.ds(r - 1, n + 2)], closed)
        c, s = c[:, m], s[:, m] * SIXTH
        S2[pl.ds(r, n)] = s
        T[pl.ds(r, n)] = (c + s) * SIXTH
    rows_loop(5, top - 5, stage_h, pieces)
    zero_edges(edge, S2, third)
    zero_edges(edge, T, third)

    def stage_i(r, n):
        _, s, _ = around(S2[pl.ds(r - 1, n + 2)], closed)
        S3[pl.ds(r, n)] = s * SIXTH
        zp, zm = zshift(T[pl.ds(r, n)], closed)
        a = BM[pl.ds(r, n), m, :] + 0.5 * (zp - zm)
        if u1 is not None:
            a = a + take(u1, window[2], r, n)
        A1[pl.ds(r, n)] = a
    rows_loop(6, top - 6, stage_i, pieces)
    zero_edges(edge, A1, third)

    def stage_j(r, n):
        if give is None:
            zp, zm = zshift(A1[pl.ds(r, n)], closed)
            d = zp - zm
        else:
            c, s, d = around(A1[pl.ds(r - 1, n + 2)], closed)
            B[pl.ds(r, n)] = 0.35 * c + 0.1 * s
        SP2[pl.ds(r, n)] = S3[pl.ds(r, n)] - 0.5 * d
    rows_loop(6, top - 6, stage_j, pieces)
    zero_edges(edge, SP2, third)

    def stage_k(r, n):
        c, s, _ = around(SP2[pl.ds(r - 1, n + 2)], closed)
        s = s * SIXTH
        S4[pl.ds(r, n)] = s
        T2[pl.ds(r, n)] = (c + s) * SIXTH
    rows_loop(7, top - 7, stage_k, pieces)
    zero_edges(edge, S4, third)
    zero_edges(edge, T2, third)
    if give is None:
        return
    own = slice(third, third + COLS)

    def stage_l(r, n):
        _, s, _ = around(S4[pl.ds(r - 1, n + 2)], closed)
        zp, zm = zshift(T2[pl.ds(r, n)], closed)
        u = B[pl.ds(r, n)] + 0.5 * (zp - zm)
        give(r - HY, n, u[:, own], s[:, own] * SIXTH)
    rows_loop(8, top - 8, stage_l, pieces)


def load_extended(dst, f, part, own, yd, yu, zd, zu):
    block = slice(HZ, HZ + COLS)
    n = PART + 2 * HY
    if part == 0:
        dst[0:HY, block, :] = yd[f]
        dst[HY:n, block, :] = own[f, 0:n - HY]
    else:
        dst[0:n - HY, block, :] = own[f, ROWS - n + HY:]
        dst[n - HY:n, block, :] = yu[f]
    r = part * PART
    for z, near, far in ((zd, 4, 0), (zu, HZ + COLS, HZ + COLS + 8)):
        dst[:, near:near + 8, :] = z[f, r:r + n]
        dst[0:HALF - r, far:far + 4, :] = z[f, EXT + r:EXT + HALF, 0:4, :]
        dst[HALF - r:n, far:far + 4, :] = z[f, EXT:EXT + r + n - HALF, 4:8, :]


def is_even(axis):
    return lax.rem(lax.axis_index(axis), 2) == 0


def strips_kernel(own, far, near):
    even = is_even("gy")
    low, high = own[:, 0:HY], own[:, ROWS - HY:]
    far[...] = jnp.where(even, low, high)
    near[...] = jnp.where(even, high, low)


def pack_kernel(own, far, near, yd, yu, z_near, z_far):
    even = is_even("gy")
    yd[...] = jnp.where(even, far[...], near[...])
    yu[...] = jnp.where(even, near[...], far[...])

    def pack(dst, whole, part):
        for r0, r1, src in ((0, HY, yd), (HY, HY + ROWS, own), (HY + ROWS, EXT, yu)):
            dst[:, r0:r1] = src[:, :, whole:whole + 8, :]
        dst[:, EXT:EXT + HY, 0:4, :] = yd[:, :, part:part + 4, :]
        dst[:, EXT + HY:, 0:4, :] = own[:, 0:HALF - HY, part:part + 4, :]
        dst[:, EXT:EXT + HALF - HY, 4:8, :] = own[:, HALF - HY:, part:part + 4, :]
        dst[:, EXT + HALF - HY:, 4:8, :] = yu[:, :, part:part + 4, :]

    @pl.when(is_even("gz"))
    def _():
        pack(z_near, 8, 4)
        pack(z_far, 0, 8)

    @pl.when(jnp.logical_not(is_even("gz")))
    def _():
        pack(z_near, 0, 8)
        pack(z_far, 8, 4)


HIGHEST = lax.Precision.HIGHEST


def edges():
    gy, gz = lax.axis_index("gy"), lax.axis_index("gz")
    return (gy == 0, gy == lax.axis_size("gy") - 1, gz == 0, gz == lax.axis_size("gz") - 1)


def iota(shape, dim):
    return lax.broadcasted_iota(jnp.int32, shape, dim)


def tile_volts(first, second, labels):
    lab = jnp.broadcast_to(labels, first.shape) - 2 * iota(first.shape, 0)
    hit = jnp.where(lab == 0, first, 0.0) + jnp.where(lab == 1, second, 0.0)
    return jnp.sum(hit, axis=0, keepdims=True)


def fill_ghost(upper, ghost, volts):
    lane, row = iota((8, LANES), 1), iota((8, LANES), 0)
    apart = jnp.where((lane >> 4) == row, jnp.broadcast_to(volts, (8, LANES)), 0.0)
    spread = ((iota((LANES, LANES), 0) & 15) == (iota((LANES, LANES), 1) >> 3)).astype(jnp.float32)
    wall = jnp.dot(apart, spread, precision=HIGHEST, preferred_element_type=jnp.float32) * (1.0 / 6.0)
    layer = iota((COLS, LANES), 0) == jnp.where(upper, COLS - 1, 0)
    for ty in range(8):
        tile = jnp.where(layer, jnp.broadcast_to(wall[ty:ty + 1], (COLS, LANES)), 0.0)
        ghost[8 * ty:8 * ty + 8] = jnp.broadcast_to(tile[None], (8, COLS, LANES))


def wall_tiles(layer, T, T2, held):
    at = slice(HY, HY + ROWS)
    w = T[at, layer, :] + T2[at, layer, :]
    held[...] = jnp.zeros((8, LANES), jnp.float32)
    held[0:TY] = jnp.sum(w.reshape(TY, 8, LANES), axis=1)
    gather = ((iota((LANES, LANES), 0) >> 3) == (iota((LANES, LANES), 1) & 15)).astype(jnp.float32)
    sums = jnp.dot(held[...], gather, precision=HIGHEST, preferred_element_type=jnp.float32)
    keep = (iota((8, LANES), 1) >> 4) == iota((8, LANES), 0)
    return jnp.sum(jnp.where(keep, sums, 0.0), axis=0, keepdims=True)


def split(refs):
    return refs[:6], refs[6:13], refs[13:21]


def wall_kernel(own, yd, yu, volts, row, *refs):
    early, mid, late = split(refs)
    held, sums = refs[21:]
    ylo, yhi, zlo, zhi = edges()
    edge = (ylo, yhi, None, None)
    is_forward = lax.axis_index("grp") == 0
    sums[...] = jnp.zeros((1, LANES), jnp.float32)

    @pl.when(jnp.logical_or(zlo, zhi))
    def _():
        for f in range(2):
            early[f][0:HY] = yd[f]
            early[f][HY:HY + ROWS] = own[f]
            early[f][HY + ROWS:] = yu[f]

    def side(window, layer):
        @pl.when(is_forward)
        def _():
            forward(edge, None, window, 2, early, mid)
            adjoint(edge, window, 2, (mid[4], window[1]), None, (early[5], window[0]), mid, late, None)

        @pl.when(jnp.logical_not(is_forward))
        def _():
            adjoint(edge, window, 2, (early[0], window[0]), (early[1], window[0]), None, mid, late, None)

        sums[...] = wall_tiles(layer, late[1], late[7], held)

    @pl.when(zlo)
    def _():
        side(LOWER, 0)

    @pl.when(zhi)
    def _():
        side(UPPER, 7)

    lane = iota((1, LANES), 1)
    out = jnp.where(lane == VOLT, volts[0], jnp.where(lane == VOLT + 1, volts[1], sums[...]))
    row[...] = jnp.broadcast_to(out, row.shape)


def bulk_kernel(part, own, yd, yu, far, near, main, send, *refs):
    early, mid, late = split(refs)
    ylo, yhi, zlo, zhi = edges()
    edge = (ylo, None, zlo, zhi) if part == 0 else (None, yhi, zlo, zhi)
    is_forward = lax.axis_index("grp") == 0

    @pl.when(is_even("gz"))
    def _():
        for f in range(2):
            load_extended(early[f], f, part, own, yd, yu, far, near)

    @pl.when(jnp.logical_not(is_even("gz")))
    def _():
        for f in range(2):
            load_extended(early[f], f, part, own, yd, yu, near, far)

    def into(ref):
        def give(r, n, u, p):
            ref[0, pl.ds(r, n)] = u
            ref[1, pl.ds(r, n)] = p
        return give

    @pl.when(is_forward)
    def _():
        forward(edge, None, BULK, 1, early, mid)
        at = (slice(HY, HY + PART), slice(BULK[1][0], BULK[1][0] + COLS))
        main[0] = mid[4][at]
        main[1] = mid[3][at]
        adjoint(edge, BULK, 1, (mid[4], BULK[1]), None, (early[5], BULK[0]), mid, late, into(send))

    @pl.when(jnp.logical_not(is_forward))
    def _():
        adjoint(edge, BULK, 1, (early[0], BULK[0]), (early[1], BULK[0]), None, mid, late, into(main))


def volts_kernel(lower, upper, rows, near, labels, response, out, grad, *refs):
    early, mid, late = split(refs)
    ghost = refs[21]
    ylo, yhi, zlo, zhi = edges()
    edge = (ylo, yhi, None, None)
    is_forward = lax.axis_index("grp") == 0
    n = rows.shape[0]
    first = jnp.broadcast_to(rows[:, VOLT:VOLT + 1], (n, LANES))
    second = jnp.broadcast_to(rows[:, VOLT + 1:VOLT + 2], (n, LANES))
    out[:, 0:PART] = lower[...]
    out[:, PART:] = upper[...]

    @pl.when(jnp.logical_or(zlo, zhi))
    def _():
        fill_ghost(zhi, ghost, tile_volts(first, second, near[...]))
        forward(edge, ghost, NEAR, 2, early, mid)

        @pl.when(is_forward)
        def _():
            out[0] += mid[4][HY:HY + ROWS]
            out[1] += mid[3][HY:HY + ROWS]

        @pl.when(jnp.logical_not(is_forward))
        def _():
            def give(r, n, u, p):
                out[0, pl.ds(r, n)] += u
                out[1, pl.ds(r, n)] += p
            adjoint(edge, NEAR, 2, (mid[4], NEAR[1]), None, (early[5], NEAR[0]), mid, late, give)

    gy, gz = lax.axis_size("gy"), lax.axis_size("gz")
    me = (lax.axis_index("grp") * gy + lax.axis_index("gy")) * gz + lax.axis_index("gz")
    pair = [jnp.zeros((gy, LANES), jnp.float32)] * 2
    block = iota((gy, LANES), 0)
    for s in range(2):
        v = jnp.concatenate([tile_volts(first, second, labels[s, g:g + 1]) for g in range(gy)], axis=0)
        r = jnp.dot(v, response[...], precision=HIGHEST, preferred_element_type=jnp.float32)
        r = [r[:, k * LANES:(k + 1) * LANES] for k in range(5)]
        w = jnp.where(block == 0, r[3], jnp.where(block == gy - 1, r[4], r[0]))
        w = w + jnp.where(block == 0, 0.0, pltpu.roll(r[1], 1, 0))
        w = w + jnp.where(block == gy - 1, 0.0, pltpu.roll(r[2], gy - 1, 0))
        for g in range(2):
            w = w + rows[pl.ds(g * gy * gz + s * (gz - 1), gy, stride=gz), :]
        for j in range(2):
            pair[j] = pair[j] + jnp.where(labels[s] == 2 * me + j, w, 0.0)
    total = [jnp.sum(p) for p in pair]
    grad[...] = jnp.where(iota((1, 2), 1) == 0, total[0], total[1])


def sum_kernel(main, lower, upper, out):
    out[0, :, 0:PART] = main[:, 0:PART] + lower[...]
    out[0, :, PART:] = main[:, PART:] + upper[...]


def wall_response():
    def near_sum(f):
        g = np.pad(f, ((0, 0), (1, 1), (1, 1), (0, 0)))
        t = g[:, 2:, 1:-1] + g[:, :-2, 1:-1] + g[:, 1:-1, 2:] + g[:, 1:-1, :-2]
        return t + np.roll(f, 1, 3) + np.roll(f, -1, 3)

    def diff(f):
        g = np.pad(f, ((0, 0), (0, 0), (1, 1), (0, 0)))
        return g[:, :, 2:] - g[:, :, :-2]

    def sums(blocks, at):
        ghost = np.zeros((TY, blocks * ROWS, 13, LANES))
        for t in range(TY):
            ghost[t, at * ROWS + 8 * t:at * ROWS + 8 * t + 8, 0, 0:8] = 1.0
        u, p, states = np.zeros_like(ghost), np.zeros_like(ghost), []
        for _ in range(2):
            source = 0.5 * diff(u)
            for _ in range(2):
                p = (near_sum(p) + ghost - source) / 6.0
            u = 0.35 * u + 0.1 * near_sum(u) + 0.5 * diff(p)
            states.append(u)
        a, q, wall = np.zeros_like(ghost), np.zeros_like(ghost), 0.0
        for u in reversed(states):
            a = a + u
            spread, total = q - 0.5 * diff(a), 0.0
            for _ in range(2):
                total = total + spread / 6.0
                spread = near_sum(spread) / 6.0
            a = 0.35 * a + 0.1 * near_sum(a) + 0.5 * diff(total)
            q = spread
            wall = wall + total[:, :, 0]
        return wall.reshape(TY, blocks, TY, 8, 16, 8).sum((3, 5))

    def matrix(got):
        m = np.zeros((LANES, LANES), np.float32)
        for t in range(TY):
            for x in range(16):
                m[t * 16 + x, 0:TY * 16] = np.roll(got[t], x, 1).reshape(-1)
        return m

    middle, low, high = sums(3, 1), sums(2, 0), sums(2, 1)
    return np.concatenate([matrix(middle[:, 1]), matrix(middle[:, 2]), matrix(middle[:, 0]),
                           matrix(low[:, 0]), matrix(high[:, 1])], axis=1)


def vmem(n):
    return [pl.BlockSpec(memory_space=pltpu.VMEM)] * n


def shape(*dims):
    return jax.ShapeDtypeStruct(dims, jnp.float32)


def swapped(array, axis, first):
    pairs = []
    for i in range(first, lax.axis_size(axis) - 1, 2):
        pairs += [(i, i + 1), (i + 1, i)]
    return lax.ppermute(array, axis, pairs)


def per_device(response, field_pairs, tile_owner, electrode_volts):
    own = field_pairs[0]
    labels = tile_owner[..., 0]
    gy, gz = lax.axis_index("gy"), lax.axis_index("gz")
    devices = lax.axis_size(AXES)
    half = shape(2, PART, COLS, LANES)
    strip, slab = shape(2, HY, COLS, LANES), shape(2, EXT * 3 // 2, 8, LANES)

    def limit(mib):
        return pltpu.CompilerParams(vmem_limit_bytes=mib * 1024 * 1024)

    far, near = pl.pallas_call(
        strips_kernel, out_shape=(strip, strip), in_specs=vmem(1), out_specs=vmem(2), compiler_params=limit(4),
    )(own)
    far = swapped(far, "gy", 1)
    near = swapped(near, "gy", 0)
    yd, yu, z_near, z_far = pl.pallas_call(
        pack_kernel, out_shape=(strip, strip, slab, slab), in_specs=vmem(3), out_specs=vmem(4), compiler_params=limit(8),
    )(own, far, near)
    far = swapped(z_far, "gz", 1)
    near = swapped(z_near, "gz", 0)

    mine, _ = lax.optimization_barrier((own, z_far))
    row = pl.pallas_call(
        wall_kernel, out_shape=shape(devices, LANES),
        in_specs=vmem(3) + [pl.BlockSpec(memory_space=pltpu.SMEM)], out_specs=vmem(1)[0],
        scratch_shapes=scratch(EXT, LOWER) + [pltpu.VMEM((8, LANES), jnp.float32), pltpu.VMEM((1, LANES), jnp.float32)],
        compiler_params=limit(12),
    )(mine, yd, yu, electrode_volts)
    rows = lax.all_to_all(row, AXES, 0, 0, tiled=True)

    mine, _ = lax.optimization_barrier((own, row))
    def bulk(part, block, load):
        return pl.pallas_call(
            functools.partial(bulk_kernel, part), out_shape=(half, half), in_specs=vmem(5), out_specs=vmem(2),
            scratch_shapes=scratch(PART + 2 * HY, BULK), compiler_params=limit(20),
            cost_estimate=pl.CostEstimate(flops=10 ** 8, bytes_accessed=load * 10 ** 6, transcendentals=0),
        )(block, yd, yu, far, near)

    main0, send = bulk(0, mine, 36)
    lower = lax.ppermute(send, "grp", [(0, 1)])
    mine, _ = lax.optimization_barrier((own, send))
    main1, send = bulk(1, mine, 9)
    send, rows = lax.optimization_barrier((send, rows))
    upper = lax.ppermute(send, "grp", [(0, 1)])

    fenced = jnp.pad(labels, ((0, 0), (1, 1), (0, 0)), constant_values=-1)
    side = (gz == lax.axis_size("gz") - 1).astype(jnp.int32)
    by_wall = lax.dynamic_slice(fenced, (side, gy * TY, 0), (1, 8, 16)).reshape(1, LANES)
    by_block = jnp.pad(labels.reshape(2, 8, TY * 16), ((0, 0), (0, 0), (0, LANES - TY * 16)), constant_values=-1)
    total, grad = pl.pallas_call(
        volts_kernel, out_shape=(shape(2, ROWS, COLS, LANES), shape(1, 2)), in_specs=vmem(6), out_specs=vmem(2),
        scratch_shapes=scratch(EXT, NEAR) + [pltpu.VMEM((EXT, COLS, LANES), jnp.float32)], compiler_params=limit(16),
    )(main0, main1, rows, by_wall, by_block, response)
    advanced = pl.pallas_call(
        sum_kernel, out_shape=shape(1, 2, ROWS, COLS, LANES), in_specs=vmem(3), out_specs=vmem(1)[0],
        compiler_params=limit(8),
    )(total, lower, upper)
    return (advanced, grad.reshape(2))


def solution(mesh):
    response = jnp.asarray(wall_response())
    placed = (P("grp", None, "gy", "gz", None), P(), P(AXES))
    return jax.shard_map(
        functools.partial(per_device, response), mesh=mesh, in_specs=placed,
        out_specs=(P("grp", None, "gy", "gz", None), P(AXES)), check_vma=False,
    )
```

```python
import functools

import jax
import jax.numpy as jnp
import numpy as np
from jax import lax
from jax.experimental import pallas as pl
from jax.experimental.pallas import tpu as pltpu
from jax.sharding import PartitionSpec as P

AXES = ("grp", "gy", "gz")
TY = 6
VOLT = TY * 16
ROWS, COLS, LANES = 48, 16, 128
HY, HZ = 8, 12
EXT = ROWS + 2 * HY
RIM = 4
HALF = EXT // 2 - RIM
PARTS = 2
PART = ROWS // PARTS
SIXTH = 1.0 / 6.0
SHARE, PIECES = 0.34, 3

BULK = ((12, 40), (8, 32), (4, 24))
NEAR = ((0, COLS),) * 3
LOWER = ((0, COLS), (0, 8), (0, 8))
UPPER = ((0, COLS), (-8, 8), (-8, 8))


def piece(outer, inner):
    start = outer[0] - inner[0]
    return slice(start, start + inner[1])


def rows_loop(first, last, body, pieces):
    n = (last - first + 1) // pieces
    for i in range(pieces):
        body(first + i * n, n)


def zshift(v, closed):
    z = v.shape[1]
    zp, zm = pltpu.roll(v, z - 1, 1), pltpu.roll(v, 1, 1)
    if closed:
        layer = lax.broadcasted_iota(jnp.int32, v.shape, 1)
        zp = jnp.where(layer == z - 1, 0.0, zp)
        zm = jnp.where(layer == 0, 0.0, zm)
    return zp, zm


def beside(c):
    n, z, _ = c.shape
    k = int(n * SHARE)
    row = lax.broadcasted_iota(jnp.int32, (LANES, LANES), 0)
    lane = lax.broadcasted_iota(jnp.int32, (LANES, LANES), 1)
    apart = (row - lane) & (LANES - 1)
    ring = jnp.where((apart == 1) | (apart == LANES - 1), 1.0, 0.0).astype(jnp.bfloat16)
    rest, total = c[:k].reshape(k * z, LANES), None
    for i in range(PIECES):
        part = rest.astype(jnp.bfloat16)
        got = jnp.dot(part, ring, preferred_element_type=jnp.float32)
        total = got if total is None else total + got
        if i < PIECES - 1:
            rest = rest - part.astype(jnp.float32)
    rolled = pltpu.roll(c[k:], 1, 2) + pltpu.roll(c[k:], LANES - 1, 2)
    return jnp.concatenate([total.reshape(k, z, LANES), rolled], axis=0)


def around(w, closed):
    c = w[1:-1]
    zp, zm = zshift(c, closed)
    s = (w[:-2] + w[2:]) + (zp + zm)
    return c, s + beside(c), zp - zm


def zero_edges(edge, ref, at):
    ylo, yhi, zlo, zhi = edge
    rows, layers, _ = ref.shape

    def clear(when, index):
        if when is not None:
            @pl.when(when)
            def _():
                part = ref.at[index]
                part[...] = jnp.zeros(part.shape, jnp.float32)
    clear(ylo, pl.ds(HY - 1, 1))
    clear(yhi, pl.ds(rows - HY, 1))
    clear(zlo, (slice(None), pl.ds(at - 1, 1)))
    clear(zhi, (slice(None), pl.ds(at + COLS, 1)))


def early_scratch(rows, window):
    return [pltpu.VMEM((rows, window[0][1], LANES), jnp.float32)] * 6


def mid_scratch(rows, window):
    return [pltpu.VMEM((rows, window[1][1], LANES), jnp.float32)] * 7


def late_scratch(rows, window):
    return [pltpu.VMEM((rows, window[2][1], LANES), jnp.float32)] * 8


def scratch(rows, window):
    return early_scratch(rows, window) + mid_scratch(rows, window) + late_scratch(rows, window)


def forward(edge, ghost, window, pieces, early, mid):
    U, V, SRC, B, Q, U1 = early
    SRC2, B2, Q2, P2, A = mid[:5]
    top = U1.shape[0] - 1
    closed = window[0][0] == 0
    m = piece(window[0], window[1])
    first, second = window[0][0], window[1][0]

    def finish(ref, at):
        if ghost is not None:
            ref[...] += ghost[...]
        zero_edges(edge, ref, at)

    def stage_a(r, n):
        c, s, d = around(U[pl.ds(r - 1, n + 2)], closed)
        src = (0.5 / 6.0) * d
        SRC[pl.ds(r, n)] = src
        B[pl.ds(r, n)] = 0.35 * c + 0.1 * s
        _, s, _ = around(V[pl.ds(r - 1, n + 2)], closed)
        Q[pl.ds(r, n)] = s * SIXTH - src
    if ghost is not None:
        Q[...] = ghost[...]
        zero_edges(edge, Q, first)
    else:
        rows_loop(1, top - 1, stage_a, pieces)
        finish(Q, first)

    def stage_b(r, n):
        _, s, _ = around(Q[pl.ds(r - 1, n + 2)], closed)
        s = s * SIXTH
        V[pl.ds(r, n)] = s if ghost is not None else s - SRC[pl.ds(r, n)]
    rows_loop(2, top - 2, stage_b, pieces)
    finish(V, first)

    def stage_c(r, n):
        zp, zm = zshift(V[pl.ds(r, n)], closed)
        u = 0.5 * (zp - zm)
        U1[pl.ds(r, n)] = u if ghost is not None else u + B[pl.ds(r, n)]
    rows_loop(3, top - 3, stage_c, pieces)
    zero_edges(edge, U1, first)

    def stage_d(r, n):
        c, s, d = around(U1[pl.ds(r - 1, n + 2)], closed)
        src = (0.5 / 6.0) * d[:, m]
        SRC2[pl.ds(r, n)] = src
        B2[pl.ds(r, n)] = 0.35 * c[:, m] + 0.1 * s[:, m]
        _, s, _ = around(V[pl.ds(r - 1, n + 2)], closed)
        Q2[pl.ds(r, n)] = s[:, m] * SIXTH - src
    rows_loop(3, top - 3, stage_d, pieces)
    finish(Q2, second)

    def stage_e(r, n):
        _, s, _ = around(Q2[pl.ds(r - 1, n + 2)], closed)
        P2[pl.ds(r, n)] = s * SIXTH - SRC2[pl.ds(r, n)]
    rows_loop(4, top - 4, stage_e, pieces)
    finish(P2, second)

    def stage_f(r, n):
        zp, zm = zshift(P2[pl.ds(r, n)], closed)
        A[pl.ds(r, n)] = B2[pl.ds(r, n)] + 0.5 * (zp - zm)
    rows_loop(4, top - 4, stage_f, pieces)
    zero_edges(edge, A, second)


def adjoint(edge, window, pieces, a2, pot, u1, mid, late, give):
    BM, SP = mid[5:7]
    S2, T, B, A1, S3, SP2, S4, T2 = late
    top = SP.shape[0] - 1
    closed = window[0][0] == 0
    second, third = window[1][0], window[2][0]
    m = piece(window[1], window[2])

    def take(source, inner, r, n):
        ref, place = source
        return ref[pl.ds(r, n), piece(place, inner), :]

    def stage_g(r, n):
        c, s, d = around(take(a2, window[1], r - 1, n + 2), closed)
        BM[pl.ds(r, n)] = 0.35 * c + 0.1 * s
        sp = -0.5 * d
        if pot is not None:
            sp = sp + take(pot, window[1], r, n)
        SP[pl.ds(r, n)] = sp
    rows_loop(4, top - 4, stage_g, pieces)
    zero_edges(edge, SP, second)

    def stage_h(r, n):
        c, s, _ = around(SP[pl.ds(r - 1, n + 2)], closed)
        c, s = c[:, m], s[:, m] * SIXTH
        S2[pl.ds(r, n)] = s
        T[pl.ds(r, n)] = (c + s) * SIXTH
    rows_loop(5, top - 5, stage_h, pieces)
    zero_edges(edge, S2, third)
    zero_edges(edge, T, third)

    def stage_i(r, n):
        _, s, _ = around(S2[pl.ds(r - 1, n + 2)], closed)
        S3[pl.ds(r, n)] = s * SIXTH
        zp, zm = zshift(T[pl.ds(r, n)], closed)
        a = BM[pl.ds(r, n), m, :] + 0.5 * (zp - zm)
        if u1 is not None:
            a = a + take(u1, window[2], r, n)
        A1[pl.ds(r, n)] = a
    rows_loop(6, top - 6, stage_i, pieces)
    zero_edges(edge, A1, third)

    def stage_j(r, n):
        if give is None:
            zp, zm = zshift(A1[pl.ds(r, n)], closed)
            d = zp - zm
        else:
            c, s, d = around(A1[pl.ds(r - 1, n + 2)], closed)
            B[pl.ds(r, n)] = 0.35 * c + 0.1 * s
        SP2[pl.ds(r, n)] = S3[pl.ds(r, n)] - 0.5 * d
    rows_loop(6, top - 6, stage_j, pieces)
    zero_edges(edge, SP2, third)

    def stage_k(r, n):
        c, s, _ = around(SP2[pl.ds(r - 1, n + 2)], closed)
        s = s * SIXTH
        S4[pl.ds(r, n)] = s
        T2[pl.ds(r, n)] = (c + s) * SIXTH
    rows_loop(7, top - 7, stage_k, pieces)
    zero_edges(edge, S4, third)
    zero_edges(edge, T2, third)
    if give is None:
        return
    own = slice(third, third + COLS)

    def stage_l(r, n):
        _, s, _ = around(S4[pl.ds(r - 1, n + 2)], closed)
        zp, zm = zshift(T2[pl.ds(r, n)], closed)
        u = B[pl.ds(r, n)] + 0.5 * (zp - zm)
        give(r - HY, n, u[:, own], s[:, own] * SIXTH)
    rows_loop(8, top - 8, stage_l, pieces)


def load_extended(dst, f, part, own, yd, yu, below, above):
    first, end = part * PART, part * PART + PART + 2 * HY
    top = HY + ROWS

    def rows(src_first, src_end, src, offset, layers, to_layer):
        r0, r1 = max(first, src_first), min(end, src_end)
        if r0 < r1:
            at = slice(offset + r0 - src_first, offset + r1 - src_first)
            dst[r0 - first:r1 - first, to_layer:to_layer + layers.stop - layers.start, :] = src[f, at, layers, :]

    block, tile = slice(0, COLS), slice(0, 8)
    rows(0, HY, yd, 0, block, HZ)
    rows(HY, top, own, 0, block, HZ)
    rows(top, EXT, yu, 0, block, HZ)
    for (z, rest), near, far in ((below, 4, 0), (above, HZ + COLS, HZ + COLS + 8)):
        rows(HY, top, z, 0, tile, near)
        rows(0, HY, rest, 0, tile, near)
        rows(top, EXT, rest, HY, tile, near)
        for k in range(2):
            rows(RIM + k * HALF, RIM + (k + 1) * HALF, rest, 2 * HY, slice(4 * k, 4 * k + 4), far)


def is_even(axis):
    return lax.rem(lax.axis_index(axis), 2) == 0


def strips_kernel(own, far, near):
    even = is_even("gy")
    low, high = own[:, 0:HY], own[:, ROWS - HY:]
    far[...] = jnp.where(even, low, high)
    near[...] = jnp.where(even, high, low)


def tiles_kernel(own, near, far):
    even = is_even("gz")
    low, high = own[:, :, 0:8, :], own[:, :, 8:16, :]
    near[...] = jnp.where(even, high, low)
    far[...] = jnp.where(even, low, high)


def pack_kernel(own, far, near, yd, yu, z_near, z_far):
    even = is_even("gy")
    yd[...] = jnp.where(even, far[...], near[...])
    yu[...] = jnp.where(even, near[...], far[...])

    def pack(dst, whole, part):
        dst[:, 0:HY] = yd[:, :, whole:whole + 8, :]
        dst[:, HY:2 * HY] = yu[:, :, whole:whole + 8, :]
        at, edge = 2 * HY, HY - RIM
        dst[:, at:at + edge, 0:4, :] = yd[:, RIM:, part:part + 4, :]
        dst[:, at + edge:, 0:4, :] = own[:, 0:HALF - edge, part:part + 4, :]
        dst[:, at:at + HALF - edge, 4:8, :] = own[:, HALF - edge:, part:part + 4, :]
        dst[:, at + HALF - edge:, 4:8, :] = yu[:, 0:edge, part:part + 4, :]

    @pl.when(is_even("gz"))
    def _():
        pack(z_near, 8, 4)
        pack(z_far, 0, 8)

    @pl.when(jnp.logical_not(is_even("gz")))
    def _():
        pack(z_near, 0, 8)
        pack(z_far, 8, 4)


HIGHEST = lax.Precision.HIGHEST


def edges():
    gy, gz = lax.axis_index("gy"), lax.axis_index("gz")
    return (gy == 0, gy == lax.axis_size("gy") - 1, gz == 0, gz == lax.axis_size("gz") - 1)


def iota(shape, dim):
    return lax.broadcasted_iota(jnp.int32, shape, dim)


def tile_volts(first, second, labels):
    lab = jnp.broadcast_to(labels, first.shape) - 2 * iota(first.shape, 0)
    hit = jnp.where(lab == 0, first, 0.0) + jnp.where(lab == 1, second, 0.0)
    return jnp.sum(hit, axis=0, keepdims=True)


def fill_ghost(upper, ghost, volts):
    lane, row = iota((8, LANES), 1), iota((8, LANES), 0)
    apart = jnp.where((lane >> 4) == row, jnp.broadcast_to(volts, (8, LANES)), 0.0)
    spread = ((iota((LANES, LANES), 0) & 15) == (iota((LANES, LANES), 1) >> 3)).astype(jnp.float32)
    wall = jnp.dot(apart, spread, precision=HIGHEST, preferred_element_type=jnp.float32) * (1.0 / 6.0)
    layer = iota((COLS, LANES), 0) == jnp.where(upper, COLS - 1, 0)
    for ty in range(8):
        tile = jnp.where(layer, jnp.broadcast_to(wall[ty:ty + 1], (COLS, LANES)), 0.0)
        ghost[8 * ty:8 * ty + 8] = jnp.broadcast_to(tile[None], (8, COLS, LANES))


def wall_tiles(layer, T, T2, held):
    at = slice(HY, HY + ROWS)
    w = T[at, layer, :] + T2[at, layer, :]
    held[...] = jnp.zeros((8, LANES), jnp.float32)
    held[0:TY] = jnp.sum(w.reshape(TY, 8, LANES), axis=1)
    gather = ((iota((LANES, LANES), 0) >> 3) == (iota((LANES, LANES), 1) & 15)).astype(jnp.float32)
    sums = jnp.dot(held[...], gather, precision=HIGHEST, preferred_element_type=jnp.float32)
    keep = (iota((8, LANES), 1) >> 4) == iota((8, LANES), 0)
    return jnp.sum(jnp.where(keep, sums, 0.0), axis=0, keepdims=True)


def split(refs):
    return refs[:6], refs[6:13], refs[13:21]


def wall_kernel(own, yd, yu, volts, row, *refs):
    early, mid, late = split(refs)
    held, sums = refs[21:]
    ylo, yhi, zlo, zhi = edges()
    edge = (ylo, yhi, None, None)
    is_forward = lax.axis_index("grp") == 0
    sums[...] = jnp.zeros((1, LANES), jnp.float32)

    @pl.when(jnp.logical_or(zlo, zhi))
    def _():
        for f in range(2):
            early[f][0:HY] = yd[f]
            early[f][HY:HY + ROWS] = own[f]
            early[f][HY + ROWS:] = yu[f]

    def side(window, layer):
        @pl.when(is_forward)
        def _():
            forward(edge, None, window, 1, early, mid)
            adjoint(edge, window, 1, (mid[4], window[1]), None, (early[5], window[0]), mid, late, None)

        @pl.when(jnp.logical_not(is_forward))
        def _():
            adjoint(edge, window, 1, (early[0], window[0]), (early[1], window[0]), None, mid, late, None)

        sums[...] = wall_tiles(layer, late[1], late[7], held)

    @pl.when(zlo)
    def _():
        side(LOWER, 0)

    @pl.when(zhi)
    def _():
        side(UPPER, 7)

    row[...] = jnp.broadcast_to(sums[...] + volts[...], row.shape)


def bulk_kernel(part, own, yd, yu, z_far, z_near, far, near, main, send, *refs):
    far, near = (z_far, far), (z_near, near)
    early, mid, late = split(refs)
    ylo, yhi, zlo, zhi = edges()
    edge = (ylo if part == 0 else None, yhi if part == PARTS - 1 else None, zlo, zhi)
    is_forward = lax.axis_index("grp") == 0

    @pl.when(is_even("gz"))
    def _():
        for f in range(2):
            load_extended(early[f], f, part, own, yd, yu, far, near)

    @pl.when(jnp.logical_not(is_even("gz")))
    def _():
        for f in range(2):
            load_extended(early[f], f, part, own, yd, yu, near, far)

    def into(ref):
        def give(r, n, u, p):
            ref[0, pl.ds(r, n)] = u
            ref[1, pl.ds(r, n)] = p
        return give

    @pl.when(is_forward)
    def _():
        forward(edge, None, BULK, 1, early, mid)
        at = (slice(HY, HY + PART), slice(BULK[1][0], BULK[1][0] + COLS))
        main[0] = mid[4][at]
        main[1] = mid[3][at]
        adjoint(edge, BULK, 1, (mid[4], BULK[1]), None, (early[5], BULK[0]), mid, late, into(send))

    @pl.when(jnp.logical_not(is_forward))
    def _():
        adjoint(edge, BULK, 1, (early[0], BULK[0]), (early[1], BULK[0]), None, mid, late, into(main))


def volts_kernel(*refs):
    parts, refs = refs[:PARTS], refs[PARTS:]
    rows, near, labels, response, out, grad = refs[:6]
    early, mid, late = split(refs[6:])
    ghost = refs[27]
    ylo, yhi, zlo, zhi = edges()
    edge = (ylo, yhi, None, None)
    is_forward = lax.axis_index("grp") == 0
    n = rows.shape[0]
    first = jnp.broadcast_to(rows[:, VOLT:VOLT + 1], (n, LANES))
    second = jnp.broadcast_to(rows[:, VOLT + 1:VOLT + 2], (n, LANES))
    for i, part in enumerate(parts):
        out[:, i * PART:(i + 1) * PART] = part[...]

    @pl.when(jnp.logical_or(zlo, zhi))
    def _():
        fill_ghost(zhi, ghost, tile_volts(first, second, near[...]))
        forward(edge, ghost, NEAR, 2, early, mid)

        @pl.when(is_forward)
        def _():
            out[0] += mid[4][HY:HY + ROWS]
            out[1] += mid[3][HY:HY + ROWS]

        @pl.when(jnp.logical_not(is_forward))
        def _():
            def give(r, n, u, p):
                out[0, pl.ds(r, n)] += u
                out[1, pl.ds(r, n)] += p
            adjoint(edge, NEAR, 2, (mid[4], NEAR[1]), None, (early[5], NEAR[0]), mid, late, give)

    gy, gz = lax.axis_size("gy"), lax.axis_size("gz")
    me = (lax.axis_index("grp") * gy + lax.axis_index("gy")) * gz + lax.axis_index("gz")
    pair = [jnp.zeros((gy, LANES), jnp.float32)] * 2
    block = iota((gy, LANES), 0)
    for s in range(2):
        v = jnp.concatenate([tile_volts(first, second, labels[s, g:g + 1]) for g in range(gy)], axis=0)
        r = jnp.dot(v, response[...], precision=HIGHEST, preferred_element_type=jnp.float32)
        r = [r[:, k * LANES:(k + 1) * LANES] for k in range(5)]
        w = jnp.where(block == 0, r[3], jnp.where(block == gy - 1, r[4], r[0]))
        w = w + jnp.where(block == 0, 0.0, pltpu.roll(r[1], 1, 0))
        w = w + jnp.where(block == gy - 1, 0.0, pltpu.roll(r[2], gy - 1, 0))
        for g in range(2):
            w = w + rows[pl.ds(g * gy * gz + s * (gz - 1), gy, stride=gz), :]
        for j in range(2):
            pair[j] = pair[j] + jnp.where(labels[s] == 2 * me + j, w, 0.0)
    total = [jnp.sum(p) for p in pair]
    grad[...] = jnp.where(iota((1, 2), 1) == 0, total[0], total[1])


def sum_kernel(main, *refs):
    out = refs[PARTS]
    for i in range(PARTS):
        at = slice(i * PART, (i + 1) * PART)
        out[0, :, at] = main[:, at] + refs[i][...]


def wall_response():
    def near_sum(f):
        g = np.pad(f, ((0, 0), (1, 1), (1, 1), (0, 0)))
        t = g[:, 2:, 1:-1] + g[:, :-2, 1:-1] + g[:, 1:-1, 2:] + g[:, 1:-1, :-2]
        return t + np.roll(f, 1, 3) + np.roll(f, -1, 3)

    def diff(f):
        g = np.pad(f, ((0, 0), (0, 0), (1, 1), (0, 0)))
        return g[:, :, 2:] - g[:, :, :-2]

    def sums(blocks, at):
        ghost = np.zeros((TY, blocks * ROWS, 13, LANES))
        for t in range(TY):
            ghost[t, at * ROWS + 8 * t:at * ROWS + 8 * t + 8, 0, 0:8] = 1.0
        u, p, states = np.zeros_like(ghost), np.zeros_like(ghost), []
        for _ in range(2):
            source = 0.5 * diff(u)
            for _ in range(2):
                p = (near_sum(p) + ghost - source) / 6.0
            u = 0.35 * u + 0.1 * near_sum(u) + 0.5 * diff(p)
            states.append(u)
        a, q, wall = np.zeros_like(ghost), np.zeros_like(ghost), 0.0
        for u in reversed(states):
            a = a + u
            spread, total = q - 0.5 * diff(a), 0.0
            for _ in range(2):
                total = total + spread / 6.0
                spread = near_sum(spread) / 6.0
            a = 0.35 * a + 0.1 * near_sum(a) + 0.5 * diff(total)
            q = spread
            wall = wall + total[:, :, 0]
        return wall.reshape(TY, blocks, TY, 8, 16, 8).sum((3, 5))

    def matrix(got):
        m = np.zeros((LANES, LANES), np.float32)
        for t in range(TY):
            for x in range(16):
                m[t * 16 + x, 0:TY * 16] = np.roll(got[t], x, 1).reshape(-1)
        return m

    middle, low, high = sums(3, 1), sums(2, 0), sums(2, 1)
    return np.concatenate([matrix(middle[:, 1]), matrix(middle[:, 2]), matrix(middle[:, 0]),
                           matrix(low[:, 0]), matrix(high[:, 1])], axis=1)


def vmem(n):
    return [pl.BlockSpec(memory_space=pltpu.VMEM)] * n


def shape(*dims):
    return jax.ShapeDtypeStruct(dims, jnp.float32)


def kept(*dims):
    return pltpu.VMEM(dims, jnp.float32)


def swapped(array, axis, first):
    pairs = []
    for i in range(first, lax.axis_size(axis) - 1, 2):
        pairs += [(i, i + 1), (i + 1, i)]
    return lax.ppermute(array, axis, pairs)


def per_device(response, field_pairs, tile_owner, electrode_volts):
    own = field_pairs[0]
    labels = tile_owner[..., 0]
    gy, gz = lax.axis_index("gy"), lax.axis_index("gz")
    devices = lax.axis_size(AXES)
    half = kept(2, PART, COLS, LANES)
    strip, tiles = kept(2, HY, COLS, LANES), kept(2, ROWS, 8, LANES)
    slab = kept(2, 2 * HY + HALF, 8, LANES)

    def limit(mib):
        return pltpu.CompilerParams(vmem_limit_bytes=mib * 1024 * 1024)

    far, near = pl.pallas_call(
        strips_kernel, out_shape=(strip, strip), in_specs=vmem(1), out_specs=vmem(2), compiler_params=limit(4),
    )(own)
    far = swapped(far, "gy", 1)
    near = swapped(near, "gy", 0)
    mine, near = lax.optimization_barrier((own, near))
    z_near, z_far = pl.pallas_call(
        tiles_kernel, out_shape=(tiles, tiles), in_specs=vmem(1), out_specs=vmem(2), compiler_params=limit(8),
    )(mine)
    z_far = swapped(z_far, "gz", 1)
    z_near = swapped(z_near, "gz", 0)
    yd, yu, near, far = pl.pallas_call(
        pack_kernel, out_shape=(strip, strip, slab, slab), in_specs=vmem(3), out_specs=vmem(4), compiler_params=limit(8),
    )(own, far, near)
    mine, _ = lax.optimization_barrier((own, far))
    far = swapped(far, "gz", 1)
    near = swapped(near, "gz", 0)

    volts = jnp.pad(electrode_volts, (VOLT, LANES - VOLT - 2))[None]
    row = pl.pallas_call(
        wall_kernel, out_shape=kept(devices, LANES),
        in_specs=vmem(4), out_specs=vmem(1)[0],
        scratch_shapes=scratch(EXT, LOWER) + [pltpu.VMEM((8, LANES), jnp.float32), pltpu.VMEM((1, LANES), jnp.float32)],
        compiler_params=limit(12),
    )(mine, yd, yu, volts)
    rows = lax.all_to_all(row, AXES, 0, 0, tiled=True)

    mine, _ = lax.optimization_barrier((own, row))
    def bulk(part, block, load):
        return pl.pallas_call(
            functools.partial(bulk_kernel, part), out_shape=(half, half), in_specs=vmem(7), out_specs=vmem(2),
            scratch_shapes=scratch(PART + 2 * HY, BULK), compiler_params=limit(20),
            cost_estimate=pl.CostEstimate(flops=10 ** 8, bytes_accessed=load * 10 ** 6, transcendentals=0),
        )(block, yd, yu, z_far, z_near, far, near)

    mains, extras = [], []
    for part in range(PARTS):
        main, send = bulk(part, mine, 36 if part == 0 else 9)
        mains.append(main)
        mine, _ = lax.optimization_barrier((own, send))
        if part == PARTS - 1:
            send, rows = lax.optimization_barrier((send, rows))
        extras.append(lax.ppermute(send, "grp", [(0, 1)]))

    fenced = jnp.pad(labels, ((0, 0), (1, 1), (0, 0)), constant_values=-1)
    side = (gz == lax.axis_size("gz") - 1).astype(jnp.int32)
    by_wall = lax.dynamic_slice(fenced, (side, gy * TY, 0), (1, 8, 16)).reshape(1, LANES)
    by_block = jnp.pad(labels.reshape(2, 8, TY * 16), ((0, 0), (0, 0), (0, LANES - TY * 16)), constant_values=-1)
    total, grad = pl.pallas_call(
        volts_kernel, out_shape=(kept(2, ROWS, COLS, LANES), shape(1, 2)), in_specs=vmem(PARTS + 4), out_specs=vmem(2),
        scratch_shapes=scratch(EXT, NEAR) + [pltpu.VMEM((EXT, COLS, LANES), jnp.float32)], compiler_params=limit(16),
    )(*mains, rows, by_wall, by_block, response)
    advanced = pl.pallas_call(
        sum_kernel, out_shape=shape(1, 2, ROWS, COLS, LANES), in_specs=vmem(PARTS + 1), out_specs=vmem(1)[0],
        compiler_params=limit(8),
    )(total, *extras)
    return (advanced, grad.reshape(2))


def solution(mesh):
    response = jnp.asarray(wall_response())
    placed = (P("grp", None, "gy", "gz", None), P(), P(AXES))
    return jax.shard_map(
        functools.partial(per_device, response), mesh=mesh, in_specs=placed,
        out_specs=(P("grp", None, "gy", "gz", None), P(AXES)), check_vma=False,
    )
```

```python
import functools

import jax
import jax.numpy as jnp
import numpy as np
from jax import lax
from jax.experimental import pallas as pl
from jax.experimental.pallas import tpu as pltpu
from jax.sharding import PartitionSpec as P

AXES = ("grp", "gy", "gz")
TY = 6
VOLT = TY * 16
ROWS, COLS, LANES = 48, 16, 128
HY, HZ = 8, 12
EXT = ROWS + 2 * HY
RIM = 4
HALF = EXT // 2 - RIM
PARTS = 3
PART = ROWS // PARTS
SIXTH = 1.0 / 6.0
SHARE, PIECES = 0.34, 3

BULK = ((12, 40), (8, 32), (4, 24))
NEAR = ((0, COLS),) * 3
LOWER = ((0, COLS), (0, 8), (0, 8))
UPPER = ((0, COLS), (-8, 8), (-8, 8))


def piece(outer, inner):
    start = outer[0] - inner[0]
    return slice(start, start + inner[1])


def rows_loop(first, last, body, pieces):
    n = (last - first + 1) // pieces
    for i in range(pieces):
        body(first + i * n, n)


def zshift(v, closed):
    z = v.shape[1]
    zp, zm = pltpu.roll(v, z - 1, 1), pltpu.roll(v, 1, 1)
    if closed:
        layer = lax.broadcasted_iota(jnp.int32, v.shape, 1)
        zp = jnp.where(layer == z - 1, 0.0, zp)
        zm = jnp.where(layer == 0, 0.0, zm)
    return zp, zm


def beside(c, share):
    n, z, _ = c.shape
    k = int(n * share)
    if k == 0:
        return pltpu.roll(c, 1, 2) + pltpu.roll(c, LANES - 1, 2)
    row = lax.broadcasted_iota(jnp.int32, (LANES, LANES), 0)
    lane = lax.broadcasted_iota(jnp.int32, (LANES, LANES), 1)
    apart = (row - lane) & (LANES - 1)
    ring = jnp.where((apart == 1) | (apart == LANES - 1), 1.0, 0.0).astype(jnp.bfloat16)
    rest, total = c[:k].reshape(k * z, LANES), None
    for i in range(PIECES):
        part = rest.astype(jnp.bfloat16)
        got = jnp.dot(part, ring, preferred_element_type=jnp.float32)
        total = got if total is None else total + got
        if i < PIECES - 1:
            rest = rest - part.astype(jnp.float32)
    rolled = pltpu.roll(c[k:], 1, 2) + pltpu.roll(c[k:], LANES - 1, 2)
    return jnp.concatenate([total.reshape(k, z, LANES), rolled], axis=0)


def around(w, closed):
    c = w[1:-1]
    zp, zm = zshift(c, closed)
    s = (w[:-2] + w[2:]) + (zp + zm)
    return c, s + beside(c, 0.0 if closed else SHARE), zp - zm


def zero_edges(edge, ref, at):
    ylo, yhi, zlo, zhi = edge
    rows, layers, _ = ref.shape

    def clear(when, index):
        if when is not None:
            @pl.when(when)
            def _():
                part = ref.at[index]
                part[...] = jnp.zeros(part.shape, jnp.float32)
    clear(ylo, pl.ds(HY - 1, 1))
    clear(yhi, pl.ds(rows - HY, 1))
    clear(zlo, (slice(None), pl.ds(at - 1, 1)))
    clear(zhi, (slice(None), pl.ds(at + COLS, 1)))


def early_scratch(rows, window):
    return [pltpu.VMEM((rows, window[0][1], LANES), jnp.float32)] * 6


def mid_scratch(rows, window):
    return [pltpu.VMEM((rows, window[1][1], LANES), jnp.float32)] * 7


def late_scratch(rows, window):
    return [pltpu.VMEM((rows, window[2][1], LANES), jnp.float32)] * 8


def scratch(rows, window):
    return early_scratch(rows, window) + mid_scratch(rows, window) + late_scratch(rows, window)


def forward(edge, ghost, window, pieces, early, mid):
    U, V, SRC, B, Q, U1 = early
    SRC2, B2, Q2, P2, A = mid[:5]
    top = U1.shape[0] - 1
    closed = window[0][0] == 0
    m = piece(window[0], window[1])
    first, second = window[0][0], window[1][0]

    def finish(ref, at):
        if ghost is not None:
            ref[...] += ghost[...]
        zero_edges(edge, ref, at)

    def stage_a(r, n):
        c, s, d = around(U[pl.ds(r - 1, n + 2)], closed)
        src = (0.5 / 6.0) * d
        SRC[pl.ds(r, n)] = src
        B[pl.ds(r, n)] = 0.35 * c + 0.1 * s
        _, s, _ = around(V[pl.ds(r - 1, n + 2)], closed)
        Q[pl.ds(r, n)] = s * SIXTH - src
    if ghost is not None:
        Q[...] = ghost[...]
        zero_edges(edge, Q, first)
    else:
        rows_loop(1, top - 1, stage_a, pieces)
        finish(Q, first)

    def stage_b(r, n):
        _, s, _ = around(Q[pl.ds(r - 1, n + 2)], closed)
        s = s * SIXTH
        V[pl.ds(r, n)] = s if ghost is not None else s - SRC[pl.ds(r, n)]
    rows_loop(2, top - 2, stage_b, pieces)
    finish(V, first)

    def stage_c(r, n):
        zp, zm = zshift(V[pl.ds(r, n)], closed)
        u = 0.5 * (zp - zm)
        U1[pl.ds(r, n)] = u if ghost is not None else u + B[pl.ds(r, n)]
    rows_loop(3, top - 3, stage_c, pieces)
    zero_edges(edge, U1, first)

    def stage_d(r, n):
        c, s, d = around(U1[pl.ds(r - 1, n + 2)], closed)
        src = (0.5 / 6.0) * d[:, m]
        SRC2[pl.ds(r, n)] = src
        B2[pl.ds(r, n)] = 0.35 * c[:, m] + 0.1 * s[:, m]
        _, s, _ = around(V[pl.ds(r - 1, n + 2)], closed)
        Q2[pl.ds(r, n)] = s[:, m] * SIXTH - src
    rows_loop(3, top - 3, stage_d, pieces)
    finish(Q2, second)

    def stage_e(r, n):
        _, s, _ = around(Q2[pl.ds(r - 1, n + 2)], closed)
        P2[pl.ds(r, n)] = s * SIXTH - SRC2[pl.ds(r, n)]
    rows_loop(4, top - 4, stage_e, pieces)
    finish(P2, second)

    def stage_f(r, n):
        zp, zm = zshift(P2[pl.ds(r, n)], closed)
        A[pl.ds(r, n)] = B2[pl.ds(r, n)] + 0.5 * (zp - zm)
    rows_loop(4, top - 4, stage_f, pieces)
    zero_edges(edge, A, second)


def adjoint(edge, window, pieces, a2, pot, u1, mid, late, give):
    BM, SP = mid[5:7]
    S2, T, B, A1, S3, SP2, S4, T2 = late
    top = SP.shape[0] - 1
    closed = window[0][0] == 0
    second, third = window[1][0], window[2][0]
    m = piece(window[1], window[2])

    def take(source, inner, r, n):
        ref, place = source
        return ref[pl.ds(r, n), piece(place, inner), :]

    def stage_g(r, n):
        c, s, d = around(take(a2, window[1], r - 1, n + 2), closed)
        BM[pl.ds(r, n)] = 0.35 * c + 0.1 * s
        sp = -0.5 * d
        if pot is not None:
            sp = sp + take(pot, window[1], r, n)
        SP[pl.ds(r, n)] = sp
    rows_loop(4, top - 4, stage_g, pieces)
    zero_edges(edge, SP, second)

    def stage_h(r, n):
        c, s, _ = around(SP[pl.ds(r - 1, n + 2)], closed)
        c, s = c[:, m], s[:, m] * SIXTH
        S2[pl.ds(r, n)] = s
        T[pl.ds(r, n)] = (c + s) * SIXTH
    rows_loop(5, top - 5, stage_h, pieces)
    zero_edges(edge, S2, third)
    zero_edges(edge, T, third)

    def stage_i(r, n):
        _, s, _ = around(S2[pl.ds(r - 1, n + 2)], closed)
        S3[pl.ds(r, n)] = s * SIXTH
        zp, zm = zshift(T[pl.ds(r, n)], closed)
        a = BM[pl.ds(r, n), m, :] + 0.5 * (zp - zm)
        if u1 is not None:
            a = a + take(u1, window[2], r, n)
        A1[pl.ds(r, n)] = a
    rows_loop(6, top - 6, stage_i, pieces)
    zero_edges(edge, A1, third)

    def stage_j(r, n):
        if give is None:
            zp, zm = zshift(A1[pl.ds(r, n)], closed)
            d = zp - zm
        else:
            c, s, d = around(A1[pl.ds(r - 1, n + 2)], closed)
            B[pl.ds(r, n)] = 0.35 * c + 0.1 * s
        SP2[pl.ds(r, n)] = S3[pl.ds(r, n)] - 0.5 * d
    rows_loop(6, top - 6, stage_j, pieces)
    zero_edges(edge, SP2, third)

    def stage_k(r, n):
        c, s, _ = around(SP2[pl.ds(r - 1, n + 2)], closed)
        s = s * SIXTH
        S4[pl.ds(r, n)] = s
        T2[pl.ds(r, n)] = (c + s) * SIXTH
    rows_loop(7, top - 7, stage_k, pieces)
    zero_edges(edge, S4, third)
    zero_edges(edge, T2, third)
    if give is None:
        return
    own = slice(third, third + COLS)

    def stage_l(r, n):
        _, s, _ = around(S4[pl.ds(r - 1, n + 2)], closed)
        zp, zm = zshift(T2[pl.ds(r, n)], closed)
        u = B[pl.ds(r, n)] + 0.5 * (zp - zm)
        give(r - HY, n, u[:, own], s[:, own] * SIXTH)
    rows_loop(8, top - 8, stage_l, 2)


def load_extended(dst, f, part, own, yd, yu, below, above):
    first, end = part * PART, part * PART + PART + 2 * HY
    top = HY + ROWS

    def rows(src_first, src_end, src, offset, layers, to_layer):
        r0, r1 = max(first, src_first), min(end, src_end)
        if r0 < r1:
            at = slice(offset + r0 - src_first, offset + r1 - src_first)
            dst[r0 - first:r1 - first, to_layer:to_layer + layers.stop - layers.start, :] = src[f, at, layers, :]

    block, tile = slice(0, COLS), slice(0, 8)
    rows(0, HY, yd, 0, block, HZ)
    rows(HY, top, own, 0, block, HZ)
    rows(top, EXT, yu, 0, block, HZ)
    for (z, rest), near, far in ((below, 4, 0), (above, HZ + COLS, HZ + COLS + 8)):
        rows(HY, top, z, 0, tile, near)
        rows(0, HY, rest, 0, tile, near)
        rows(top, EXT, rest, HY, tile, near)
        for k in range(2):
            rows(RIM + k * HALF, RIM + (k + 1) * HALF, rest, 2 * HY, slice(4 * k, 4 * k + 4), far)


def is_even(axis):
    return lax.rem(lax.axis_index(axis), 2) == 0


def strips_kernel(own, far, near):
    even = is_even("gy")
    low, high = own[:, 0:HY], own[:, ROWS - HY:]
    far[...] = jnp.where(even, low, high)
    near[...] = jnp.where(even, high, low)


def tiles_kernel(own, near, far):
    even = is_even("gz")
    low, high = own[:, :, 0:8, :], own[:, :, 8:16, :]
    near[...] = jnp.where(even, high, low)
    far[...] = jnp.where(even, low, high)


def pack_kernel(own, far, near, yd, yu, near_out, far_out, z_near, z_far, sems):
    even = is_even("gy")
    yd[...] = jnp.where(even, far[...], near[...])
    yu[...] = jnp.where(even, near[...], far[...])

    def pack(dst, whole, part):
        dst[:, 0:HY] = yd[:, :, whole:whole + 8, :]
        dst[:, HY:2 * HY] = yu[:, :, whole:whole + 8, :]
        at, edge = 2 * HY, HY - RIM
        dst[:, at:at + edge, 0:4, :] = yd[:, RIM:, part:part + 4, :]
        dst[:, at + edge:, 0:4, :] = own[:, 0:HALF - edge, part:part + 4, :]
        dst[:, at:at + HALF - edge, 4:8, :] = own[:, HALF - edge:, part:part + 4, :]
        dst[:, at + HALF - edge:, 4:8, :] = yu[:, 0:edge, part:part + 4, :]

    copies = [pltpu.make_async_copy(*pair, sems.at[i]) for i, pair in enumerate(((z_far, far_out), (z_near, near_out)))]
    upward = is_even("gz")

    def fill(dst, when, copy):
        @pl.when(when)
        def _():
            pack(dst, 8, 4)

        @pl.when(jnp.logical_not(when))
        def _():
            pack(dst, 0, 8)
        copy.start()
    fill(z_far, jnp.logical_not(upward), copies[0])
    fill(z_near, upward, copies[1])
    for copy in copies:
        copy.wait()


HIGHEST = lax.Precision.HIGHEST


def edges():
    gy, gz = lax.axis_index("gy"), lax.axis_index("gz")
    return (gy == 0, gy == lax.axis_size("gy") - 1, gz == 0, gz == lax.axis_size("gz") - 1)


def iota(shape, dim):
    return lax.broadcasted_iota(jnp.int32, shape, dim)


def tile_volts(first, second, labels):
    lab = jnp.broadcast_to(labels, first.shape) - 2 * iota(first.shape, 0)
    hit = jnp.where(lab == 0, first, 0.0) + jnp.where(lab == 1, second, 0.0)
    return jnp.sum(hit, axis=0, keepdims=True)


def fill_ghost(upper, ghost, volts):
    lane, row = iota((8, LANES), 1), iota((8, LANES), 0)
    apart = jnp.where((lane >> 4) == row, jnp.broadcast_to(volts, (8, LANES)), 0.0)
    spread = ((iota((LANES, LANES), 0) & 15) == (iota((LANES, LANES), 1) >> 3)).astype(jnp.float32)
    wall = jnp.dot(apart, spread, precision=HIGHEST, preferred_element_type=jnp.float32) * (1.0 / 6.0)
    layer = iota((COLS, LANES), 0) == jnp.where(upper, COLS - 1, 0)
    for ty in range(8):
        tile = jnp.where(layer, jnp.broadcast_to(wall[ty:ty + 1], (COLS, LANES)), 0.0)
        ghost[8 * ty:8 * ty + 8] = jnp.broadcast_to(tile[None], (8, COLS, LANES))


def wall_tiles(layer, T, T2, held):
    at = slice(HY, HY + ROWS)
    w = T[at, layer, :] + T2[at, layer, :]
    held[...] = jnp.zeros((8, LANES), jnp.float32)
    held[0:TY] = jnp.sum(w.reshape(TY, 8, LANES), axis=1)
    gather = ((iota((LANES, LANES), 0) >> 3) == (iota((LANES, LANES), 1) & 15)).astype(jnp.float32)
    sums = jnp.dot(held[...], gather, precision=HIGHEST, preferred_element_type=jnp.float32)
    keep = (iota((8, LANES), 1) >> 4) == iota((8, LANES), 0)
    return jnp.sum(jnp.where(keep, sums, 0.0), axis=0, keepdims=True)


def split(refs):
    return refs[:6], refs[6:13], refs[13:21]


def wall_kernel(own, yd, yu, volts, row, *refs):
    early, mid, late = split(refs)
    held, sums = refs[21:]
    ylo, yhi, zlo, zhi = edges()
    edge = (ylo, yhi, None, None)
    is_forward = lax.axis_index("grp") == 0
    sums[...] = jnp.zeros((1, LANES), jnp.float32)

    @pl.when(jnp.logical_or(zlo, zhi))
    def _():
        for f in range(2):
            early[f][0:HY] = yd[f]
            early[f][HY:HY + ROWS] = own[f]
            early[f][HY + ROWS:] = yu[f]

    def side(window, layer):
        @pl.when(is_forward)
        def _():
            forward(edge, None, window, 1, early, mid)
            adjoint(edge, window, 1, (mid[4], window[1]), None, (early[5], window[0]), mid, late, None)

        @pl.when(jnp.logical_not(is_forward))
        def _():
            adjoint(edge, window, 1, (early[0], window[0]), (early[1], window[0]), None, mid, late, None)

        sums[...] = wall_tiles(layer, late[1], late[7], held)

    @pl.when(zlo)
    def _():
        side(LOWER, 0)

    @pl.when(zhi)
    def _():
        side(UPPER, 7)

    row[...] = jnp.broadcast_to(sums[...] + volts[...], row.shape)


def bulk_kernel(part, own, yd, yu, z_far, z_near, far, near, main_out, send_out, *refs):
    far, near = (z_far, far), (z_near, near)
    early, mid, late = split(refs)
    main, send, sems = refs[21:]
    ylo, yhi, zlo, zhi = edges()
    edge = (ylo if part == 0 else None, yhi if part == PARTS - 1 else None, zlo, zhi)
    is_forward = lax.axis_index("grp") == 0

    @pl.when(is_even("gz"))
    def _():
        for f in range(2):
            load_extended(early[f], f, part, own, yd, yu, far, near)

    @pl.when(jnp.logical_not(is_even("gz")))
    def _():
        for f in range(2):
            load_extended(early[f], f, part, own, yd, yu, near, far)

    def leave(ref, out, rows, copies):
        copy = pltpu.make_async_copy(ref.at[:, rows], out.at[:, rows], sems.at[len(copies)])
        copy.start()
        copies.append(copy)

    def into(ref, out, copies):
        def give(r, n, u, p):
            ref[0, pl.ds(r, n)] = u
            ref[1, pl.ds(r, n)] = p
            leave(ref, out, pl.ds(r, n), copies)
        return give

    @pl.when(is_forward)
    def _():
        copies = []
        forward(edge, None, BULK, 1, early, mid)
        at = (slice(HY, HY + PART), slice(BULK[1][0], BULK[1][0] + COLS))
        main[0] = mid[4][at]
        main[1] = mid[3][at]
        leave(main, main_out, pl.ds(0, PART), copies)
        adjoint(edge, BULK, 1, (mid[4], BULK[1]), None, (early[5], BULK[0]), mid, late, into(send, send_out, copies))
        for copy in copies:
            copy.wait()

    @pl.when(jnp.logical_not(is_forward))
    def _():
        copies = []
        adjoint(edge, BULK, 1, (early[0], BULK[0]), (early[1], BULK[0]), None, mid, late, into(main, main_out, copies))
        for copy in copies:
            copy.wait()


def volts_kernel(*refs):
    parts, refs = refs[:PARTS], refs[PARTS:]
    rows, near, labels, far_response, out, grad = refs[:6]
    early, mid, late = split(refs[6:])
    ghost, response, sems = refs[27:]
    copies = [pltpu.make_async_copy(part, out.at[:, i * PART:(i + 1) * PART], sems.at[i]) for i, part in enumerate(parts)]
    fetch = pltpu.make_async_copy(far_response, response, sems.at[PARTS])
    for copy in copies:
        copy.start()
    fetch.start()
    ylo, yhi, zlo, zhi = edges()
    edge = (ylo, yhi, None, None)
    at_wall = jnp.logical_or(zlo, zhi)
    is_forward = lax.axis_index("grp") == 0
    n = rows.shape[0]
    first = jnp.broadcast_to(rows[:, VOLT:VOLT + 1], (n, LANES))
    second = jnp.broadcast_to(rows[:, VOLT + 1:VOLT + 2], (n, LANES))

    @pl.when(at_wall)
    def _():
        fill_ghost(zhi, ghost, tile_volts(first, second, near[...]))
        forward(edge, ghost, NEAR, 1, early, mid)

    for copy in copies:
        copy.wait()

    @pl.when(jnp.logical_and(at_wall, is_forward))
    def _():
        out[0] += mid[4][HY:HY + ROWS]
        out[1] += mid[3][HY:HY + ROWS]

    @pl.when(jnp.logical_and(at_wall, jnp.logical_not(is_forward)))
    def _():
        def give(r, n, u, p):
            out[0, pl.ds(r, n)] += u
            out[1, pl.ds(r, n)] += p
        adjoint(edge, NEAR, 1, (mid[4], NEAR[1]), None, (early[5], NEAR[0]), mid, late, give)

    fetch.wait()
    gy, gz = lax.axis_size("gy"), lax.axis_size("gz")
    me = (lax.axis_index("grp") * gy + lax.axis_index("gy")) * gz + lax.axis_index("gz")
    pair = [jnp.zeros((gy, LANES), jnp.float32)] * 2
    block = iota((gy, LANES), 0)
    for s in range(2):
        v = jnp.concatenate([tile_volts(first, second, labels[s, g:g + 1]) for g in range(gy)], axis=0)
        r = jnp.dot(v, response[...], precision=HIGHEST, preferred_element_type=jnp.float32)
        r = [r[:, k * LANES:(k + 1) * LANES] for k in range(5)]
        w = jnp.where(block == 0, r[3], jnp.where(block == gy - 1, r[4], r[0]))
        w = w + jnp.where(block == 0, 0.0, pltpu.roll(r[1], 1, 0))
        w = w + jnp.where(block == gy - 1, 0.0, pltpu.roll(r[2], gy - 1, 0))
        for g in range(2):
            w = w + rows[pl.ds(g * gy * gz + s * (gz - 1), gy, stride=gz), :]
        for j in range(2):
            pair[j] = pair[j] + jnp.where(labels[s] == 2 * me + j, w, 0.0)
    total = [jnp.sum(p) for p in pair]
    grad[...] = jnp.where(iota((1, 2), 1) == 0, total[0], total[1])


def sum_kernel(main, *refs):
    out = refs[PARTS]
    for i in range(PARTS):
        at = slice(i * PART, (i + 1) * PART)
        out[0, :, at] = main[:, at] + refs[i][...]


def wall_response():
    def near_sum(f):
        g = np.pad(f, ((0, 0), (1, 1), (1, 1), (0, 0)))
        t = g[:, 2:, 1:-1] + g[:, :-2, 1:-1] + g[:, 1:-1, 2:] + g[:, 1:-1, :-2]
        return t + np.roll(f, 1, 3) + np.roll(f, -1, 3)

    def diff(f):
        g = np.pad(f, ((0, 0), (0, 0), (1, 1), (0, 0)))
        return g[:, :, 2:] - g[:, :, :-2]

    def sums(blocks, at):
        ghost = np.zeros((TY, blocks * ROWS, 13, LANES))
        for t in range(TY):
            ghost[t, at * ROWS + 8 * t:at * ROWS + 8 * t + 8, 0, 0:8] = 1.0
        u, p, states = np.zeros_like(ghost), np.zeros_like(ghost), []
        for _ in range(2):
            source = 0.5 * diff(u)
            for _ in range(2):
                p = (near_sum(p) + ghost - source) / 6.0
            u = 0.35 * u + 0.1 * near_sum(u) + 0.5 * diff(p)
            states.append(u)
        a, q, wall = np.zeros_like(ghost), np.zeros_like(ghost), 0.0
        for u in reversed(states):
            a = a + u
            spread, total = q - 0.5 * diff(a), 0.0
            for _ in range(2):
                total = total + spread / 6.0
                spread = near_sum(spread) / 6.0
            a = 0.35 * a + 0.1 * near_sum(a) + 0.5 * diff(total)
            q = spread
            wall = wall + total[:, :, 0]
        return wall.reshape(TY, blocks, TY, 8, 16, 8).sum((3, 5))

    def matrix(got):
        m = np.zeros((LANES, LANES), np.float32)
        for t in range(TY):
            for x in range(16):
                m[t * 16 + x, 0:TY * 16] = np.roll(got[t], x, 1).reshape(-1)
        return m

    middle, low, high = sums(3, 1), sums(2, 0), sums(2, 1)
    return np.concatenate([matrix(middle[:, 1]), matrix(middle[:, 2]), matrix(middle[:, 0]),
                           matrix(low[:, 0]), matrix(high[:, 1])], axis=1)


def vmem(n):
    return [pl.BlockSpec(memory_space=pltpu.VMEM)] * n


def shape(*dims):
    return jax.ShapeDtypeStruct(dims, jnp.float32)


def kept(*dims):
    return pltpu.VMEM(dims, jnp.float32)


def in_hbm(array):
    return pltpu.with_memory_space_constraint(array, pltpu.HBM)


def swapped(array, axis, first):
    pairs = []
    for i in range(first, lax.axis_size(axis) - 1, 2):
        pairs += [(i, i + 1), (i + 1, i)]
    return lax.ppermute(array, axis, pairs)


def per_device(response, field_pairs, tile_owner, electrode_volts):
    own = field_pairs[0]
    labels = tile_owner[..., 0]
    gy, gz = lax.axis_index("gy"), lax.axis_index("gz")
    devices = lax.axis_size(AXES)
    half = pltpu.HBM((2, PART, COLS, LANES), jnp.float32)
    strip, tiles = kept(2, HY, COLS, LANES), kept(2, ROWS, 8, LANES)
    slab = pltpu.HBM((2, 2 * HY + HALF, 8, LANES), jnp.float32)

    def limit(mib):
        return pltpu.CompilerParams(vmem_limit_bytes=mib * 1024 * 1024)

    far, near = pl.pallas_call(
        strips_kernel, out_shape=(strip, strip), in_specs=vmem(1), out_specs=vmem(2), compiler_params=limit(4),
    )(own)
    far = swapped(far, "gy", 1)
    near = swapped(near, "gy", 0)
    mine, near = lax.optimization_barrier((own, near))
    z_near, z_far = pl.pallas_call(
        tiles_kernel, out_shape=(tiles, tiles), in_specs=vmem(1), out_specs=vmem(2), compiler_params=limit(8),
    )(mine)
    z_far = swapped(z_far, "gz", 1)
    z_near = swapped(z_near, "gz", 0)
    yd, yu, near, far = pl.pallas_call(
        pack_kernel, out_shape=(strip, strip, slab, slab), in_specs=vmem(3),
        out_specs=vmem(2) + [pl.BlockSpec(memory_space=pl.ANY)] * 2,
        scratch_shapes=[pltpu.VMEM((2, 2 * HY + HALF, 8, LANES), jnp.float32)] * 2 + [pltpu.SemaphoreType.DMA((2,))],
        compiler_params=limit(8),
    )(own, far, near)
    volts = jnp.pad(electrode_volts, (VOLT, LANES - VOLT - 2))[None]
    row = pl.pallas_call(
        wall_kernel, out_shape=kept(devices, LANES), in_specs=vmem(4), out_specs=vmem(1)[0],
        scratch_shapes=scratch(EXT, LOWER) + [pltpu.VMEM((8, LANES), jnp.float32), pltpu.VMEM((1, LANES), jnp.float32)],
        compiler_params=limit(12),
    )(own, yd, yu, volts)
    far, near, row = lax.optimization_barrier((far, near, row))
    far = swapped(far, "gz", 1)
    near = swapped(near, "gz", 0)
    rows = lax.all_to_all(row, AXES, 0, 0, tiled=True)

    mine, _ = lax.optimization_barrier((own, row))
    def bulk(part, block, load):
        return pl.pallas_call(
            functools.partial(bulk_kernel, part), out_shape=(half, half), in_specs=vmem(7),
            out_specs=[pl.BlockSpec(memory_space=pl.ANY)] * 2,
            scratch_shapes=scratch(PART + 2 * HY, BULK) + [pltpu.VMEM((2, PART, COLS, LANES), jnp.float32)] * 2
            + [pltpu.SemaphoreType.DMA((3,))], compiler_params=limit(20),
            cost_estimate=pl.CostEstimate(flops=10 ** 8, bytes_accessed=load * 10 ** 6, transcendentals=0),
        )(block, yd, yu, z_far, z_near, far, near)

    mains, extras = [], []
    for part in range(PARTS):
        main, send = bulk(part, mine, 36 if part == 0 else 9)
        mains.append(main)
        mine, _ = lax.optimization_barrier((own, send))
        if part == PARTS - 1:
            send, rows = lax.optimization_barrier((send, rows))
        extras.append(lax.ppermute(send, "grp", [(0, 1)]))

    fenced = jnp.pad(labels, ((0, 0), (1, 1), (0, 0)), constant_values=-1)
    side = (gz == lax.axis_size("gz") - 1).astype(jnp.int32)
    by_wall = lax.dynamic_slice(fenced, (side, gy * TY, 0), (1, 8, 16)).reshape(1, LANES)
    by_block = jnp.pad(labels.reshape(2, 8, TY * 16), ((0, 0), (0, 0), (0, LANES - TY * 16)), constant_values=-1)
    total, grad = pl.pallas_call(
        volts_kernel, out_shape=(kept(2, ROWS, COLS, LANES), shape(1, 2)),
        in_specs=[pl.BlockSpec(memory_space=pl.ANY)] * PARTS + vmem(3) + [pl.BlockSpec(memory_space=pl.ANY)], out_specs=vmem(2),
        scratch_shapes=scratch(EXT, NEAR) + [pltpu.VMEM((EXT, COLS, LANES), jnp.float32), pltpu.VMEM(response.shape, jnp.float32),
                                             pltpu.SemaphoreType.DMA((PARTS + 1,))],
        compiler_params=limit(16),
    )(*[in_hbm(main) for main in mains], rows, by_wall, by_block, in_hbm(response))
    advanced = pl.pallas_call(
        sum_kernel, out_shape=shape(1, 2, ROWS, COLS, LANES), in_specs=vmem(PARTS + 1), out_specs=vmem(1)[0],
        compiler_params=limit(8),
    )(total, *extras)
    return (advanced, grad.reshape(2))


def solution(mesh):
    response = jnp.asarray(wall_response())
    placed = (P("grp", None, "gy", "gz", None), P(), P(AXES))
    return jax.shard_map(
        functools.partial(per_device, response), mesh=mesh, in_specs=placed,
        out_specs=(P("grp", None, "gy", "gz", None), P(AXES)), check_vma=False,
    )
```

```python
import functools

import jax
import jax.numpy as jnp
import numpy as np
from jax import lax
from jax.experimental import pallas as pl
from jax.experimental.pallas import tpu as pltpu
from jax.sharding import PartitionSpec as P

AXES = ("grp", "gy", "gz")
TY = 6
VOLT = (TY + 1) * 16
ROWS, COLS, LANES = 48, 16, 128
HY, HZ = 8, 12
EXT = ROWS + 2 * HY
RIM = 4
HALF = EXT // 2 - RIM
PARTS = 3
PART = ROWS // PARTS
SIXTH = 1.0 / 6.0
SHARE, PIECES = 0.34, 3

BULK = ((12, 40), (8, 32), (4, 24))
NEAR = ((0, COLS),) * 3
LOWER = ((0, COLS), (0, 8), (0, 8))
UPPER = ((0, COLS), (-8, 8), (-8, 8))


def piece(outer, inner):
    start = outer[0] - inner[0]
    return slice(start, start + inner[1])


def rows_loop(first, last, body, pieces):
    n = (last - first + 1) // pieces
    for i in range(pieces):
        body(first + i * n, n)


def zshift(v, ends):
    z = v.shape[1]
    zp, zm = pltpu.roll(v, z - 1, 1), pltpu.roll(v, 1, 1)
    if ends is None:
        layer = lax.broadcasted_iota(jnp.int32, v.shape, 1)
        return jnp.where(layer == z - 1, 0.0, zp), jnp.where(layer == 0, 0.0, zm)

    def cut(shifted, at, when):
        g = at // 8 * 8
        hit = (lax.broadcasted_iota(jnp.int32, (1, 8, LANES), 1) == at - g) & when
        tile = jnp.where(jnp.broadcast_to(hit, (v.shape[0], 8, LANES)), 0.0, shifted[:, g:g + 8])
        return jnp.concatenate([part for part in (shifted[:, :g], tile, shifted[:, g + 8:]) if part.shape[1]], axis=1)
    at, below, above = ends
    return cut(zp, at + COLS - 1, above), cut(zm, at, below)


def beside(c, share):
    n, z, _ = c.shape
    k = int(n * share)
    if k == 0:
        return pltpu.roll(c, 1, 2) + pltpu.roll(c, LANES - 1, 2)
    row = lax.broadcasted_iota(jnp.int32, (LANES, LANES), 0)
    lane = lax.broadcasted_iota(jnp.int32, (LANES, LANES), 1)
    apart = (row - lane) & (LANES - 1)
    ring = jnp.where((apart == 1) | (apart == LANES - 1), 1.0, 0.0).astype(jnp.bfloat16)
    rest, total = c[:k].reshape(k * z, LANES), None
    for i in range(PIECES):
        part = rest.astype(jnp.bfloat16)
        got = jnp.dot(part, ring, preferred_element_type=jnp.float32)
        total = got if total is None else total + got
        if i < PIECES - 1:
            rest = rest - part.astype(jnp.float32)
    rolled = pltpu.roll(c[k:], 1, 2) + pltpu.roll(c[k:], LANES - 1, 2)
    return jnp.concatenate([total.reshape(k, z, LANES), rolled], axis=0)


def around(w, ends):
    c = w[1:-1]
    zp, zm = zshift(c, ends)
    s = (w[:-2] + w[2:]) + (zp + zm)
    return c, s + beside(c, 0.0 if ends is None else SHARE), zp - zm


def zero_edges(edge, ref):
    for when, r in ((edge[0], HY - 1), (edge[1], ref.shape[0] - HY)):
        if when is not None:
            ref[r] = jnp.where(when, 0.0, ref[r])


def early_scratch(rows, window):
    return [pltpu.VMEM((rows, window[0][1], LANES), jnp.float32)] * 6


def mid_scratch(rows, window):
    return [pltpu.VMEM((rows, window[1][1], LANES), jnp.float32)] * 7


def late_scratch(rows, window):
    return [pltpu.VMEM((rows, window[2][1], LANES), jnp.float32)] * 8


def scratch(rows, window):
    return early_scratch(rows, window) + mid_scratch(rows, window) + late_scratch(rows, window)


def forward(edge, ghost, window, pieces, early, mid, spread=False):
    U, V, SRC, B, Q, U1 = early
    SRC2, B2, Q2, P2, A = mid[:5]
    top = U1.shape[0] - 1
    closed = window[0][0] == 0
    ends = [None if closed else (part[0],) + edge[2:] for part in window]

    def span(k):
        return (1, top - 1) if spread else (k, top - k)

    m = piece(window[0], window[1])

    def finish(ref):
        if ghost is not None:
            ref[...] += ghost[...]
        zero_edges(edge, ref)

    def stage_a(r, n):
        c, s, d = around(U[pl.ds(r - 1, n + 2)], ends[0])
        src = (0.5 / 6.0) * d
        SRC[pl.ds(r, n)] = src
        B[pl.ds(r, n)] = 0.35 * c + 0.1 * s
        _, s, _ = around(V[pl.ds(r - 1, n + 2)], ends[0])
        Q[pl.ds(r, n)] = s * SIXTH - src
    if ghost is not None:
        Q[...] = ghost[...]
        zero_edges(edge, Q)
    else:
        rows_loop(*span(1), stage_a, pieces)
        finish(Q)

    def stage_b(r, n):
        _, s, _ = around(Q[pl.ds(r - 1, n + 2)], ends[0])
        s = s * SIXTH
        V[pl.ds(r, n)] = s if ghost is not None else s - SRC[pl.ds(r, n)]
    rows_loop(*span(2), stage_b, pieces)
    finish(V)

    def stage_c(r, n):
        zp, zm = zshift(V[pl.ds(r, n)], ends[0])
        u = 0.5 * (zp - zm)
        U1[pl.ds(r, n)] = u if ghost is not None else u + B[pl.ds(r, n)]
    rows_loop(*span(3), stage_c, pieces)
    zero_edges(edge, U1)

    def stage_d(r, n):
        c, s, d = around(U1[pl.ds(r - 1, n + 2)], ends[0])
        src = (0.5 / 6.0) * d[:, m]
        SRC2[pl.ds(r, n)] = src
        B2[pl.ds(r, n)] = 0.35 * c[:, m] + 0.1 * s[:, m]
        _, s, _ = around(V[pl.ds(r - 1, n + 2)], ends[0])
        Q2[pl.ds(r, n)] = s[:, m] * SIXTH - src
    rows_loop(*span(3), stage_d, pieces)
    finish(Q2)

    def stage_e(r, n):
        _, s, _ = around(Q2[pl.ds(r - 1, n + 2)], ends[1])
        P2[pl.ds(r, n)] = s * SIXTH - SRC2[pl.ds(r, n)]
    rows_loop(*span(4), stage_e, pieces)
    if ghost is not None:
        P2[...] += ghost[...]

    def stage_f(r, n):
        zp, zm = zshift(P2[pl.ds(r, n)], ends[1])
        A[pl.ds(r, n)] = B2[pl.ds(r, n)] + 0.5 * (zp - zm)
    rows_loop(*span(4), stage_f, pieces)
    zero_edges(edge, A)


def adjoint(edge, window, pieces, a2, pot, u1, mid, late, give, spread=False):
    BM, SP = mid[5:7]
    S2, T, B, A1, S3, SP2, S4, T2 = late
    top = SP.shape[0] - 1
    closed = window[0][0] == 0
    ends = [None if closed else (part[0],) + edge[2:] for part in window]

    def span(k):
        return (1, top - 1) if spread else (k, top - k)

    third = window[2][0]
    m = piece(window[1], window[2])

    def take(source, inner, r, n):
        ref, place = source
        return ref[pl.ds(r, n), piece(place, inner), :]

    def stage_g(r, n):
        c, s, d = around(take(a2, window[1], r - 1, n + 2), ends[1])
        BM[pl.ds(r, n)] = 0.35 * c + 0.1 * s
        sp = -0.5 * d
        if pot is not None:
            sp = sp + take(pot, window[1], r, n)
        SP[pl.ds(r, n)] = sp
    rows_loop(*span(4), stage_g, pieces)
    zero_edges(edge, SP)

    def stage_h(r, n):
        c, s, _ = around(SP[pl.ds(r - 1, n + 2)], ends[1])
        c, s = c[:, m], s[:, m] * SIXTH
        S2[pl.ds(r, n)] = s
        T[pl.ds(r, n)] = (c + s) * SIXTH
    rows_loop(*span(5), stage_h, pieces)
    zero_edges(edge, S2)

    def stage_i(r, n):
        _, s, _ = around(S2[pl.ds(r - 1, n + 2)], ends[2])
        S3[pl.ds(r, n)] = s * SIXTH
        zp, zm = zshift(T[pl.ds(r, n)], ends[2])
        a = BM[pl.ds(r, n), m, :] + 0.5 * (zp - zm)
        if u1 is not None:
            a = a + take(u1, window[2], r, n)
        A1[pl.ds(r, n)] = a
    rows_loop(*span(6), stage_i, pieces)
    zero_edges(edge, A1)

    def stage_j(r, n):
        if give is None:
            zp, zm = zshift(A1[pl.ds(r, n)], ends[2])
            d = zp - zm
        else:
            c, s, d = around(A1[pl.ds(r - 1, n + 2)], ends[2])
            B[pl.ds(r, n)] = 0.35 * c + 0.1 * s
        SP2[pl.ds(r, n)] = S3[pl.ds(r, n)] - 0.5 * d
    rows_loop(*span(6), stage_j, pieces)
    zero_edges(edge, SP2)

    def stage_k(r, n):
        c, s, _ = around(SP2[pl.ds(r - 1, n + 2)], ends[2])
        s = s * SIXTH
        S4[pl.ds(r, n)] = s
        T2[pl.ds(r, n)] = (c + s) * SIXTH
    rows_loop(*span(7), stage_k, pieces)
    zero_edges(edge, S4)
    if give is None:
        return
    own = slice(third, third + COLS)

    def stage_l(r, n):
        _, s, _ = around(S4[pl.ds(r - 1, n + 2)], ends[2])
        zp, zm = zshift(T2[pl.ds(r, n)], ends[2])
        u = B[pl.ds(r, n)] + 0.5 * (zp - zm)
        give(r - HY, n, u[:, own], s[:, own] * SIXTH)
    rows_loop(*span(8), stage_l, 2)


def load_extended(dst, f, part, own, yd, yu, below, above):
    first, end = part * PART, part * PART + PART + 2 * HY
    top = HY + ROWS

    def rows(src_first, src_end, src, offset, layers, to_layer):
        r0, r1 = max(first, src_first), min(end, src_end)
        if r0 < r1:
            at = slice(offset + r0 - src_first, offset + r1 - src_first)
            dst[r0 - first:r1 - first, to_layer:to_layer + layers.stop - layers.start, :] = src[f, at, layers, :]

    block, tile = slice(0, COLS), slice(0, 8)
    rows(0, HY, yd, 0, block, HZ)
    rows(HY, top, own, 0, block, HZ)
    rows(top, EXT, yu, 0, block, HZ)
    for (z, rest), near, far in ((below, 4, 0), (above, HZ + COLS, HZ + COLS + 8)):
        rows(HY, top, z, 0, tile, near)
        rows(0, HY, rest, 0, tile, near)
        rows(top, EXT, rest, HY, tile, near)
        for k in range(2):
            rows(RIM + k * HALF, RIM + (k + 1) * HALF, rest, 2 * HY, slice(4 * k, 4 * k + 4), far)


def is_even(axis):
    return lax.rem(lax.axis_index(axis), 2) == 0


def strips_kernel(own, far, near):
    even = is_even("gy")
    low, high = own[:, 0:HY], own[:, ROWS - HY:]
    far[...] = jnp.where(even, low, high)
    near[...] = jnp.where(even, high, low)


def tiles_kernel(own, near, far):
    even = is_even("gz")
    low, high = own[:, :, 0:8, :], own[:, :, 8:16, :]
    near[...] = jnp.where(even, high, low)
    far[...] = jnp.where(even, low, high)


def pack_kernel(own, far, near, yd, yu, near_out, far_out, z_near, z_far, sems):
    even = is_even("gy")
    yd[...] = jnp.where(even, far[...], near[...])
    yu[...] = jnp.where(even, near[...], far[...])

    def pack(dst, whole, part):
        dst[:, 0:HY] = yd[:, :, whole:whole + 8, :]
        dst[:, HY:2 * HY] = yu[:, :, whole:whole + 8, :]
        at, edge = 2 * HY, HY - RIM
        dst[:, at:at + edge, 0:4, :] = yd[:, RIM:, part:part + 4, :]
        dst[:, at + edge:, 0:4, :] = own[:, 0:HALF - edge, part:part + 4, :]
        dst[:, at:at + HALF - edge, 4:8, :] = own[:, HALF - edge:, part:part + 4, :]
        dst[:, at + HALF - edge:, 4:8, :] = yu[:, 0:edge, part:part + 4, :]

    copies = [pltpu.make_async_copy(*pair, sems.at[i]) for i, pair in enumerate(((z_far, far_out), (z_near, near_out)))]
    upward = is_even("gz")

    def fill(dst, when, copy):
        @pl.when(when)
        def _():
            pack(dst, 8, 4)

        @pl.when(jnp.logical_not(when))
        def _():
            pack(dst, 0, 8)
        copy.start()
    fill(z_far, jnp.logical_not(upward), copies[0])
    fill(z_near, upward, copies[1])
    for copy in copies:
        copy.wait()


HIGHEST = lax.Precision.HIGHEST


def edges():
    gy, gz = lax.axis_index("gy"), lax.axis_index("gz")
    return (gy == 0, gy == lax.axis_size("gy") - 1, gz == 0, gz == lax.axis_size("gz") - 1)


def iota(shape, dim):
    return lax.broadcasted_iota(jnp.int32, shape, dim)


def tile_volts(first, second, labels):
    lab = jnp.broadcast_to(labels, first.shape) - 2 * iota(first.shape, 0)
    hit = jnp.where(lab == 0, first, 0.0) + jnp.where(lab == 1, second, 0.0)
    return jnp.sum(hit, axis=0, keepdims=True)


def fill_ghost(upper, ghost, volts):
    lane, row = iota((8, LANES), 1), iota((8, LANES), 0)
    apart = jnp.where((lane >> 4) == row, jnp.broadcast_to(volts, (8, LANES)), 0.0)
    spread = ((iota((LANES, LANES), 0) & 15) == (iota((LANES, LANES), 1) >> 3)).astype(jnp.float32)
    wall = jnp.dot(apart, spread, precision=HIGHEST, preferred_element_type=jnp.float32) * (1.0 / 6.0)
    layer = iota((COLS, LANES), 0) == jnp.where(upper, COLS - 1, 0)
    for ty in range(8):
        tile = jnp.where(layer, jnp.broadcast_to(wall[ty:ty + 1], (COLS, LANES)), 0.0)
        ghost[8 * ty:8 * ty + 8] = jnp.broadcast_to(tile[None], (8, COLS, LANES))


def wall_tiles(layer, T, T2):
    w = jnp.sum((T[:, layer, :] + T2[:, layer, :]).reshape(8, 8, LANES), axis=1)
    gather = ((iota((LANES, LANES), 0) >> 3) == (iota((LANES, LANES), 1) & 15)).astype(jnp.float32)
    sums = jnp.dot(w, gather, precision=HIGHEST, preferred_element_type=jnp.float32)
    first = lax.rem(lax.axis_index("gy"), 2)
    lane = iota((8, LANES), 1)
    keep = ((lane >> 4) + first == iota((8, LANES), 0)) & (lane < VOLT)
    return jnp.sum(jnp.where(keep, sums, 0.0), axis=0, keepdims=True)


def split(refs):
    return refs[:6], refs[6:13], refs[13:21]


def wall_kernel(own, near, volts, row, *refs):
    early, mid, late = split(refs)
    sums = refs[21]
    ylo, yhi, zlo, zhi = edges()
    edge = (ylo, yhi, None, None)
    is_forward = lax.axis_index("grp") == 0
    sums[...] = jnp.zeros((1, LANES), jnp.float32)

    @pl.when(jnp.logical_or(zlo, zhi))
    def _():
        for ref in early + mid + late:
            for r in (0, EXT - 1):
                ref[r] = jnp.zeros(ref.shape[1:], jnp.float32)
        for f in range(2):
            early[f][0:HY] = jnp.where(is_even("gy"), 0.0, near[f])
            early[f][HY:HY + ROWS] = own[f]
            early[f][HY + ROWS:] = jnp.where(is_even("gy"), near[f], 0.0)

    def side(window, layer):
        @pl.when(is_forward)
        def _():
            forward(edge, None, window, 1, early, mid, True)
            adjoint(edge, window, 1, (mid[4], window[1]), None, (early[5], window[0]), mid, late, None, True)

        @pl.when(jnp.logical_not(is_forward))
        def _():
            adjoint(edge, window, 1, (early[0], window[0]), (early[1], window[0]), None, mid, late, None, True)

        sums[...] = wall_tiles(layer, late[1], late[7])

    @pl.when(zlo)
    def _():
        side(LOWER, 0)

    @pl.when(zhi)
    def _():
        side(UPPER, 7)

    row[...] = jnp.broadcast_to(sums[...] + volts[...], row.shape)


def bulk_kernel(part, own, yd, yu, z_far, z_near, far, near, main_out, send_out, *refs):
    far, near = (z_far, far), (z_near, near)
    early, mid, late = split(refs)
    main, send, sems = refs[21:]
    ylo, yhi, zlo, zhi = edges()
    edge = (ylo if part == 0 else None, yhi if part == PARTS - 1 else None, zlo, zhi)
    is_forward = lax.axis_index("grp") == 0

    @pl.when(is_even("gz"))
    def _():
        for f in range(2):
            load_extended(early[f], f, part, own, yd, yu, far, near)

    @pl.when(jnp.logical_not(is_even("gz")))
    def _():
        for f in range(2):
            load_extended(early[f], f, part, own, yd, yu, near, far)

    def leave(ref, out, rows, copies):
        copy = pltpu.make_async_copy(ref.at[:, rows], out.at[:, rows], sems.at[len(copies)])
        copy.start()
        copies.append(copy)

    def into(ref, out, copies):
        def give(r, n, u, p):
            ref[0, pl.ds(r, n)] = u
            ref[1, pl.ds(r, n)] = p
            leave(ref, out, pl.ds(r, n), copies)
        return give

    @pl.when(is_forward)
    def _():
        copies = []
        forward(edge, None, BULK, 1, early, mid)
        at = (slice(HY, HY + PART), slice(BULK[1][0], BULK[1][0] + COLS))
        main[0] = mid[4][at]
        main[1] = mid[3][at]
        leave(main, main_out, pl.ds(0, PART), copies)
        adjoint(edge, BULK, 1, (mid[4], BULK[1]), None, (early[5], BULK[0]), mid, late, into(send, send_out, copies))
        for copy in copies:
            copy.wait()

    @pl.when(jnp.logical_not(is_forward))
    def _():
        copies = []
        adjoint(edge, BULK, 1, (early[0], BULK[0]), (early[1], BULK[0]), None, mid, late, into(main, main_out, copies))
        for copy in copies:
            copy.wait()


def volts_kernel(*refs):
    parts, refs = refs[:PARTS], refs[PARTS:]
    rows, near, labels, far_response, out, grad = refs[:6]
    early, mid, late = split(refs[6:])
    ghost, response, sems = refs[27:]
    copies = [pltpu.make_async_copy(part, out.at[:, i * PART:(i + 1) * PART], sems.at[i]) for i, part in enumerate(parts)]
    fetch = pltpu.make_async_copy(far_response, response, sems.at[PARTS])
    for copy in copies:
        copy.start()
    fetch.start()
    ylo, yhi, zlo, zhi = edges()
    edge = (ylo, yhi, None, None)
    at_wall = jnp.logical_or(zlo, zhi)
    is_forward = lax.axis_index("grp") == 0
    n = rows.shape[0]
    first = jnp.broadcast_to(rows[:, VOLT:VOLT + 1], (n, LANES))
    second = jnp.broadcast_to(rows[:, VOLT + 1:VOLT + 2], (n, LANES))

    @pl.when(at_wall)
    def _():
        fill_ghost(zhi, ghost, tile_volts(first, second, near[...]))
        forward(edge, ghost, NEAR, 1, early, mid)

    for copy in copies:
        copy.wait()

    @pl.when(jnp.logical_and(at_wall, is_forward))
    def _():
        out[0] += mid[4][HY:HY + ROWS]
        out[1] += mid[3][HY:HY + ROWS]

    @pl.when(jnp.logical_and(at_wall, jnp.logical_not(is_forward)))
    def _():
        def give(r, n, u, p):
            out[0, pl.ds(r, n)] += u
            out[1, pl.ds(r, n)] += p
        adjoint(edge, NEAR, 1, (mid[4], NEAR[1]), None, (early[5], NEAR[0]), mid, late, give)

    fetch.wait()
    gy, gz = lax.axis_size("gy"), lax.axis_size("gz")
    me = (lax.axis_index("grp") * gy + lax.axis_index("gy")) * gz + lax.axis_index("gz")
    pair = [jnp.zeros((gy, LANES), jnp.float32)] * 2
    block, lane = iota((gy, LANES), 0), iota((gy, LANES), 1)
    for s in range(2):
        v = jnp.concatenate([tile_volts(first, second, labels[s, g:g + 1]) for g in range(gy)], axis=0)
        r = jnp.dot(v, response[...], precision=HIGHEST, preferred_element_type=jnp.float32)
        r = [r[:, k * LANES:(k + 1) * LANES] for k in range(5)]
        w = jnp.where(block == 0, r[3], jnp.where(block == gy - 1, r[4], r[0]))
        w = w + jnp.where(block == 0, 0.0, pltpu.roll(r[1], 1, 0))
        w = w + jnp.where(block == gy - 1, 0.0, pltpu.roll(r[2], gy - 1, 0))
        got = sum(rows[pl.ds(g * gy * gz + s * (gz - 1), gy, stride=gz), :] for g in range(2))
        odd = (block & 1) == 1
        w = w + jnp.where(odd, got, pltpu.roll(got, LANES - 16, 1))
        below = pltpu.roll(pltpu.roll(got, 32, 1), 1, 0)
        above = pltpu.roll(pltpu.roll(got, 80, 1), gy - 1, 0)
        w = w + jnp.where((block > 0) & jnp.logical_not(odd) & (lane < 16), below, 0.0)
        w = w + jnp.where((block < gy - 1) & odd & (lane >= 80), above, 0.0)
        for j in range(2):
            pair[j] = pair[j] + jnp.where(labels[s] == 2 * me + j, w, 0.0)
    total = [jnp.sum(p) for p in pair]
    grad[...] = jnp.where(iota((1, 2), 1) == 0, total[0], total[1])


def sum_kernel(main, *refs):
    out = refs[PARTS]
    for i in range(PARTS):
        at = slice(i * PART, (i + 1) * PART)
        out[0, :, at] = main[:, at] + refs[i][...]


def wall_response():
    def near_sum(f):
        g = np.pad(f, ((0, 0), (1, 1), (1, 1), (0, 0)))
        t = g[:, 2:, 1:-1] + g[:, :-2, 1:-1] + g[:, 1:-1, 2:] + g[:, 1:-1, :-2]
        return t + np.roll(f, 1, 3) + np.roll(f, -1, 3)

    def diff(f):
        g = np.pad(f, ((0, 0), (0, 0), (1, 1), (0, 0)))
        return g[:, :, 2:] - g[:, :, :-2]

    def sums(blocks, at):
        ghost = np.zeros((TY, blocks * ROWS, 13, LANES))
        for t in range(TY):
            ghost[t, at * ROWS + 8 * t:at * ROWS + 8 * t + 8, 0, 0:8] = 1.0
        u, p, states = np.zeros_like(ghost), np.zeros_like(ghost), []
        for _ in range(2):
            source = 0.5 * diff(u)
            for _ in range(2):
                p = (near_sum(p) + ghost - source) / 6.0
            u = 0.35 * u + 0.1 * near_sum(u) + 0.5 * diff(p)
            states.append(u)
        a, q, wall = np.zeros_like(ghost), np.zeros_like(ghost), 0.0
        for u in reversed(states):
            a = a + u
            spread, total = q - 0.5 * diff(a), 0.0
            for _ in range(2):
                total = total + spread / 6.0
                spread = near_sum(spread) / 6.0
            a = 0.35 * a + 0.1 * near_sum(a) + 0.5 * diff(total)
            q = spread
            wall = wall + total[:, :, 0]
        return wall.reshape(TY, blocks, TY, 8, 16, 8).sum((3, 5))

    def matrix(got):
        m = np.zeros((LANES, LANES), np.float32)
        for t in range(TY):
            for x in range(16):
                m[t * 16 + x, 0:TY * 16] = np.roll(got[t], x, 1).reshape(-1)
        return m

    middle, low, high = sums(3, 1), sums(2, 0), sums(2, 1)
    return np.concatenate([matrix(middle[:, 1]), matrix(middle[:, 2]), matrix(middle[:, 0]),
                           matrix(low[:, 0]), matrix(high[:, 1])], axis=1)


def vmem(n):
    return [pl.BlockSpec(memory_space=pltpu.VMEM)] * n


def shape(*dims):
    return jax.ShapeDtypeStruct(dims, jnp.float32)


def kept(*dims):
    return pltpu.VMEM(dims, jnp.float32)


def in_hbm(array):
    return pltpu.with_memory_space_constraint(array, pltpu.HBM)


def swapped(array, axis, first):
    pairs = []
    for i in range(first, lax.axis_size(axis) - 1, 2):
        pairs += [(i, i + 1), (i + 1, i)]
    return lax.ppermute(array, axis, pairs)


def per_device(response, field_pairs, tile_owner, electrode_volts):
    own = field_pairs[0]
    labels = tile_owner[..., 0]
    gy, gz = lax.axis_index("gy"), lax.axis_index("gz")
    devices = lax.axis_size(AXES)
    half = pltpu.HBM((2, PART, COLS, LANES), jnp.float32)
    strip, tiles = kept(2, HY, COLS, LANES), kept(2, ROWS, 8, LANES)
    slab = pltpu.HBM((2, 2 * HY + HALF, 8, LANES), jnp.float32)

    def limit(mib):
        return pltpu.CompilerParams(vmem_limit_bytes=mib * 1024 * 1024)

    far, near = pl.pallas_call(
        strips_kernel, out_shape=(strip, strip), in_specs=vmem(1), out_specs=vmem(2), compiler_params=limit(4),
    )(own)
    far = swapped(far, "gy", 1)
    near = swapped(near, "gy", 0)
    mine, near = lax.optimization_barrier((own, near))
    row = pl.pallas_call(
        wall_kernel, out_shape=kept(devices, LANES), in_specs=vmem(3), out_specs=vmem(1)[0],
        scratch_shapes=scratch(EXT, LOWER) + [pltpu.VMEM((1, LANES), jnp.float32)], compiler_params=limit(12),
    )(mine, near, jnp.pad(electrode_volts, (VOLT, LANES - VOLT - 2))[None])
    mine, row = lax.optimization_barrier((mine, row))
    z_near, z_far = pl.pallas_call(
        tiles_kernel, out_shape=(tiles, tiles), in_specs=vmem(1), out_specs=vmem(2), compiler_params=limit(8),
    )(mine)
    z_far = swapped(z_far, "gz", 1)
    z_near = swapped(z_near, "gz", 0)
    yd, yu, near, far = pl.pallas_call(
        pack_kernel, out_shape=(strip, strip, slab, slab), in_specs=vmem(3),
        out_specs=vmem(2) + [pl.BlockSpec(memory_space=pl.ANY)] * 2,
        scratch_shapes=[pltpu.VMEM((2, 2 * HY + HALF, 8, LANES), jnp.float32)] * 2 + [pltpu.SemaphoreType.DMA((2,))],
        compiler_params=limit(8),
    )(own, far, near)
    far, near, row = lax.optimization_barrier((far, near, row))
    far = swapped(far, "gz", 1)
    near = swapped(near, "gz", 0)
    rows = lax.all_to_all(row, AXES, 0, 0, tiled=True)

    mine, _ = lax.optimization_barrier((own, row))
    def bulk(part, block, load):
        return pl.pallas_call(
            functools.partial(bulk_kernel, part), out_shape=(half, half), in_specs=vmem(7),
            out_specs=[pl.BlockSpec(memory_space=pl.ANY)] * 2,
            scratch_shapes=scratch(PART + 2 * HY, BULK) + [pltpu.VMEM((2, PART, COLS, LANES), jnp.float32)] * 2
            + [pltpu.SemaphoreType.DMA((3,))], compiler_params=limit(20),
            cost_estimate=pl.CostEstimate(flops=10 ** 8, bytes_accessed=load * 10 ** 6, transcendentals=0),
        )(block, yd, yu, z_far, z_near, far, near)

    mains, extras = [], []
    for part in range(PARTS):
        main, send = bulk(part, mine, 36 if part == 0 else 9)
        mains.append(main)
        mine, _ = lax.optimization_barrier((own, send))
        if part == PARTS - 1:
            send, rows = lax.optimization_barrier((send, rows))
        extras.append(lax.ppermute(send, "grp", [(0, 1)]))

    fenced = jnp.pad(labels, ((0, 0), (1, 1), (0, 0)), constant_values=-1)
    side = (gz == lax.axis_size("gz") - 1).astype(jnp.int32)
    by_wall = lax.dynamic_slice(fenced, (side, gy * TY, 0), (1, 8, 16)).reshape(1, LANES)
    by_block = jnp.pad(labels.reshape(2, 8, TY * 16), ((0, 0), (0, 0), (0, LANES - TY * 16)), constant_values=-1)
    total, grad = pl.pallas_call(
        volts_kernel, out_shape=(kept(2, ROWS, COLS, LANES), shape(1, 2)),
        in_specs=[pl.BlockSpec(memory_space=pl.ANY)] * PARTS + vmem(3) + [pl.BlockSpec(memory_space=pl.ANY)], out_specs=vmem(2),
        scratch_shapes=scratch(EXT, NEAR) + [pltpu.VMEM((EXT, COLS, LANES), jnp.float32), pltpu.VMEM(response.shape, jnp.float32),
                                             pltpu.SemaphoreType.DMA((PARTS + 1,))],
        compiler_params=limit(16),
    )(*[in_hbm(main) for main in mains], rows, by_wall, by_block, in_hbm(response))
    advanced = pl.pallas_call(
        sum_kernel, out_shape=shape(1, 2, ROWS, COLS, LANES), in_specs=vmem(PARTS + 1), out_specs=vmem(1)[0],
        compiler_params=limit(8),
    )(total, *extras)
    return (advanced, grad.reshape(2))


def solution(mesh):
    response = jnp.asarray(wall_response())
    placed = (P("grp", None, "gy", "gz", None), P(), P(AXES))
    return jax.shard_map(
        functools.partial(per_device, response), mesh=mesh, in_specs=placed,
        out_specs=(P("grp", None, "gy", "gz", None), P(AXES)), check_vma=False,
    )
```

```python
import functools

import jax
import jax.numpy as jnp
import numpy as np
from jax import lax
from jax.experimental import pallas as pl
from jax.experimental.pallas import tpu as pltpu
from jax.sharding import PartitionSpec as P

AXES = ("grp", "gy", "gz")
TY = 6
VOLT = (TY + 1) * 16
ROWS, COLS, LANES = 48, 16, 128
HY, HZ = 8, 12
EXT = ROWS + 2 * HY
RIM = 4
HALF = EXT // 2 - RIM
PARTS = 3
PART = ROWS // PARTS
SIXTH = 1.0 / 6.0
SHARE, PIECES = 0.34, 3

BULK = ((12, 40), (8, 32), (4, 24))
NEAR = ((0, COLS),) * 3
LOWER = ((0, COLS), (0, 8), (0, 8))
UPPER = ((0, COLS), (-8, 8), (-8, 8))


def piece(outer, inner):
    start = outer[0] - inner[0]
    return slice(start, start + inner[1])


def rows_loop(first, last, body, pieces):
    n = (last - first + 1) // pieces
    for i in range(pieces):
        body(first + i * n, n)


def zshift(v, ends):
    z = v.shape[1]
    zp, zm = pltpu.roll(v, z - 1, 1), pltpu.roll(v, 1, 1)
    if ends is None:
        layer = lax.broadcasted_iota(jnp.int32, v.shape, 1)
        return jnp.where(layer == z - 1, 0.0, zp), jnp.where(layer == 0, 0.0, zm)

    def cut(shifted, at, when):
        g = at // 8 * 8
        hit = (lax.broadcasted_iota(jnp.int32, (1, 8, LANES), 1) == at - g) & when
        tile = jnp.where(jnp.broadcast_to(hit, (v.shape[0], 8, LANES)), 0.0, shifted[:, g:g + 8])
        return jnp.concatenate([part for part in (shifted[:, :g], tile, shifted[:, g + 8:]) if part.shape[1]], axis=1)
    at, below, above = ends
    return cut(zp, at + COLS - 1, above), cut(zm, at, below)


def beside(c, share):
    n, z, _ = c.shape
    k = int(n * share)
    if k == 0:
        return pltpu.roll(c, 1, 2) + pltpu.roll(c, LANES - 1, 2)
    row = lax.broadcasted_iota(jnp.int32, (LANES, LANES), 0)
    lane = lax.broadcasted_iota(jnp.int32, (LANES, LANES), 1)
    apart = (row - lane) & (LANES - 1)
    ring = jnp.where((apart == 1) | (apart == LANES - 1), 1.0, 0.0).astype(jnp.bfloat16)
    rest, total = c[:k].reshape(k * z, LANES), None
    for i in range(PIECES):
        part = rest.astype(jnp.bfloat16)
        got = jnp.dot(part, ring, preferred_element_type=jnp.float32)
        total = got if total is None else total + got
        if i < PIECES - 1:
            rest = rest - part.astype(jnp.float32)
    rolled = pltpu.roll(c[k:], 1, 2) + pltpu.roll(c[k:], LANES - 1, 2)
    return jnp.concatenate([total.reshape(k, z, LANES), rolled], axis=0)


def around(w, ends):
    c = w[1:-1]
    zp, zm = zshift(c, ends)
    s = (w[:-2] + w[2:]) + (zp + zm)
    return c, s + beside(c, 0.0 if ends is None else SHARE), zp - zm


def zero_edges(edge, ref):
    for when, r in ((edge[0], HY - 1), (edge[1], ref.shape[0] - HY)):
        if when is not None:
            ref[r] = jnp.where(when, 0.0, ref[r])


def early_scratch(rows, window):
    return [pltpu.VMEM((rows, window[0][1], LANES), jnp.float32)] * 6


def mid_scratch(rows, window):
    return [pltpu.VMEM((rows, window[1][1], LANES), jnp.float32)] * 7


def late_scratch(rows, window):
    return [pltpu.VMEM((rows, window[2][1], LANES), jnp.float32)] * 8


def scratch(rows, window):
    return early_scratch(rows, window) + mid_scratch(rows, window) + late_scratch(rows, window)


def forward(edge, ghost, window, pieces, early, mid, spread=False):
    U, V, SRC, B, Q, U1 = early
    SRC2, B2, Q2, P2, A = mid[:5]
    top = U1.shape[0] - 1
    closed = window[0][0] == 0
    ends = [None if closed else (part[0],) + edge[2:] for part in window]

    def span(k):
        return (1, top - 1) if spread else (k, top - k)

    m = piece(window[0], window[1])

    def finish(ref):
        if ghost is not None:
            ref[...] += ghost[...]
        zero_edges(edge, ref)

    def stage_a(r, n):
        c, s, d = around(U[pl.ds(r - 1, n + 2)], ends[0])
        src = (0.5 / 6.0) * d
        SRC[pl.ds(r, n)] = src
        B[pl.ds(r, n)] = 0.35 * c + 0.1 * s
        _, s, _ = around(V[pl.ds(r - 1, n + 2)], ends[0])
        Q[pl.ds(r, n)] = s * SIXTH - src
    if ghost is not None:
        Q[...] = ghost[...]
        zero_edges(edge, Q)
    else:
        rows_loop(*span(1), stage_a, pieces)
        finish(Q)

    def stage_b(r, n):
        _, s, _ = around(Q[pl.ds(r - 1, n + 2)], ends[0])
        s = s * SIXTH
        V[pl.ds(r, n)] = s if ghost is not None else s - SRC[pl.ds(r, n)]
    rows_loop(*span(2), stage_b, pieces)
    finish(V)

    def stage_c(r, n):
        zp, zm = zshift(V[pl.ds(r, n)], ends[0])
        u = 0.5 * (zp - zm)
        U1[pl.ds(r, n)] = u if ghost is not None else u + B[pl.ds(r, n)]
    rows_loop(*span(3), stage_c, pieces)
    zero_edges(edge, U1)

    def stage_d(r, n):
        c, s, d = around(U1[pl.ds(r - 1, n + 2)], ends[0])
        src = (0.5 / 6.0) * d[:, m]
        SRC2[pl.ds(r, n)] = src
        B2[pl.ds(r, n)] = 0.35 * c[:, m] + 0.1 * s[:, m]
        _, s, _ = around(V[pl.ds(r - 1, n + 2)], ends[0])
        Q2[pl.ds(r, n)] = s[:, m] * SIXTH - src
    rows_loop(*span(3), stage_d, pieces)
    finish(Q2)

    def stage_e(r, n):
        _, s, _ = around(Q2[pl.ds(r - 1, n + 2)], ends[1])
        P2[pl.ds(r, n)] = s * SIXTH - SRC2[pl.ds(r, n)]
    rows_loop(*span(4), stage_e, pieces)
    if ghost is not None:
        P2[...] += ghost[...]

    def stage_f(r, n):
        zp, zm = zshift(P2[pl.ds(r, n)], ends[1])
        A[pl.ds(r, n)] = B2[pl.ds(r, n)] + 0.5 * (zp - zm)
    rows_loop(*span(4), stage_f, pieces)
    zero_edges(edge, A)


def adjoint(edge, window, pieces, a2, pot, u1, mid, late, give, spread=False):
    BM, SP = mid[5:7]
    S2, T, B, A1, S3, SP2, S4, T2 = late
    top = SP.shape[0] - 1
    closed = window[0][0] == 0
    ends = [None if closed else (part[0],) + edge[2:] for part in window]

    def span(k):
        return (1, top - 1) if spread else (k, top - k)

    third = window[2][0]
    m = piece(window[1], window[2])

    def take(source, inner, r, n):
        ref, place = source
        return ref[pl.ds(r, n), piece(place, inner), :]

    def stage_g(r, n):
        c, s, d = around(take(a2, window[1], r - 1, n + 2), ends[1])
        BM[pl.ds(r, n)] = 0.35 * c + 0.1 * s
        sp = -0.5 * d
        if pot is not None:
            sp = sp + take(pot, window[1], r, n)
        SP[pl.ds(r, n)] = sp
    rows_loop(*span(4), stage_g, pieces)
    zero_edges(edge, SP)

    def stage_h(r, n):
        c, s, _ = around(SP[pl.ds(r - 1, n + 2)], ends[1])
        c, s = c[:, m], s[:, m] * SIXTH
        S2[pl.ds(r, n)] = s
        T[pl.ds(r, n)] = (c + s) * SIXTH
    rows_loop(*span(5), stage_h, pieces)
    zero_edges(edge, S2)

    def stage_i(r, n):
        _, s, _ = around(S2[pl.ds(r - 1, n + 2)], ends[2])
        S3[pl.ds(r, n)] = s * SIXTH
        zp, zm = zshift(T[pl.ds(r, n)], ends[2])
        a = BM[pl.ds(r, n), m, :] + 0.5 * (zp - zm)
        if u1 is not None:
            a = a + take(u1, window[2], r, n)
        A1[pl.ds(r, n)] = a
    rows_loop(*span(6), stage_i, pieces)
    zero_edges(edge, A1)

    def stage_j(r, n):
        if give is None:
            zp, zm = zshift(A1[pl.ds(r, n)], ends[2])
            d = zp - zm
        else:
            c, s, d = around(A1[pl.ds(r - 1, n + 2)], ends[2])
            B[pl.ds(r, n)] = 0.35 * c + 0.1 * s
        SP2[pl.ds(r, n)] = S3[pl.ds(r, n)] - 0.5 * d
    rows_loop(*span(6), stage_j, pieces)
    zero_edges(edge, SP2)

    def stage_k(r, n):
        c, s, _ = around(SP2[pl.ds(r - 1, n + 2)], ends[2])
        s = s * SIXTH
        S4[pl.ds(r, n)] = s
        T2[pl.ds(r, n)] = (c + s) * SIXTH
    rows_loop(*span(7), stage_k, pieces)
    zero_edges(edge, S4)
    if give is None:
        return
    own = slice(third, third + COLS)

    def stage_l(r, n):
        _, s, _ = around(S4[pl.ds(r - 1, n + 2)], ends[2])
        zp, zm = zshift(T2[pl.ds(r, n)], ends[2])
        u = B[pl.ds(r, n)] + 0.5 * (zp - zm)
        give(r - HY, n, u[:, own], s[:, own] * SIXTH)
    rows_loop(*span(8), stage_l, 2)


def load_extended(dst, f, part, own, yd, yu, below, above):
    first, end = part * PART, part * PART + PART + 2 * HY
    top = HY + ROWS

    def rows(src_first, src_end, src, offset, layers, to_layer):
        r0, r1 = max(first, src_first), min(end, src_end)
        if r0 < r1:
            at = slice(offset + r0 - src_first, offset + r1 - src_first)
            dst[r0 - first:r1 - first, to_layer:to_layer + layers.stop - layers.start, :] = src[f, at, layers, :]

    block, tile = slice(0, COLS), slice(0, 8)
    rows(0, HY, yd, 0, block, HZ)
    rows(HY, top, own, 0, block, HZ)
    rows(top, EXT, yu, 0, block, HZ)
    for (z, rest), near, far in ((below, 4, 0), (above, HZ + COLS, HZ + COLS + 8)):
        rows(HY, top, z, 0, tile, near)
        rows(0, HY, rest, 0, tile, near)
        rows(top, EXT, rest, HY, tile, near)
        for k in range(2):
            rows(RIM + k * HALF, RIM + (k + 1) * HALF, rest, 2 * HY, slice(4 * k, 4 * k + 4), far)


def is_even(axis):
    return lax.rem(lax.axis_index(axis), 2) == 0


def strips_kernel(own, far, near):
    even = is_even("gy")
    low, high = own[:, 0:HY], own[:, ROWS - HY:]
    far[...] = jnp.where(even, low, high)
    near[...] = jnp.where(even, high, low)


def tiles_kernel(own, near, far):
    even = is_even("gz")
    low, high = own[:, :, 0:8, :], own[:, :, 8:16, :]
    near[...] = jnp.where(even, high, low)
    far[...] = jnp.where(even, low, high)


def pack_kernel(own, far, near, yd, yu, near_out, far_out, z_near, z_far, sems):
    even = is_even("gy")
    yd[...] = jnp.where(even, far[...], near[...])
    yu[...] = jnp.where(even, near[...], far[...])

    def pack(dst, whole, part):
        dst[:, 0:HY] = yd[:, :, whole:whole + 8, :]
        dst[:, HY:2 * HY] = yu[:, :, whole:whole + 8, :]
        at, edge = 2 * HY, HY - RIM
        dst[:, at:at + edge, 0:4, :] = yd[:, RIM:, part:part + 4, :]
        dst[:, at + edge:, 0:4, :] = own[:, 0:HALF - edge, part:part + 4, :]
        dst[:, at:at + HALF - edge, 4:8, :] = own[:, HALF - edge:, part:part + 4, :]
        dst[:, at + HALF - edge:, 4:8, :] = yu[:, 0:edge, part:part + 4, :]

    copies = [pltpu.make_async_copy(*pair, sems.at[i]) for i, pair in enumerate(((z_far, far_out), (z_near, near_out)))]
    upward = is_even("gz")

    def fill(dst, when, copy):
        @pl.when(when)
        def _():
            pack(dst, 8, 4)

        @pl.when(jnp.logical_not(when))
        def _():
            pack(dst, 0, 8)
        copy.start()
    fill(z_far, jnp.logical_not(upward), copies[0])
    fill(z_near, upward, copies[1])
    for copy in copies:
        copy.wait()


HIGHEST = lax.Precision.HIGHEST


def edges():
    gy, gz = lax.axis_index("gy"), lax.axis_index("gz")
    return (gy == 0, gy == lax.axis_size("gy") - 1, gz == 0, gz == lax.axis_size("gz") - 1)


def iota(shape, dim):
    return lax.broadcasted_iota(jnp.int32, shape, dim)


def tile_volts(first, second, labels):
    lab = jnp.broadcast_to(labels, first.shape) - 2 * iota(first.shape, 0)
    hit = jnp.where(lab == 0, first, 0.0) + jnp.where(lab == 1, second, 0.0)
    return jnp.sum(hit, axis=0, keepdims=True)


def fill_ghost(upper, ghost, volts):
    lane, row = iota((8, LANES), 1), iota((8, LANES), 0)
    apart = jnp.where((lane >> 4) == row, jnp.broadcast_to(volts, (8, LANES)), 0.0)
    spread = ((iota((LANES, LANES), 0) & 15) == (iota((LANES, LANES), 1) >> 3)).astype(jnp.float32)
    wall = jnp.dot(apart, spread, precision=HIGHEST, preferred_element_type=jnp.float32) * (1.0 / 6.0)
    layer = iota((COLS, LANES), 0) == jnp.where(upper, COLS - 1, 0)
    for ty in range(8):
        tile = jnp.where(layer, jnp.broadcast_to(wall[ty:ty + 1], (COLS, LANES)), 0.0)
        ghost[8 * ty:8 * ty + 8] = jnp.broadcast_to(tile[None], (8, COLS, LANES))


def wall_tiles(layer, T, T2):
    w = jnp.sum((T[:, layer, :] + T2[:, layer, :]).reshape(8, 8, LANES), axis=1)
    gather = ((iota((LANES, LANES), 0) >> 3) == (iota((LANES, LANES), 1) & 15)).astype(jnp.float32)
    sums = jnp.dot(w, gather, precision=HIGHEST, preferred_element_type=jnp.float32)
    first = lax.rem(lax.axis_index("gy"), 2)
    lane = iota((8, LANES), 1)
    keep = ((lane >> 4) + first == iota((8, LANES), 0)) & (lane < VOLT)
    return jnp.sum(jnp.where(keep, sums, 0.0), axis=0, keepdims=True)


def split(refs):
    return refs[:6], refs[6:13], refs[13:21]


def wall_kernel(own, near, volts, row, *refs):
    early, mid, late = split(refs)
    sums = refs[21]
    ylo, yhi, zlo, zhi = edges()
    edge = (ylo, yhi, None, None)
    is_forward = lax.axis_index("grp") == 0
    sums[...] = jnp.zeros((1, LANES), jnp.float32)

    @pl.when(jnp.logical_or(zlo, zhi))
    def _():
        for ref in early + mid + late:
            for r in (0, EXT - 1):
                ref[r] = jnp.zeros(ref.shape[1:], jnp.float32)
        for f in range(2):
            early[f][0:HY] = jnp.where(is_even("gy"), 0.0, near[f])
            early[f][HY:HY + ROWS] = own[f]
            early[f][HY + ROWS:] = jnp.where(is_even("gy"), near[f], 0.0)

    def side(window, layer):
        @pl.when(is_forward)
        def _():
            forward(edge, None, window, 1, early, mid, True)
            adjoint(edge, window, 1, (mid[4], window[1]), None, (early[5], window[0]), mid, late, None, True)

        @pl.when(jnp.logical_not(is_forward))
        def _():
            adjoint(edge, window, 1, (early[0], window[0]), (early[1], window[0]), None, mid, late, None, True)

        sums[...] = wall_tiles(layer, late[1], late[7])

    @pl.when(zlo)
    def _():
        side(LOWER, 0)

    @pl.when(zhi)
    def _():
        side(UPPER, 7)

    row[...] = jnp.broadcast_to(sums[...] + volts[...], row.shape)


def bulk_kernel(part, own, yd, yu, z_far, z_near, far, near, main_out, send_out, *refs):
    far, near = (z_far, far), (z_near, near)
    early, mid, late = split(refs)
    main, send, sems = refs[21:]
    ylo, yhi, zlo, zhi = edges()
    edge = (ylo if part == 0 else None, yhi if part == PARTS - 1 else None, zlo, zhi)
    is_forward = lax.axis_index("grp") == 0

    @pl.when(is_even("gz"))
    def _():
        for f in range(2):
            load_extended(early[f], f, part, own, yd, yu, far, near)

    @pl.when(jnp.logical_not(is_even("gz")))
    def _():
        for f in range(2):
            load_extended(early[f], f, part, own, yd, yu, near, far)

    def leave(ref, out, rows, copies):
        copy = pltpu.make_async_copy(ref.at[:, rows], out.at[:, rows], sems.at[len(copies)])
        copy.start()
        copies.append(copy)

    def into(ref, out, copies):
        def give(r, n, u, p):
            ref[0, pl.ds(r, n)] = u
            ref[1, pl.ds(r, n)] = p
            leave(ref, out, pl.ds(r, n), copies)
        return give

    @pl.when(is_forward)
    def _():
        copies = []
        forward(edge, None, BULK, 1, early, mid)
        at = (slice(HY, HY + PART), slice(BULK[1][0], BULK[1][0] + COLS))
        main[0] = mid[4][at]
        main[1] = mid[3][at]
        leave(main, main_out, pl.ds(0, PART), copies)
        adjoint(edge, BULK, 1, (mid[4], BULK[1]), None, (early[5], BULK[0]), mid, late, into(send, send_out, copies))
        for copy in copies:
            copy.wait()

    @pl.when(jnp.logical_not(is_forward))
    def _():
        copies = []
        adjoint(edge, BULK, 1, (early[0], BULK[0]), (early[1], BULK[0]), None, mid, late, into(main, main_out, copies))
        for copy in copies:
            copy.wait()


def volts_kernel(*refs):
    parts, refs = refs[:PARTS], refs[PARTS:]
    rows, near, labels, far_response, out, grad = refs[:6]
    early, mid, late = split(refs[6:])
    ghost, response, sems = refs[27:]
    copies = [pltpu.make_async_copy(part, out.at[:, i * PART:(i + 1) * PART], sems.at[i]) for i, part in enumerate(parts)]
    fetch = pltpu.make_async_copy(far_response, response, sems.at[PARTS])
    for copy in copies:
        copy.start()
    fetch.start()
    ylo, yhi, zlo, zhi = edges()
    edge = (ylo, yhi, None, None)
    at_wall = jnp.logical_or(zlo, zhi)
    is_forward = lax.axis_index("grp") == 0
    n = rows.shape[0]
    first = jnp.broadcast_to(rows[:, VOLT:VOLT + 1], (n, LANES))
    second = jnp.broadcast_to(rows[:, VOLT + 1:VOLT + 2], (n, LANES))

    @pl.when(at_wall)
    def _():
        fill_ghost(zhi, ghost, tile_volts(first, second, near[...]))
        forward(edge, ghost, NEAR, 1, early, mid)

    for copy in copies:
        copy.wait()

    @pl.when(jnp.logical_and(at_wall, is_forward))
    def _():
        out[0] += mid[4][HY:HY + ROWS]
        out[1] += mid[3][HY:HY + ROWS]

    @pl.when(jnp.logical_and(at_wall, jnp.logical_not(is_forward)))
    def _():
        def give(r, n, u, p):
            out[0, pl.ds(r, n)] += u
            out[1, pl.ds(r, n)] += p
        adjoint(edge, NEAR, 1, (mid[4], NEAR[1]), None, (early[5], NEAR[0]), mid, late, give)

    fetch.wait()
    gy, gz = lax.axis_size("gy"), lax.axis_size("gz")
    me = (lax.axis_index("grp") * gy + lax.axis_index("gy")) * gz + lax.axis_index("gz")
    pair = [jnp.zeros((gy, LANES), jnp.float32)] * 2
    block, lane = iota((gy, LANES), 0), iota((gy, LANES), 1)
    for s in range(2):
        v = jnp.concatenate([tile_volts(first, second, labels[s, g:g + 1]) for g in range(gy)], axis=0)
        r = jnp.dot(v, response[...], precision=HIGHEST, preferred_element_type=jnp.float32)
        r = [r[:, k * LANES:(k + 1) * LANES] for k in range(5)]
        w = jnp.where(block == 0, r[3], jnp.where(block == gy - 1, r[4], r[0]))
        w = w + jnp.where(block == 0, 0.0, pltpu.roll(r[1], 1, 0))
        w = w + jnp.where(block == gy - 1, 0.0, pltpu.roll(r[2], gy - 1, 0))
        got = sum(rows[pl.ds(g * gy * gz + s * (gz - 1), gy, stride=gz), :] for g in range(2))
        odd = (block & 1) == 1
        w = w + jnp.where(odd, got, pltpu.roll(got, LANES - 16, 1))
        below = pltpu.roll(pltpu.roll(got, 32, 1), 1, 0)
        above = pltpu.roll(pltpu.roll(got, 80, 1), gy - 1, 0)
        w = w + jnp.where((block > 0) & jnp.logical_not(odd) & (lane < 16), below, 0.0)
        w = w + jnp.where((block < gy - 1) & odd & (lane >= 80), above, 0.0)
        for j in range(2):
            pair[j] = pair[j] + jnp.where(labels[s] == 2 * me + j, w, 0.0)
    total = [jnp.sum(p) for p in pair]
    grad[...] = jnp.where(iota((1, 2), 1) == 0, total[0], total[1])


def sum_kernel(which, main, *refs):
    extras, (out, total, sems) = refs[:len(which)], refs[-3:]
    copies = []
    for n, i in enumerate(which):
        at = slice(i * PART, (i + 1) * PART)
        total[:, n * PART:(n + 1) * PART] = main[:, at] + extras[n][...]
        copies.append(pltpu.make_async_copy(total.at[:, n * PART:(n + 1) * PART], out.at[0, :, at], sems.at[n]))
        copies[-1].start()
    for copy in copies:
        copy.wait()


def last_sum_kernel(which, main, extra, before, out, total, sems):
    sum_kernel(which, main, extra, out, total, sems)


def wall_response():
    def near_sum(f):
        g = np.pad(f, ((0, 0), (1, 1), (1, 1), (0, 0)))
        t = g[:, 2:, 1:-1] + g[:, :-2, 1:-1] + g[:, 1:-1, 2:] + g[:, 1:-1, :-2]
        return t + np.roll(f, 1, 3) + np.roll(f, -1, 3)

    def diff(f):
        g = np.pad(f, ((0, 0), (0, 0), (1, 1), (0, 0)))
        return g[:, :, 2:] - g[:, :, :-2]

    def sums(blocks, at):
        ghost = np.zeros((TY, blocks * ROWS, 13, LANES))
        for t in range(TY):
            ghost[t, at * ROWS + 8 * t:at * ROWS + 8 * t + 8, 0, 0:8] = 1.0
        u, p, states = np.zeros_like(ghost), np.zeros_like(ghost), []
        for _ in range(2):
            source = 0.5 * diff(u)
            for _ in range(2):
                p = (near_sum(p) + ghost - source) / 6.0
            u = 0.35 * u + 0.1 * near_sum(u) + 0.5 * diff(p)
            states.append(u)
        a, q, wall = np.zeros_like(ghost), np.zeros_like(ghost), 0.0
        for u in reversed(states):
            a = a + u
            spread, total = q - 0.5 * diff(a), 0.0
            for _ in range(2):
                total = total + spread / 6.0
                spread = near_sum(spread) / 6.0
            a = 0.35 * a + 0.1 * near_sum(a) + 0.5 * diff(total)
            q = spread
            wall = wall + total[:, :, 0]
        return wall.reshape(TY, blocks, TY, 8, 16, 8).sum((3, 5))

    def matrix(got):
        m = np.zeros((LANES, LANES), np.float32)
        for t in range(TY):
            for x in range(16):
                m[t * 16 + x, 0:TY * 16] = np.roll(got[t], x, 1).reshape(-1)
        return m

    middle, low, high = sums(3, 1), sums(2, 0), sums(2, 1)
    return np.concatenate([matrix(middle[:, 1]), matrix(middle[:, 2]), matrix(middle[:, 0]),
                           matrix(low[:, 0]), matrix(high[:, 1])], axis=1)


def vmem(n):
    return [pl.BlockSpec(memory_space=pltpu.VMEM)] * n


def shape(*dims):
    return jax.ShapeDtypeStruct(dims, jnp.float32)


def kept(*dims):
    return pltpu.VMEM(dims, jnp.float32)


def in_hbm(array):
    return pltpu.with_memory_space_constraint(array, pltpu.HBM)


def swapped(array, axis, first):
    pairs = []
    for i in range(first, lax.axis_size(axis) - 1, 2):
        pairs += [(i, i + 1), (i + 1, i)]
    return lax.ppermute(array, axis, pairs)


def per_device(response, field_pairs, tile_owner, electrode_volts):
    own = field_pairs[0]
    labels = tile_owner[..., 0]
    gy, gz = lax.axis_index("gy"), lax.axis_index("gz")
    devices = lax.axis_size(AXES)
    half = pltpu.HBM((2, PART, COLS, LANES), jnp.float32)
    strip, tiles = kept(2, HY, COLS, LANES), kept(2, ROWS, 8, LANES)
    slab = pltpu.HBM((2, 2 * HY + HALF, 8, LANES), jnp.float32)

    def limit(mib):
        return pltpu.CompilerParams(vmem_limit_bytes=mib * 1024 * 1024)

    far, near = pl.pallas_call(
        strips_kernel, out_shape=(strip, strip), in_specs=vmem(1), out_specs=vmem(2), compiler_params=limit(4),
    )(own)
    far = swapped(far, "gy", 1)
    near = swapped(near, "gy", 0)
    mine, near = lax.optimization_barrier((own, near))
    row = pl.pallas_call(
        wall_kernel, out_shape=kept(devices, LANES), in_specs=vmem(3), out_specs=vmem(1)[0],
        scratch_shapes=scratch(EXT, LOWER) + [pltpu.VMEM((1, LANES), jnp.float32)], compiler_params=limit(12),
    )(mine, near, jnp.pad(electrode_volts, (VOLT, LANES - VOLT - 2))[None])
    mine, row = lax.optimization_barrier((mine, row))
    z_near, z_far = pl.pallas_call(
        tiles_kernel, out_shape=(tiles, tiles), in_specs=vmem(1), out_specs=vmem(2), compiler_params=limit(8),
    )(mine)
    z_far = swapped(z_far, "gz", 1)
    z_near = swapped(z_near, "gz", 0)
    yd, yu, near, far = pl.pallas_call(
        pack_kernel, out_shape=(strip, strip, slab, slab), in_specs=vmem(3),
        out_specs=vmem(2) + [pl.BlockSpec(memory_space=pl.ANY)] * 2,
        scratch_shapes=[pltpu.VMEM((2, 2 * HY + HALF, 8, LANES), jnp.float32)] * 2 + [pltpu.SemaphoreType.DMA((2,))],
        compiler_params=limit(8),
    )(own, far, near)
    far, near, row = lax.optimization_barrier((far, near, row))
    far = swapped(far, "gz", 1)
    near = swapped(near, "gz", 0)
    rows = lax.all_to_all(row, AXES, 0, 0, tiled=True)

    mine, _ = lax.optimization_barrier((own, row))
    def bulk(part, block, load):
        return pl.pallas_call(
            functools.partial(bulk_kernel, part), out_shape=(half, half), in_specs=vmem(7),
            out_specs=[pl.BlockSpec(memory_space=pl.ANY)] * 2,
            scratch_shapes=scratch(PART + 2 * HY, BULK) + [pltpu.VMEM((2, PART, COLS, LANES), jnp.float32)] * 2
            + [pltpu.SemaphoreType.DMA((3,))], compiler_params=limit(20),
            cost_estimate=pl.CostEstimate(flops=10 ** 8, bytes_accessed=load * 10 ** 6, transcendentals=0),
        )(block, yd, yu, z_far, z_near, far, near)

    mains, extras = [], []
    for part in range(PARTS):
        main, send = bulk(part, mine, 36 if part == 0 else 9)
        mains.append(main)
        mine, _ = lax.optimization_barrier((own, send))
        if part == PARTS - 1:
            send, rows = lax.optimization_barrier((send, rows))
        extras.append(lax.ppermute(send, "grp", [(0, 1)]))

    fenced = jnp.pad(labels, ((0, 0), (1, 1), (0, 0)), constant_values=-1)
    side = (gz == lax.axis_size("gz") - 1).astype(jnp.int32)
    by_wall = lax.dynamic_slice(fenced, (side, gy * TY, 0), (1, 8, 16)).reshape(1, LANES)
    by_block = jnp.pad(labels.reshape(2, 8, TY * 16), ((0, 0), (0, 0), (0, LANES - TY * 16)), constant_values=-1)
    total, grad = pl.pallas_call(
        volts_kernel, out_shape=(kept(2, ROWS, COLS, LANES), shape(1, 2)),
        in_specs=[pl.BlockSpec(memory_space=pl.ANY)] * PARTS + vmem(3) + [pl.BlockSpec(memory_space=pl.ANY)], out_specs=vmem(2),
        scratch_shapes=scratch(EXT, NEAR) + [pltpu.VMEM((EXT, COLS, LANES), jnp.float32), pltpu.VMEM(response.shape, jnp.float32),
                                             pltpu.SemaphoreType.DMA((PARTS + 1,))],
        compiler_params=limit(16),
    )(*[in_hbm(main) for main in mains], rows, by_wall, by_block, in_hbm(response))
    def sums(kernel, which, operands, specs, aliases):
        return pl.pallas_call(
            functools.partial(kernel, which), out_shape=pltpu.HBM((1, 2, ROWS, COLS, LANES), jnp.float32), in_specs=specs,
            out_specs=pl.BlockSpec(memory_space=pl.ANY), input_output_aliases=aliases,
            scratch_shapes=[pltpu.VMEM((2, len(which) * PART, COLS, LANES), jnp.float32), pltpu.SemaphoreType.DMA((len(which),))],
            compiler_params=limit(8),
        )(*operands)

    early = tuple(range(PARTS - 1))
    advanced = sums(sum_kernel, early, (total, *extras[:-1]), vmem(PARTS), {})
    advanced = sums(last_sum_kernel, (PARTS - 1,), (total, extras[-1], advanced),
                    vmem(2) + [pl.BlockSpec(memory_space=pl.ANY)], {2: 0})
    return (advanced, grad.reshape(2))


def solution(mesh):
    response = jnp.asarray(wall_response())
    placed = (P("grp", None, "gy", "gz", None), P(), P(AXES))
    return jax.shard_map(
        functools.partial(per_device, response), mesh=mesh, in_specs=placed,
        out_specs=(P("grp", None, "gy", "gz", None), P(AXES)), check_vma=False,
    )
```

```python
import functools

import jax
import jax.numpy as jnp
import numpy as np
from jax import lax
from jax.experimental import pallas as pl
from jax.experimental.pallas import tpu as pltpu
from jax.sharding import PartitionSpec as P

AXES = ("grp", "gy", "gz")
TY = 6
VOLT = (TY + 1) * 16
ROWS, COLS, LANES = 48, 16, 128
HY, HZ = 8, 12
EXT = ROWS + 2 * HY
RIM = 4
HALF = EXT // 2 - RIM
PARTS = 3
PART = ROWS // PARTS
SIXTH = 1.0 / 6.0
SHARE, PIECES = 0.2, 3

BULK = ((12, 40), (8, 32), (4, 24))
NEAR = ((0, COLS),) * 3
LOWER = ((0, COLS), (0, 8), (0, 8))
UPPER = ((0, COLS), (-8, 8), (-8, 8))


def piece(outer, inner):
    start = outer[0] - inner[0]
    return slice(start, start + inner[1])


def rows_loop(first, last, body, pieces):
    n = (last - first + 1) // pieces
    for i in range(pieces):
        body(first + i * n, n)


def zshift(v, ends):
    z = v.shape[1]
    zp, zm = pltpu.roll(v, z - 1, 1), pltpu.roll(v, 1, 1)
    if ends is None:
        layer = lax.broadcasted_iota(jnp.int32, v.shape, 1)
        return jnp.where(layer == z - 1, 0.0, zp), jnp.where(layer == 0, 0.0, zm)

    def cut(shifted, at, when):
        g = at // 8 * 8
        hit = (lax.broadcasted_iota(jnp.int32, (1, 8, LANES), 1) == at - g) & when
        tile = jnp.where(jnp.broadcast_to(hit, (v.shape[0], 8, LANES)), 0.0, shifted[:, g:g + 8])
        return jnp.concatenate([part for part in (shifted[:, :g], tile, shifted[:, g + 8:]) if part.shape[1]], axis=1)
    at, below, above = ends
    return cut(zp, at + COLS - 1, above), cut(zm, at, below)


def beside(c, share):
    n, z, _ = c.shape
    k = int(n * share)
    if k == 0:
        return pltpu.roll(c, 1, 2) + pltpu.roll(c, LANES - 1, 2)
    row = lax.broadcasted_iota(jnp.int32, (LANES, LANES), 0)
    lane = lax.broadcasted_iota(jnp.int32, (LANES, LANES), 1)
    apart = (row - lane) & (LANES - 1)
    ring = jnp.where((apart == 1) | (apart == LANES - 1), 1.0, 0.0).astype(jnp.bfloat16)
    rest, total = c[:k].reshape(k * z, LANES), None
    for i in range(PIECES):
        part = rest.astype(jnp.bfloat16)
        got = jnp.dot(part, ring, preferred_element_type=jnp.float32)
        total = got if total is None else total + got
        if i < PIECES - 1:
            rest = rest - part.astype(jnp.float32)
    rolled = pltpu.roll(c[k:], 1, 2) + pltpu.roll(c[k:], LANES - 1, 2)
    return jnp.concatenate([total.reshape(k, z, LANES), rolled], axis=0)


def around(w, ends):
    c = w[1:-1]
    zp, zm = zshift(c, ends)
    s = (w[:-2] + w[2:]) + (zp + zm)
    return c, s + beside(c, 0.0 if ends is None else SHARE), zp - zm


def zero_edges(edge, ref):
    for when, r in ((edge[0], HY - 1), (edge[1], ref.shape[0] - HY)):
        if when is not None:
            ref[r] = jnp.where(when, 0.0, ref[r])


def early_scratch(rows, window):
    return [pltpu.VMEM((rows, window[0][1], LANES), jnp.float32)] * 6


def mid_scratch(rows, window):
    return [pltpu.VMEM((rows, window[1][1], LANES), jnp.float32)] * 7


def late_scratch(rows, window):
    return [pltpu.VMEM((rows, window[2][1], LANES), jnp.float32)] * 8


def scratch(rows, window):
    return early_scratch(rows, window) + mid_scratch(rows, window) + late_scratch(rows, window)


def forward(edge, ghost, window, pieces, early, mid, spread=False):
    U, V, SRC, B, Q, U1 = early
    SRC2, B2, Q2, P2, A = mid[:5]
    top = U1.shape[0] - 1
    closed = window[0][0] == 0
    ends = [None if closed else (part[0],) + edge[2:] for part in window]

    def span(k):
        return (1, top - 1) if spread else (k, top - k)

    m = piece(window[0], window[1])

    def finish(ref):
        if ghost is not None:
            ref[...] += ghost[...]
        zero_edges(edge, ref)

    def stage_a(r, n):
        c, s, d = around(U[pl.ds(r - 1, n + 2)], ends[0])
        src = (0.5 / 6.0) * d
        SRC[pl.ds(r, n)] = src
        B[pl.ds(r, n)] = 0.35 * c + 0.1 * s
        _, s, _ = around(V[pl.ds(r - 1, n + 2)], ends[0])
        Q[pl.ds(r, n)] = s * SIXTH - src
    if ghost is not None:
        Q[...] = ghost[...]
        zero_edges(edge, Q)
    else:
        rows_loop(*span(1), stage_a, pieces)
        finish(Q)

    def stage_b(r, n):
        _, s, _ = around(Q[pl.ds(r - 1, n + 2)], ends[0])
        s = s * SIXTH
        V[pl.ds(r, n)] = s if ghost is not None else s - SRC[pl.ds(r, n)]
    rows_loop(*span(2), stage_b, pieces)
    finish(V)

    def stage_c(r, n):
        zp, zm = zshift(V[pl.ds(r, n)], ends[0])
        u = 0.5 * (zp - zm)
        U1[pl.ds(r, n)] = u if ghost is not None else u + B[pl.ds(r, n)]
    rows_loop(*span(3), stage_c, pieces)
    zero_edges(edge, U1)

    def stage_d(r, n):
        c, s, d = around(U1[pl.ds(r - 1, n + 2)], ends[0])
        src = (0.5 / 6.0) * d[:, m]
        SRC2[pl.ds(r, n)] = src
        B2[pl.ds(r, n)] = 0.35 * c[:, m] + 0.1 * s[:, m]
        _, s, _ = around(V[pl.ds(r - 1, n + 2)], ends[0])
        Q2[pl.ds(r, n)] = s[:, m] * SIXTH - src
    rows_loop(*span(3), stage_d, pieces)
    finish(Q2)

    def stage_e(r, n):
        _, s, _ = around(Q2[pl.ds(r - 1, n + 2)], ends[1])
        P2[pl.ds(r, n)] = s * SIXTH - SRC2[pl.ds(r, n)]
    rows_loop(*span(4), stage_e, pieces)
    if ghost is not None:
        P2[...] += ghost[...]

    def stage_f(r, n):
        zp, zm = zshift(P2[pl.ds(r, n)], ends[1])
        A[pl.ds(r, n)] = B2[pl.ds(r, n)] + 0.5 * (zp - zm)
    rows_loop(*span(4), stage_f, pieces)
    zero_edges(edge, A)


def adjoint(edge, window, pieces, a2, pot, u1, mid, late, give, spread=False):
    BM, SP = mid[5:7]
    S2, T, B, A1, S3, SP2, S4, T2 = late
    top = SP.shape[0] - 1
    closed = window[0][0] == 0
    ends = [None if closed else (part[0],) + edge[2:] for part in window]

    def span(k):
        return (1, top - 1) if spread else (k, top - k)

    third = window[2][0]
    m = piece(window[1], window[2])

    def take(source, inner, r, n):
        ref, place = source
        return ref[pl.ds(r, n), piece(place, inner), :]

    def stage_g(r, n):
        c, s, d = around(take(a2, window[1], r - 1, n + 2), ends[1])
        BM[pl.ds(r, n)] = 0.35 * c + 0.1 * s
        sp = -0.5 * d
        if pot is not None:
            sp = sp + take(pot, window[1], r, n)
        SP[pl.ds(r, n)] = sp
    rows_loop(*span(4), stage_g, pieces)
    zero_edges(edge, SP)

    def stage_h(r, n):
        c, s, _ = around(SP[pl.ds(r - 1, n + 2)], ends[1])
        c, s = c[:, m], s[:, m] * SIXTH
        S2[pl.ds(r, n)] = s
        T[pl.ds(r, n)] = (c + s) * SIXTH
    rows_loop(*span(5), stage_h, pieces)
    zero_edges(edge, S2)

    def stage_i(r, n):
        _, s, _ = around(S2[pl.ds(r - 1, n + 2)], ends[2])
        S3[pl.ds(r, n)] = s * SIXTH
        zp, zm = zshift(T[pl.ds(r, n)], ends[2])
        a = BM[pl.ds(r, n), m, :] + 0.5 * (zp - zm)
        if u1 is not None:
            a = a + take(u1, window[2], r, n)
        A1[pl.ds(r, n)] = a
    rows_loop(*span(6), stage_i, pieces)
    zero_edges(edge, A1)

    def stage_j(r, n):
        if give is None:
            zp, zm = zshift(A1[pl.ds(r, n)], ends[2])
            d = zp - zm
        else:
            c, s, d = around(A1[pl.ds(r - 1, n + 2)], ends[2])
            B[pl.ds(r, n)] = 0.35 * c + 0.1 * s
        SP2[pl.ds(r, n)] = S3[pl.ds(r, n)] - 0.5 * d
    rows_loop(*span(6), stage_j, pieces)
    zero_edges(edge, SP2)

    def stage_k(r, n):
        c, s, _ = around(SP2[pl.ds(r - 1, n + 2)], ends[2])
        s = s * SIXTH
        S4[pl.ds(r, n)] = s
        T2[pl.ds(r, n)] = (c + s) * SIXTH
    rows_loop(*span(7), stage_k, pieces)
    zero_edges(edge, S4)
    if give is None:
        return
    own = slice(third, third + COLS)

    def stage_l(r, n):
        _, s, _ = around(S4[pl.ds(r - 1, n + 2)], ends[2])
        zp, zm = zshift(T2[pl.ds(r, n)], ends[2])
        u = B[pl.ds(r, n)] + 0.5 * (zp - zm)
        give(r - HY, n, u[:, own], s[:, own] * SIXTH)
    rows_loop(*span(8), stage_l, 2)


def load_extended(dst, f, part, own, yd, yu, below, above):
    first, end = part * PART, part * PART + PART + 2 * HY
    top = HY + ROWS

    def rows(src_first, src_end, src, offset, layers, to_layer):
        r0, r1 = max(first, src_first), min(end, src_end)
        if r0 < r1:
            at = slice(offset + r0 - src_first, offset + r1 - src_first)
            dst[r0 - first:r1 - first, to_layer:to_layer + layers.stop - layers.start, :] = src[f, at, layers, :]

    block, tile = slice(0, COLS), slice(0, 8)
    rows(0, HY, yd, 0, block, HZ)
    rows(HY, top, own, 0, block, HZ)
    rows(top, EXT, yu, 0, block, HZ)
    for (z, rest), near, far in ((below, 4, 0), (above, HZ + COLS, HZ + COLS + 8)):
        rows(HY, top, z, 0, tile, near)
        rows(0, HY, rest, 0, tile, near)
        rows(top, EXT, rest, HY, tile, near)
        for k in range(2):
            rows(RIM + k * HALF, RIM + (k + 1) * HALF, rest, 2 * HY, slice(4 * k, 4 * k + 4), far)


def is_even(axis):
    return lax.rem(lax.axis_index(axis), 2) == 0


def strips_kernel(own, far, near):
    even = is_even("gy")
    low, high = own[:, 0:HY], own[:, ROWS - HY:]
    far[...] = jnp.where(even, low, high)
    near[...] = jnp.where(even, high, low)


def tiles_kernel(own, near, far):
    even = is_even("gz")
    low, high = own[:, :, 0:8, :], own[:, :, 8:16, :]
    near[...] = jnp.where(even, high, low)
    far[...] = jnp.where(even, low, high)


def pack_kernel(own, far, near, yd, yu, near_out, far_out, z_near, z_far, sems):
    even = is_even("gy")
    yd[...] = jnp.where(even, far[...], near[...])
    yu[...] = jnp.where(even, near[...], far[...])

    def pack(dst, whole, part):
        dst[:, 0:HY] = yd[:, :, whole:whole + 8, :]
        dst[:, HY:2 * HY] = yu[:, :, whole:whole + 8, :]
        at, edge = 2 * HY, HY - RIM
        dst[:, at:at + edge, 0:4, :] = yd[:, RIM:, part:part + 4, :]
        dst[:, at + edge:, 0:4, :] = own[:, 0:HALF - edge, part:part + 4, :]
        dst[:, at:at + HALF - edge, 4:8, :] = own[:, HALF - edge:, part:part + 4, :]
        dst[:, at + HALF - edge:, 4:8, :] = yu[:, 0:edge, part:part + 4, :]

    copies = [pltpu.make_async_copy(*pair, sems.at[i]) for i, pair in enumerate(((z_far, far_out), (z_near, near_out)))]
    upward = is_even("gz")

    def fill(dst, when, copy):
        @pl.when(when)
        def _():
            pack(dst, 8, 4)

        @pl.when(jnp.logical_not(when))
        def _():
            pack(dst, 0, 8)
        copy.start()
    fill(z_far, jnp.logical_not(upward), copies[0])
    fill(z_near, upward, copies[1])
    for copy in copies:
        copy.wait()


HIGHEST = lax.Precision.HIGHEST


def edges():
    gy, gz = lax.axis_index("gy"), lax.axis_index("gz")
    return (gy == 0, gy == lax.axis_size("gy") - 1, gz == 0, gz == lax.axis_size("gz") - 1)


def iota(shape, dim):
    return lax.broadcasted_iota(jnp.int32, shape, dim)


def tile_volts(first, second, labels):
    lab = jnp.broadcast_to(labels, first.shape) - 2 * iota(first.shape, 0)
    hit = jnp.where(lab == 0, first, 0.0) + jnp.where(lab == 1, second, 0.0)
    return jnp.sum(hit, axis=0, keepdims=True)


def fill_ghost(upper, ghost, volts):
    lane, row = iota((8, LANES), 1), iota((8, LANES), 0)
    apart = jnp.where((lane >> 4) == row, jnp.broadcast_to(volts, (8, LANES)), 0.0)
    spread = ((iota((LANES, LANES), 0) & 15) == (iota((LANES, LANES), 1) >> 3)).astype(jnp.float32)
    wall = jnp.dot(apart, spread, precision=HIGHEST, preferred_element_type=jnp.float32) * (1.0 / 6.0)
    layer = iota((COLS, LANES), 0) == jnp.where(upper, COLS - 1, 0)
    for ty in range(8):
        tile = jnp.where(layer, jnp.broadcast_to(wall[ty:ty + 1], (COLS, LANES)), 0.0)
        ghost[8 * ty:8 * ty + 8] = jnp.broadcast_to(tile[None], (8, COLS, LANES))


def wall_tiles(layer, T, T2):
    w = jnp.sum((T[:, layer, :] + T2[:, layer, :]).reshape(8, 8, LANES), axis=1)
    gather = ((iota((LANES, LANES), 0) >> 3) == (iota((LANES, LANES), 1) & 15)).astype(jnp.float32)
    sums = jnp.dot(w, gather, precision=HIGHEST, preferred_element_type=jnp.float32)
    first = lax.rem(lax.axis_index("gy"), 2)
    lane = iota((8, LANES), 1)
    keep = ((lane >> 4) + first == iota((8, LANES), 0)) & (lane < VOLT)
    return jnp.sum(jnp.where(keep, sums, 0.0), axis=0, keepdims=True)


def split(refs):
    return refs[:6], refs[6:13], refs[13:21]


def wall_kernel(own, near, volts, row, *refs):
    early, mid, late = split(refs)
    sums = refs[21]
    ylo, yhi, zlo, zhi = edges()
    edge = (ylo, yhi, None, None)
    is_forward = lax.axis_index("grp") == 0
    sums[...] = jnp.zeros((1, LANES), jnp.float32)

    @pl.when(jnp.logical_or(zlo, zhi))
    def _():
        for ref in early + mid + late:
            for r in (0, EXT - 1):
                ref[r] = jnp.zeros(ref.shape[1:], jnp.float32)
        for f in range(2):
            early[f][0:HY] = jnp.where(is_even("gy"), 0.0, near[f])
            early[f][HY:HY + ROWS] = own[f]
            early[f][HY + ROWS:] = jnp.where(is_even("gy"), near[f], 0.0)

    def side(window, layer):
        @pl.when(is_forward)
        def _():
            forward(edge, None, window, 1, early, mid, True)
            adjoint(edge, window, 1, (mid[4], window[1]), None, (early[5], window[0]), mid, late, None, True)

        @pl.when(jnp.logical_not(is_forward))
        def _():
            adjoint(edge, window, 1, (early[0], window[0]), (early[1], window[0]), None, mid, late, None, True)

        sums[...] = wall_tiles(layer, late[1], late[7])

    @pl.when(zlo)
    def _():
        side(LOWER, 0)

    @pl.when(zhi)
    def _():
        side(UPPER, 7)

    row[...] = jnp.broadcast_to(sums[...] + volts[...], row.shape)


def bulk_kernel(part, own, yd, yu, z_far, z_near, far, near, main_out, send_out, *refs):
    far, near = (z_far, far), (z_near, near)
    early, mid, late = split(refs)
    main, send, sems = refs[21:]
    ylo, yhi, zlo, zhi = edges()
    edge = (ylo if part == 0 else None, yhi if part == PARTS - 1 else None, zlo, zhi)
    is_forward = lax.axis_index("grp") == 0

    @pl.when(is_even("gz"))
    def _():
        for f in range(2):
            load_extended(early[f], f, part, own, yd, yu, far, near)

    @pl.when(jnp.logical_not(is_even("gz")))
    def _():
        for f in range(2):
            load_extended(early[f], f, part, own, yd, yu, near, far)

    def leave(ref, out, rows, copies):
        copy = pltpu.make_async_copy(ref.at[:, rows], out.at[:, rows], sems.at[len(copies)])
        copy.start()
        copies.append(copy)

    def into(ref, out, copies):
        def give(r, n, u, p):
            ref[0, pl.ds(r, n)] = u
            ref[1, pl.ds(r, n)] = p
            leave(ref, out, pl.ds(r, n), copies)
        return give

    @pl.when(is_forward)
    def _():
        copies = []
        forward(edge, None, BULK, 1, early, mid)
        at = (slice(HY, HY + PART), slice(BULK[1][0], BULK[1][0] + COLS))
        main[0] = mid[4][at]
        main[1] = mid[3][at]
        leave(main, main_out, pl.ds(0, PART), copies)
        adjoint(edge, BULK, 1, (mid[4], BULK[1]), None, (early[5], BULK[0]), mid, late, into(send, send_out, copies))
        for copy in copies:
            copy.wait()

    @pl.when(jnp.logical_not(is_forward))
    def _():
        copies = []
        adjoint(edge, BULK, 1, (early[0], BULK[0]), (early[1], BULK[0]), None, mid, late, into(main, main_out, copies))
        for copy in copies:
            copy.wait()


def volts_kernel(*refs):
    parts, refs = refs[:PARTS], refs[PARTS:]
    rows, near, labels, far_response, out, grad = refs[:6]
    early, mid, late = split(refs[6:])
    ghost, response, sems = refs[27:]
    copies = [pltpu.make_async_copy(part, out.at[:, i * PART:(i + 1) * PART], sems.at[i]) for i, part in enumerate(parts)]
    fetch = pltpu.make_async_copy(far_response, response, sems.at[PARTS])
    for copy in copies:
        copy.start()
    fetch.start()
    ylo, yhi, zlo, zhi = edges()
    edge = (ylo, yhi, None, None)
    at_wall = jnp.logical_or(zlo, zhi)
    is_forward = lax.axis_index("grp") == 0
    n = rows.shape[0]
    first = jnp.broadcast_to(rows[:, VOLT:VOLT + 1], (n, LANES))
    second = jnp.broadcast_to(rows[:, VOLT + 1:VOLT + 2], (n, LANES))

    @pl.when(at_wall)
    def _():
        fill_ghost(zhi, ghost, tile_volts(first, second, near[...]))
        forward(edge, ghost, NEAR, 1, early, mid)

    for copy in copies:
        copy.wait()

    @pl.when(jnp.logical_and(at_wall, is_forward))
    def _():
        out[0] += mid[4][HY:HY + ROWS]
        out[1] += mid[3][HY:HY + ROWS]

    @pl.when(jnp.logical_and(at_wall, jnp.logical_not(is_forward)))
    def _():
        def give(r, n, u, p):
            out[0, pl.ds(r, n)] += u
            out[1, pl.ds(r, n)] += p
        adjoint(edge, NEAR, 1, (mid[4], NEAR[1]), None, (early[5], NEAR[0]), mid, late, give)

    fetch.wait()
    gy, gz = lax.axis_size("gy"), lax.axis_size("gz")
    me = (lax.axis_index("grp") * gy + lax.axis_index("gy")) * gz + lax.axis_index("gz")
    pair = [jnp.zeros((gy, LANES), jnp.float32)] * 2
    block, lane = iota((gy, LANES), 0), iota((gy, LANES), 1)
    for s in range(2):
        v = jnp.concatenate([tile_volts(first, second, labels[s, g:g + 1]) for g in range(gy)], axis=0)
        r = jnp.dot(v, response[...], precision=HIGHEST, preferred_element_type=jnp.float32)
        r = [r[:, k * LANES:(k + 1) * LANES] for k in range(5)]
        w = jnp.where(block == 0, r[3], jnp.where(block == gy - 1, r[4], r[0]))
        w = w + jnp.where(block == 0, 0.0, pltpu.roll(r[1], 1, 0))
        w = w + jnp.where(block == gy - 1, 0.0, pltpu.roll(r[2], gy - 1, 0))
        got = sum(rows[pl.ds(g * gy * gz + s * (gz - 1), gy, stride=gz), :] for g in range(2))
        odd = (block & 1) == 1
        w = w + jnp.where(odd, got, pltpu.roll(got, LANES - 16, 1))
        below = pltpu.roll(pltpu.roll(got, 32, 1), 1, 0)
        above = pltpu.roll(pltpu.roll(got, 80, 1), gy - 1, 0)
        w = w + jnp.where((block > 0) & jnp.logical_not(odd) & (lane < 16), below, 0.0)
        w = w + jnp.where((block < gy - 1) & odd & (lane >= 80), above, 0.0)
        for j in range(2):
            pair[j] = pair[j] + jnp.where(labels[s] == 2 * me + j, w, 0.0)
    total = [jnp.sum(p) for p in pair]
    grad[...] = jnp.where(iota((1, 2), 1) == 0, total[0], total[1])


def sum_kernel(which, main, *refs):
    extras, (out, total, sems) = refs[:len(which)], refs[-3:]
    copies = []
    for n, i in enumerate(which):
        at = slice(i * PART, (i + 1) * PART)
        total[:, n * PART:(n + 1) * PART] = main[:, at] + extras[n][...]
        copies.append(pltpu.make_async_copy(total.at[:, n * PART:(n + 1) * PART], out.at[0, :, at], sems.at[n]))
        copies[-1].start()
    for copy in copies:
        copy.wait()


def last_sum_kernel(which, main, extra, before, out, total, sems):
    sum_kernel(which, main, extra, out, total, sems)


def wall_response():
    def near_sum(f):
        g = np.pad(f, ((0, 0), (1, 1), (1, 1), (0, 0)))
        t = g[:, 2:, 1:-1] + g[:, :-2, 1:-1] + g[:, 1:-1, 2:] + g[:, 1:-1, :-2]
        return t + np.roll(f, 1, 3) + np.roll(f, -1, 3)

    def diff(f):
        g = np.pad(f, ((0, 0), (0, 0), (1, 1), (0, 0)))
        return g[:, :, 2:] - g[:, :, :-2]

    def sums(blocks, at):
        ghost = np.zeros((TY, blocks * ROWS, 13, LANES))
        for t in range(TY):
            ghost[t, at * ROWS + 8 * t:at * ROWS + 8 * t + 8, 0, 0:8] = 1.0
        u, p, states = np.zeros_like(ghost), np.zeros_like(ghost), []
        for _ in range(2):
            source = 0.5 * diff(u)
            for _ in range(2):
                p = (near_sum(p) + ghost - source) / 6.0
            u = 0.35 * u + 0.1 * near_sum(u) + 0.5 * diff(p)
            states.append(u)
        a, q, wall = np.zeros_like(ghost), np.zeros_like(ghost), 0.0
        for u in reversed(states):
            a = a + u
            spread, total = q - 0.5 * diff(a), 0.0
            for _ in range(2):
                total = total + spread / 6.0
                spread = near_sum(spread) / 6.0
            a = 0.35 * a + 0.1 * near_sum(a) + 0.5 * diff(total)
            q = spread
            wall = wall + total[:, :, 0]
        return wall.reshape(TY, blocks, TY, 8, 16, 8).sum((3, 5))

    def matrix(got):
        m = np.zeros((LANES, LANES), np.float32)
        for t in range(TY):
            for x in range(16):
                m[t * 16 + x, 0:TY * 16] = np.roll(got[t], x, 1).reshape(-1)
        return m

    middle, low, high = sums(3, 1), sums(2, 0), sums(2, 1)
    return np.concatenate([matrix(middle[:, 1]), matrix(middle[:, 2]), matrix(middle[:, 0]),
                           matrix(low[:, 0]), matrix(high[:, 1])], axis=1)


def vmem(n):
    return [pl.BlockSpec(memory_space=pltpu.VMEM)] * n


def shape(*dims):
    return jax.ShapeDtypeStruct(dims, jnp.float32)


def kept(*dims):
    return pltpu.VMEM(dims, jnp.float32)


def in_hbm(array):
    return pltpu.with_memory_space_constraint(array, pltpu.HBM)


def swapped(array, axis, first):
    pairs = []
    for i in range(first, lax.axis_size(axis) - 1, 2):
        pairs += [(i, i + 1), (i + 1, i)]
    return lax.ppermute(array, axis, pairs)


def per_device(response, field_pairs, tile_owner, electrode_volts):
    own = field_pairs[0]
    labels = tile_owner[..., 0]
    gy, gz = lax.axis_index("gy"), lax.axis_index("gz")
    devices = lax.axis_size(AXES)
    half = pltpu.HBM((2, PART, COLS, LANES), jnp.float32)
    strip, tiles = kept(2, HY, COLS, LANES), kept(2, ROWS, 8, LANES)
    slab = pltpu.HBM((2, 2 * HY + HALF, 8, LANES), jnp.float32)

    def limit(mib):
        return pltpu.CompilerParams(vmem_limit_bytes=mib * 1024 * 1024)

    far, near = pl.pallas_call(
        strips_kernel, out_shape=(strip, strip), in_specs=vmem(1), out_specs=vmem(2), compiler_params=limit(4),
    )(own)
    far = swapped(far, "gy", 1)
    near = swapped(near, "gy", 0)
    mine, near = lax.optimization_barrier((own, near))
    row = pl.pallas_call(
        wall_kernel, out_shape=kept(devices, LANES), in_specs=vmem(3), out_specs=vmem(1)[0],
        scratch_shapes=scratch(EXT, LOWER) + [pltpu.VMEM((1, LANES), jnp.float32)], compiler_params=limit(12),
    )(mine, near, jnp.pad(electrode_volts, (VOLT, LANES - VOLT - 2))[None])
    mine, row = lax.optimization_barrier((mine, row))
    z_near, z_far = pl.pallas_call(
        tiles_kernel, out_shape=(tiles, tiles), in_specs=vmem(1), out_specs=vmem(2), compiler_params=limit(8),
    )(mine)
    z_far = swapped(z_far, "gz", 1)
    z_near = swapped(z_near, "gz", 0)
    yd, yu, near, far = pl.pallas_call(
        pack_kernel, out_shape=(strip, strip, slab, slab), in_specs=vmem(3),
        out_specs=vmem(2) + [pl.BlockSpec(memory_space=pl.ANY)] * 2,
        scratch_shapes=[pltpu.VMEM((2, 2 * HY + HALF, 8, LANES), jnp.float32)] * 2 + [pltpu.SemaphoreType.DMA((2,))],
        compiler_params=limit(8),
    )(own, far, near)
    far, near, row = lax.optimization_barrier((far, near, row))
    far = swapped(far, "gz", 1)
    near = swapped(near, "gz", 0)
    rows = lax.all_to_all(row, AXES, 0, 0, tiled=True)

    mine, _ = lax.optimization_barrier((own, row))
    def bulk(part, block, load):
        return pl.pallas_call(
            functools.partial(bulk_kernel, part), out_shape=(half, half), in_specs=vmem(7),
            out_specs=[pl.BlockSpec(memory_space=pl.ANY)] * 2,
            scratch_shapes=scratch(PART + 2 * HY, BULK) + [pltpu.VMEM((2, PART, COLS, LANES), jnp.float32)] * 2
            + [pltpu.SemaphoreType.DMA((3,))], compiler_params=limit(20),
            cost_estimate=pl.CostEstimate(flops=10 ** 8, bytes_accessed=load * 10 ** 6, transcendentals=0),
        )(block, yd, yu, z_far, z_near, far, near)

    mains, extras = [], []
    for part in range(PARTS):
        main, send = bulk(part, mine, 36 if part == 0 else 9)
        mains.append(main)
        mine, _ = lax.optimization_barrier((own, send))
        if part == PARTS - 1:
            send, rows = lax.optimization_barrier((send, rows))
        extras.append(lax.ppermute(send, "grp", [(0, 1)]))

    fenced = jnp.pad(labels, ((0, 0), (1, 1), (0, 0)), constant_values=-1)
    side = (gz == lax.axis_size("gz") - 1).astype(jnp.int32)
    by_wall = lax.dynamic_slice(fenced, (side, gy * TY, 0), (1, 8, 16)).reshape(1, LANES)
    by_block = jnp.pad(labels.reshape(2, 8, TY * 16), ((0, 0), (0, 0), (0, LANES - TY * 16)), constant_values=-1)
    total, grad = pl.pallas_call(
        volts_kernel, out_shape=(kept(2, ROWS, COLS, LANES), shape(1, 2)),
        in_specs=[pl.BlockSpec(memory_space=pl.ANY)] * PARTS + vmem(3) + [pl.BlockSpec(memory_space=pl.ANY)], out_specs=vmem(2),
        scratch_shapes=scratch(EXT, NEAR) + [pltpu.VMEM((EXT, COLS, LANES), jnp.float32), pltpu.VMEM(response.shape, jnp.float32),
                                             pltpu.SemaphoreType.DMA((PARTS + 1,))],
        compiler_params=limit(16),
    )(*[in_hbm(main) for main in mains], rows, by_wall, by_block, in_hbm(response))
    def sums(kernel, which, operands, specs, aliases):
        return pl.pallas_call(
            functools.partial(kernel, which), out_shape=pltpu.HBM((1, 2, ROWS, COLS, LANES), jnp.float32), in_specs=specs,
            out_specs=pl.BlockSpec(memory_space=pl.ANY), input_output_aliases=aliases,
            scratch_shapes=[pltpu.VMEM((2, len(which) * PART, COLS, LANES), jnp.float32), pltpu.SemaphoreType.DMA((len(which),))],
            compiler_params=limit(8),
        )(*operands)

    early = tuple(range(PARTS - 1))
    advanced = sums(sum_kernel, early, (total, *extras[:-1]), vmem(PARTS), {})
    advanced = sums(last_sum_kernel, (PARTS - 1,), (total, extras[-1], advanced),
                    vmem(2) + [pl.BlockSpec(memory_space=pl.ANY)], {2: 0})
    return (advanced, grad.reshape(2))


def solution(mesh):
    response = jnp.asarray(wall_response())
    placed = (P("grp", None, "gy", "gz", None), P(), P(AXES))
    return jax.shard_map(
        functools.partial(per_device, response), mesh=mesh, in_specs=placed,
        out_specs=(P("grp", None, "gy", "gz", None), P(AXES)), check_vma=False,
    )
```
